128 devices in a mesh: grp: 8 (over y, core), sub: 16 (over x, z).
Axes of the slice: x: 4, y: 4, z: 4, core: 2. Of those that a mesh axis runs over, the one named last changes fastest.
Arguments:
- nodes: bfloat16 [262144, 128], P(('grp', 'sub')), may hold values from -6 to 6
- edges: bfloat16 [1572864, 128], P(('grp', 'sub')), may hold values from -6 to 6
- senders: int32 [1572864], P(('grp', 'sub')), may hold values from 0 to 2303
- receivers: int32 [1572864], P(('grp', 'sub')), may hold values from 0 to 2047
- edge_live: int32 [128], P(('grp', 'sub')), may hold values from 3072 to 12288, as said below
- halo_rows: int32 [256, 128], P(('grp', 'sub')), may hold values from 0 to 2047
- pool_fine: int32 [262144], P(('grp', 'sub')), may hold values from 0 to 4095, as said below
- mid_edges: bfloat16 [196608, 128], P(('grp', 'sub')), may hold values from -6 to 6
- mid_senders: int32 [196608], P(('grp', 'sub')), may hold values from 0 to 4095
- mid_receivers: int32 [196608], P(('grp', 'sub')), may hold values from 0 to 255
- pool_mid: int32 [32768], P(('grp', 'sub')), may hold values from 0 to 2047
- coarse_edges: bfloat16 [12288, 128], replicated, may hold values from -6 to 6
- coarse_senders: int32 [12288], replicated, may hold values from 0 to 2047
- coarse_receivers: int32 [12288], replicated, may hold values from 0 to 2047
- w_edge_in: bfloat16 [3, 384, 128], replicated, may hold values from -0.3125 to 0.3125
- w_edge_out: bfloat16 [3, 128, 128], replicated, may hold values from -0.5 to 0.5
- w_node_in: bfloat16 [3, 256, 128], replicated, may hold values from -0.375 to 0.375
- w_node_out: bfloat16 [3, 128, 128], replicated, may hold values from -0.5 to 0.5
- cotangent: bfloat16 [262144, 128], P(('grp', 'sub')), may hold values from -6 to 6
Outputs:
- result: bfloat16 [262144, 128], P(('grp', 'sub'))
- grad_nodes: float32 [262144, 128], P(('grp', 'sub'))
- grad_edge_in: float32 [3, 384, 128], replicated
- grad_edge_out: float32 [3, 128, 128], replicated
- grad_node_in: float32 [3, 256, 128], replicated
- grad_node_out: float32 [3, 128, 128], replicated
The draws below stay inside these ranges and needn't reach their ends.
Inputs may be any that keep to these rules, and one draw needn't show every extreme that they name: `edge_live`: fine edge slots past a partition's count are padding; some partition fills all 12288 slots. `pool_fine`: A fine node pools into any level-2 node of its own group; most of a partition's nodes go to level-2 nodes owned by its own sub index.
All inputs are finite; a program needn't handle non-finite values.
Results may differ from the reference program's by a relative error of at most 0.02.
Values may be sent and summed in bfloat16 or wider, within the bound.
No kernel may reach another device: no remote copies, remote signals or barrier semaphores. Data moves between devices by JAX's collectives and lax.ppermute only.
A program may use at most 192 MiB of HBM per device.

```python
import math
import jax
import jax.numpy as jnp
import numpy as np
from jax import lax

D = 128
LEVELS = 3
NODE_DEV = 2048
EDGE_DEV = 12288
HALO = 128
L2_DEV = 256
E2_DEV = 1536
MID_GROUP = 4096
COARSE = 2048
COARSE_EDGES = 12288
NODES = 262144
EDGES = 1572864
MIDS = 32768
MID_EDGES = 196608
N_GRP = 8
N_SUB = 16


def draw_edge_live(key, part):
    key = jax.random.fold_in(key, 7)
    first_key, second_key = jax.random.split(key)
    device_count = N_GRP * N_SUB
    counts = jax.random.randint(first_key, (device_count,), EDGE_DEV // 4, EDGE_DEV + 1)
    fullest = jax.random.randint(second_key, (), 0, device_count)
    return jnp.where(jnp.arange(device_count) == fullest, EDGE_DEV, counts).astype(jnp.int32)


def draw_pool_fine(key, part):
    key = jax.random.fold_in(key, 11)
    first_key, second_key, third_key, fourth_key = jax.random.split(key, 4)
    total = NODE_DEV * N_GRP * N_SUB
    position = jnp.arange(total, dtype=jnp.int32)
    device = position // NODE_DEV
    within = position % NODE_DEV
    own_sub = device % N_SUB
    first_pick = jax.random.randint(first_key, (total,), 0, L2_DEV)
    second_pick = jax.random.randint(second_key, (total,), 0, L2_DEV)
    local = jnp.minimum(first_pick, second_pick)
    side = jax.random.randint(third_key, (total,), 0, 4)
    offset = jax.random.randint(fourth_key, (total,), 0, N_SUB)
    step = jnp.where(side == 0, offset, 0)
    step = jnp.where(within == 0, N_SUB // 2, step)
    target_sub = (own_sub + step) % N_SUB
    return (target_sub * L2_DEV + local).astype(jnp.int32)


def plant(array, own_key, low, largest):
    shape = array.shape
    place = [jax.random.randint(jax.random.fold_in(own_key, axis), (), 0, shape[axis]) for axis in range(len(shape))]
    array = array.at[tuple(place)].set(low)
    longest = shape.index(max(shape))
    place[longest] = (place[longest] + 1) % shape[longest]
    return array.at[tuple(place)].set(largest)


def shard_levels(rng, shape, shards, least, largest):
    def one(dim, parts):
        steps = jax.random.uniform(jax.random.fold_in(jax.random.fold_in(rng, 6), dim), (parts,), jnp.float32, least / len(shards), largest / len(shards))
        return jnp.repeat(jnp.exp(steps), shape[dim] // parts).reshape((-1,) + (1,) * (len(shape) - dim - 1))

    factor_of = one(*shards[0])
    for cut in shards[1:]:
        factor_of = factor_of * one(*cut)
    return factor_of


def rank_table(amount, lean):
    portions = [(1 << 20) // math.isqrt(grade ** lean) + 1 for grade in range(1, amount + 1)]
    width = 1 + sum(portions) // (1 << 30)
    return np.cumsum(np.array([max(1, weight // width) for weight in portions]))


def ranked(stream_key, extent, amount, slope):
    grid = rank_table(amount, slope)
    ticket = jax.random.randint(jax.random.fold_in(stream_key, 1), extent, 0, int(grid[amount - 1]))
    standing = jnp.searchsorted(jnp.asarray(grid, jnp.int32), ticket, side="right")
    return jax.random.permutation(jax.random.fold_in(stream_key, 2), amount)[standing].astype(jnp.int32)


def bell_draw(key, shape, spread, bound, shards=(), kind=jnp.bfloat16):
    factor_of = shard_levels(key, shape, shards, -0.22, 0.18) if shards else 1.0
    array = jax.random.normal(key, shape, jnp.float32) * spread * factor_of
    return jnp.minimum(jnp.maximum(array, -bound), bound).astype(kind)


def setup_inputs(seed: int = 0) -> dict:
    streams_of = jax.random.split(jax.random.key(seed), 20)
    return {
        "nodes": bell_draw(streams_of[0], (NODES, D), 1.0, 6.0, ((0, 128),)),
        "edges": bell_draw(streams_of[1], (EDGES, D), 1.0, 6.0, ((0, 128),)),
        "senders": plant(jax.random.randint(streams_of[2], (EDGES,), 0, NODE_DEV + 2 * HALO), jax.random.fold_in(streams_of[2], 1), 0, (NODE_DEV + 2 * HALO) - 1).astype(jnp.int32),
        "receivers": plant(jax.random.randint(streams_of[3], (EDGES,), 0, NODE_DEV), jax.random.fold_in(streams_of[3], 1), 0, NODE_DEV - 1).astype(jnp.int32),
        "edge_live": draw_edge_live(jax.random.fold_in(streams_of[19], 71), 0),
        "halo_rows": plant(jax.random.randint(streams_of[5], (2 * N_GRP * N_SUB, HALO), 0, NODE_DEV), jax.random.fold_in(streams_of[5], 1), 0, NODE_DEV - 1).astype(jnp.int32),
        "pool_fine": draw_pool_fine(jax.random.fold_in(streams_of[19], 71), 0),
        "mid_edges": bell_draw(streams_of[7], (MID_EDGES, D), 1.0, 6.0, ((0, 128),)),
        "mid_senders": plant(jax.random.randint(streams_of[8], (MID_EDGES,), 0, MID_GROUP), jax.random.fold_in(streams_of[8], 1), 0, MID_GROUP - 1).astype(jnp.int32),
        "mid_receivers": plant(jax.random.randint(streams_of[9], (MID_EDGES,), 0, L2_DEV), jax.random.fold_in(streams_of[9], 1), 0, L2_DEV - 1).astype(jnp.int32),
        "pool_mid": plant(ranked(streams_of[10], (MIDS,), COARSE, 1), jax.random.fold_in(streams_of[10], 3), 0, COARSE - 1).astype(jnp.int32),
        "coarse_edges": bell_draw(streams_of[11], (COARSE_EDGES, D), 1.0, 6.0),
        "coarse_senders": plant(jax.random.randint(streams_of[12], (COARSE_EDGES,), 0, COARSE), jax.random.fold_in(streams_of[12], 1), 0, COARSE - 1).astype(jnp.int32),
        "coarse_receivers": plant(jax.random.randint(streams_of[13], (COARSE_EDGES,), 0, COARSE), jax.random.fold_in(streams_of[13], 1), 0, COARSE - 1).astype(jnp.int32),
        "w_edge_in": bell_draw(streams_of[14], (LEVELS, 3 * D, D), (3 * D) ** -0.5, 0.3125),
        "w_edge_out": bell_draw(streams_of[15], (LEVELS, D, D), D ** -0.5, 0.5),
        "w_node_in": bell_draw(streams_of[16], (LEVELS, 2 * D, D), (2 * D) ** -0.5, 0.375),
        "w_node_out": bell_draw(streams_of[17], (LEVELS, D, D), D ** -0.5, 0.5),
        "cotangent": bell_draw(streams_of[18], (NODES, D), 1.0, 6.0, ((0, 128),)),
    }


epsilon = 1e-05

def mlp_forward(inputs, weight_in, weight_out):
    preact = jnp.dot(inputs, weight_in, preferred_element_type=jnp.float32)
    hidden = jax.nn.silu(preact).astype(jnp.bfloat16)
    output = jnp.dot(hidden, weight_out, preferred_element_type=jnp.float32)
    centred = output - lax.optimization_barrier(jnp.mean(output, axis=-1, keepdims=True))
    inv_std = lax.rsqrt(lax.optimization_barrier(jnp.mean(centred * centred, axis=-1, keepdims=True)) + epsilon)
    normed = centred * inv_std
    return (normed, (preact, hidden, normed, inv_std))

def mlp_backward(upstream, inputs, weight_out, kept_values):
    preact, hidden, normed, inv_std = kept_values
    centred_grad = upstream - lax.optimization_barrier(jnp.mean(upstream, axis=-1, keepdims=True)) - normed * lax.optimization_barrier(jnp.mean(upstream * normed, axis=-1, keepdims=True))
    grad_output = (inv_std * centred_grad).astype(jnp.bfloat16)
    grad_weight_out = jnp.dot(hidden.T, grad_output, preferred_element_type=jnp.float32)
    grad_hidden = jnp.dot(grad_output, weight_out.T, preferred_element_type=jnp.float32)
    sigmoid_pre = jax.nn.sigmoid(preact)
    grad_preact = (grad_hidden * sigmoid_pre * (1.0 + preact * (1.0 - sigmoid_pre))).astype(jnp.bfloat16)
    grad_weight_in = jnp.dot(inputs.T, grad_preact, preferred_element_type=jnp.float32)
    return (grad_preact, grad_weight_in, grad_weight_out)

def layer_forward(source_table, own_nodes, edge_feat, sender_ids, receiver_ids, edge_mask, params):
    edge_in, edge_out, node_in, node_out = params
    edge_inputs = jnp.concatenate([jnp.take(source_table, sender_ids, axis=0), jnp.take(own_nodes, receiver_ids, axis=0), edge_feat], axis=1)
    message, edge_kept = mlp_forward(edge_inputs, edge_in, edge_out)
    updated = edge_feat.astype(jnp.float32) + message
    if edge_mask is not None:
        updated = updated * edge_mask[:, None]
    collected = jax.ops.segment_sum(updated, receiver_ids, num_segments=own_nodes.shape[0]).astype(jnp.bfloat16)
    node_inputs = jnp.concatenate([own_nodes, collected], axis=1)
    node_delta, node_kept = mlp_forward(node_inputs, node_in, node_out)
    return (own_nodes.astype(jnp.float32) + node_delta, (edge_inputs, edge_kept, node_inputs, node_kept))

def layer_backward(upstream, table_rows, own_nodes, sender_ids, receiver_ids, edge_mask, params, kept_values):
    edge_in, edge_out, node_in, node_out = params
    edge_inputs, edge_kept, node_inputs, node_kept = kept_values
    feature = own_nodes.shape[1]
    node_grad, grad_node_in, grad_node_out = mlp_backward(upstream, node_inputs, node_out, node_kept)
    grad_own = upstream + jnp.dot(node_grad, node_in[:feature].T, preferred_element_type=jnp.float32)
    grad_collected = jnp.dot(node_grad, node_in[feature:].T, preferred_element_type=jnp.float32)
    grad_updated = jnp.take(grad_collected, receiver_ids, axis=0)
    if edge_mask is not None:
        grad_updated = grad_updated * edge_mask[:, None]
    edge_grad, grad_edge_in, grad_edge_out = mlp_backward(grad_updated, edge_inputs, edge_out, edge_kept)
    sender_grad = jnp.dot(edge_grad, edge_in[:feature].T, preferred_element_type=jnp.float32)
    receiver_grad = jnp.dot(edge_grad, edge_in[feature:2 * feature].T, preferred_element_type=jnp.float32)
    grad_table = jax.ops.segment_sum(sender_grad, sender_ids, num_segments=table_rows)
    grad_own = grad_own + jax.ops.segment_sum(receiver_grad, receiver_ids, num_segments=own_nodes.shape[0])
    return (grad_own, grad_table, (grad_edge_in, grad_edge_out, grad_node_in, grad_node_out))

def level_weights(w_edge_in, w_edge_out, w_node_in, w_node_out, level):
    return (w_edge_in[level], w_edge_out[level], w_node_in[level], w_node_out[level])

def reference(nodes, edges, senders, receivers, edge_live, halo_rows, pool_fine, mid_edges, mid_senders, mid_receivers, pool_mid, coarse_edges, coarse_senders, coarse_receivers, w_edge_in, w_edge_out, w_node_in, w_node_out, cotangent):
    devices = N_GRP * N_SUB
    feature = D
    halo_width = HALO
    group_mids = L2_DEV * N_SUB
    node_dev = nodes.reshape(devices, NODE_DEV, feature)
    edge_dev = edges.reshape(devices, EDGE_DEV, feature)
    send_dev = senders.reshape(devices, EDGE_DEV)
    recv_dev = receivers.reshape(devices, EDGE_DEV)
    halo_dev = halo_rows.reshape(devices, 2, halo_width)
    outgoing = jax.vmap(lambda block, rows: jnp.take(block, rows.reshape(-1), axis=0).reshape(2, halo_width, feature))(node_dev, halo_dev)
    blank = jnp.zeros((1, halo_width, feature), jnp.bfloat16)
    from_prev = jnp.concatenate([blank, outgoing[:-1, 0]], axis=0)
    from_next = jnp.concatenate([outgoing[1:, 1], blank], axis=0)
    tables = jnp.concatenate([node_dev, from_prev, from_next], axis=1)
    masks = (jnp.arange(EDGE_DEV, dtype=jnp.int32)[None, :] < edge_live[:, None]).astype(jnp.float32)
    fine_params = level_weights(w_edge_in, w_edge_out, w_node_in, w_node_out, 0)
    mid_params = level_weights(w_edge_in, w_edge_out, w_node_in, w_node_out, 1)
    coarse_params = level_weights(w_edge_in, w_edge_out, w_node_in, w_node_out, 2)

    def fine_forward(device):
        return layer_forward(tables[device], node_dev[device], edge_dev[device], send_dev[device], recv_dev[device], masks[device], fine_params)[0]
    fine_new = lax.map(fine_forward, jnp.arange(devices))
    fine_group = fine_new.reshape(N_GRP, N_SUB * NODE_DEV, feature)
    pool_group = pool_fine.reshape(N_GRP, N_SUB * NODE_DEV)
    pooled = jax.vmap(lambda values, ids: jax.ops.segment_sum(values, ids, num_segments=group_mids))(fine_group, pool_group)
    counts = jax.vmap(lambda ids: jax.ops.segment_sum(jnp.ones(ids.shape, jnp.float32), ids, num_segments=group_mids))(pool_group)
    mid_tables = (pooled / jnp.maximum(counts, 1.0)[:, :, None]).astype(jnp.bfloat16)
    mid_own_all = mid_tables.reshape(devices, L2_DEV, feature)
    mid_edge_dev = mid_edges.reshape(devices, E2_DEV, feature)
    mid_send_dev = mid_senders.reshape(devices, E2_DEV)
    mid_recv_dev = mid_receivers.reshape(devices, E2_DEV)

    def mid_forward(device):
        return layer_forward(mid_tables[device // N_SUB], mid_own_all[device], mid_edge_dev[device], mid_send_dev[device], mid_recv_dev[device], None, mid_params)[0]
    mid_new = lax.map(mid_forward, jnp.arange(devices))
    flat_mid = mid_new.reshape(devices * L2_DEV, feature)
    coarse_sums = jax.ops.segment_sum(flat_mid, pool_mid, num_segments=COARSE)
    coarse_counts = jax.ops.segment_sum(jnp.ones(pool_mid.shape, jnp.float32), pool_mid, num_segments=COARSE)
    coarse_in = (coarse_sums / jnp.maximum(coarse_counts, 1.0)[:, None]).astype(jnp.bfloat16)
    coarse_new, coarse_kept = layer_forward(coarse_in, coarse_in, coarse_edges, coarse_senders, coarse_receivers, None, coarse_params)
    mid_out = (flat_mid + jnp.take(coarse_new, pool_mid, axis=0)).astype(jnp.bfloat16)
    lift_tables = mid_out.reshape(N_GRP, group_mids, feature)
    lifted = jax.vmap(lambda table, ids: jnp.take(table, ids, axis=0))(lift_tables, pool_group)
    result = (fine_group + lifted).astype(jnp.bfloat16).reshape(devices * NODE_DEV, feature)
    grad_out = cotangent.astype(jnp.float32).reshape(N_GRP, N_SUB * NODE_DEV, feature)
    grad_mid = jax.vmap(lambda values, ids: jax.ops.segment_sum(values, ids, num_segments=group_mids))(grad_out, pool_group).reshape(devices * L2_DEV, feature)
    grad_coarse = jax.ops.segment_sum(grad_mid, pool_mid, num_segments=COARSE)
    coarse_own, coarse_table, coarse_grads = layer_backward(grad_coarse, COARSE, coarse_in, coarse_senders, coarse_receivers, None, coarse_params, coarse_kept)
    grad_coarse_part = (coarse_own + coarse_table) / jnp.maximum(coarse_counts, 1.0)[:, None]
    grad_mid = grad_mid + jnp.take(grad_coarse_part, pool_mid, axis=0)
    grad_mid_dev = grad_mid.reshape(devices, L2_DEV, feature)

    def mid_group(group):

        def member_step(carry, member):
            table_sum, weight_sum = carry
            device = group * N_SUB + member
            unused_new, kept_values = layer_forward(mid_tables[group], mid_own_all[device], mid_edge_dev[device], mid_send_dev[device], mid_recv_dev[device], None, mid_params)
            grad_own, grad_table, weight_terms = layer_backward(grad_mid_dev[device], group_mids, mid_own_all[device], mid_send_dev[device], mid_recv_dev[device], None, mid_params, kept_values)
            weight_sum = jax.tree.map(lambda left, right: left + right, weight_sum, weight_terms)
            return ((table_sum + grad_table, weight_sum), grad_own)
        start = (jnp.zeros((group_mids, feature), jnp.float32), (jnp.zeros((3 * feature, feature), jnp.float32), jnp.zeros((feature, feature), jnp.float32), jnp.zeros((2 * feature, feature), jnp.float32), jnp.zeros((feature, feature), jnp.float32)))
        (table_sum, weight_sum), owns = lax.scan(member_step, start, jnp.arange(N_SUB))
        return (table_sum + owns.reshape(group_mids, feature), weight_sum)
    grad_tables, mid_weight_terms = lax.map(mid_group, jnp.arange(N_GRP))
    mid_grads = jax.tree.map(lambda stacked: lax.optimization_barrier(jnp.sum(stacked, axis=0)), mid_weight_terms)
    grad_partial = grad_tables / jnp.maximum(counts, 1.0)[:, :, None]
    grad_fine = grad_out + jax.vmap(lambda table, ids: jnp.take(table, ids, axis=0))(grad_partial, pool_group)
    grad_fine = grad_fine.reshape(devices, NODE_DEV, feature)

    def fine_backward(device):
        unused_new, kept_values = layer_forward(tables[device], node_dev[device], edge_dev[device], send_dev[device], recv_dev[device], masks[device], fine_params)
        grad_own, grad_table, weight_terms = layer_backward(grad_fine[device], NODE_DEV + 2 * halo_width, node_dev[device], send_dev[device], recv_dev[device], masks[device], fine_params, kept_values)
        return (grad_own + grad_table[:NODE_DEV], grad_table[NODE_DEV:NODE_DEV + halo_width], grad_table[NODE_DEV + halo_width:], weight_terms)
    grad_local, to_prev, to_next, fine_weight_terms = lax.map(fine_backward, jnp.arange(devices))
    fine_grads = jax.tree.map(lambda stacked: lax.optimization_barrier(jnp.sum(stacked, axis=0)), fine_weight_terms)
    blank_grad = jnp.zeros((1, halo_width, feature), jnp.float32)
    lower = jnp.concatenate([blank_grad, to_next[:-1]], axis=0)
    upper = jnp.concatenate([to_prev[1:], blank_grad], axis=0)
    returned = jax.vmap(lambda low, high, rows: jax.ops.segment_sum(low, rows[1], num_segments=NODE_DEV) + jax.ops.segment_sum(high, rows[0], num_segments=NODE_DEV))(lower, upper, halo_dev)
    grad_nodes = (grad_local + returned).reshape(devices * NODE_DEV, feature)
    stacks = [jnp.stack([fine_grads[slot], mid_grads[slot], coarse_grads[slot]]) for slot in range(4)]
    return (result, grad_nodes, stacks[0], stacks[1], stacks[2], stacks[3])
```

```python
import functools
import jax
import jax.numpy as jnp
from jax import lax
from jax.experimental import pallas as pl
from jax.experimental.pallas import tpu as pltpu
from jax.sharding import PartitionSpec as P

epsilon = 1e-05
F32 = jnp.float32
BF16 = jnp.bfloat16
LANES = 128
VMEM_LIMIT = 56 * 1024 * 1024


def dot(a, b):
    return jnp.dot(a, b, preferred_element_type=F32)


def dot_nt(a, b):
    return lax.dot_general(a, b, (((1,), (1,)), ((), ())), preferred_element_type=F32)


def dot_tn(a, b):
    return lax.dot_general(a, b, (((0,), (0,)), ((), ())), preferred_element_type=F32)


def halves(values):
    high = values.astype(BF16)
    low = (values - high.astype(F32)).astype(BF16)
    return jnp.concatenate([high, low], axis=1)


def as_columns(rows):
    count = rows.shape[0]
    return jnp.concatenate(
        [jnp.broadcast_to(rows[k : k + 1, :], (LANES, LANES)).T for k in range(count)], axis=0
    )


def one_hot(columns, width):
    lane = lax.broadcasted_iota(jnp.int32, (1, LANES), 1).astype(F32)
    return jnp.concatenate(
        [
            jnp.where(columns == lane + float(LANES * j), 1.0, 0.0).astype(BF16)
            for j in range(width // LANES)
        ],
        axis=1,
    )


def one_hot_t(rows, height):
    place = lax.broadcasted_iota(jnp.int32, (height, LANES), 0).astype(F32)
    return jnp.concatenate(
        [
            jnp.where(place == rows[k : k + 1, :], 1.0, 0.0).astype(BF16)
            for k in range(rows.shape[0])
        ],
        axis=1,
    )


def gather(columns, table2):
    half = table2.shape[0]
    upper = columns >= float(half)
    local = jnp.where(upper, columns - float(half), columns)
    both = dot(one_hot(local, half), table2)
    return jnp.where(upper, both[:, LANES:], both[:, :LANES])


def spread(rows, columns, values, half):
    local = jnp.where(rows >= float(half), rows - float(half), rows)
    upper = columns >= float(half)
    values = values.astype(F32)
    both = jnp.concatenate(
        [jnp.where(upper, 0.0, values).astype(BF16), jnp.where(upper, values, 0.0).astype(BF16)],
        axis=1,
    )
    return dot(one_hot_t(local, half), both)


def widened(weight_out):
    row_mean = jnp.broadcast_to(
        jnp.mean(weight_out.astype(F32), axis=1, keepdims=True), weight_out.shape
    )
    high = row_mean.astype(BF16)
    low = (row_mean - high.astype(F32)).astype(BF16)
    top = jnp.concatenate([weight_out, high], axis=1)
    return jnp.concatenate(
        [top, jnp.concatenate([jnp.zeros_like(weight_out), low], axis=1)], axis=0
    )


def lane_mean(values):
    return dot(values.astype(BF16), jnp.full((LANES, LANES), 1.0 / LANES, BF16))


def mlp_rest(preact, wide_out):
    sigmoid_pre = jax.nn.sigmoid(preact)
    hidden = (preact * sigmoid_pre).astype(BF16)
    both = dot(jnp.concatenate([hidden, hidden], axis=1), wide_out)
    centred = both[:, :LANES] - both[:, LANES:]
    inv_std = lax.rsqrt(lane_mean(centred * centred) + epsilon)
    return sigmoid_pre, hidden, centred * inv_std, inv_std


def fill_halves(target, source, half):
    target[:, :LANES] = source[:half, :]
    target[:, LANES:] = source[half:, :]


def forward_kernel(
    block, masked, live, send, recv, edges, table, own, edge_in, edge_out, node_in, node_out,
    new, collected, preact, table2, own2, wide, total,
):
    step = pl.program_id(0)
    table_half, own_half = table2.shape[0], own2.shape[0]

    @pl.when(step == 0)
    def _():
        fill_halves(table2, table, table_half)
        fill_halves(own2, own, own_half)
        wide[...] = widened(edge_out[...])
        total[...] = jnp.zeros_like(total)

    send_rows = send[...].reshape(block // LANES, LANES).astype(F32)
    recv_rows = recv[...].reshape(block // LANES, LANES).astype(F32)
    recv_columns = as_columns(recv_rows)
    from_send = gather(as_columns(send_rows), table2[...]).astype(BF16)
    from_recv = gather(recv_columns, own2[...]).astype(BF16)
    feat = edges[...]
    pre = dot(jnp.concatenate([from_send, from_recv], axis=1), edge_in[: 2 * LANES, :])
    pre = pre + dot(feat, edge_in[2 * LANES :, :])
    preact[...] = pre
    _, _, normed, _ = mlp_rest(pre, wide[...])
    updated = feat.astype(F32) + normed
    if masked:
        slot = step * block + lax.broadcasted_iota(jnp.int32, (block, LANES), 0)
        updated = jnp.where(slot < live[0], updated, 0.0)
    total[...] += spread(recv_rows, recv_columns, updated, own_half)

    @pl.when(step == pl.num_programs(0) - 1)
    def _():
        wide_node = widened(node_out[...])
        rows = min(own_half, 512)
        for start in range(0, 2 * own_half, rows):
            place = pl.ds(start, rows)
            if start < own_half:
                gathered = total[start : start + rows, :LANES].astype(BF16)
            else:
                gathered = total[start - own_half : start - own_half + rows, LANES:].astype(BF16)
            collected[place, :] = gathered
            mine = own[place, :]
            pre_node = dot(jnp.concatenate([mine, gathered], axis=1), node_in[...])
            _, _, node_normed, _ = mlp_rest(pre_node, wide_node)
            new[place, :] = mine.astype(F32) + node_normed


def whole(array):
    rank = array.ndim
    return pl.BlockSpec(array.shape, lambda step: (0,) * rank)


def layer_forward(table, own, edges, send, recv, live, params, block, masked):
    count, feature = edges.shape
    steps = count // block
    send3 = send.reshape(steps, block // LANES, LANES)
    recv3 = recv.reshape(steps, block // LANES, LANES)
    ids = pl.BlockSpec((1, block // LANES, LANES), lambda step: (step, 0, 0))
    edge_spec = pl.BlockSpec((block, feature), lambda step: (step, 0))
    nodes, rows = own.shape[0], table.shape[0]
    full = lambda n: pl.BlockSpec((n, feature), lambda step: (0, 0))
    return pl.pallas_call(
        functools.partial(forward_kernel, block, masked),
        grid=(steps,),
        in_specs=[pl.BlockSpec(memory_space=pltpu.SMEM), ids, ids, edge_spec, whole(table), whole(own)]
        + [whole(weight) for weight in params],
        out_specs=[full(nodes), full(nodes), edge_spec],
        out_shape=[
            jax.ShapeDtypeStruct((nodes, feature), F32),
            jax.ShapeDtypeStruct((nodes, feature), BF16),
            jax.ShapeDtypeStruct((count, feature), F32),
        ],
        scratch_shapes=[
            pltpu.VMEM((rows // 2, 2 * feature), BF16),
            pltpu.VMEM((nodes // 2, 2 * feature), BF16),
            pltpu.VMEM((2 * feature, 2 * feature), BF16),
            pltpu.VMEM((nodes // 2, 2 * feature), F32),
        ],
        compiler_params=pltpu.CompilerParams(vmem_limit_bytes=VMEM_LIMIT),
        cost_estimate=pl.CostEstimate(
            flops=2 * count * feature * (rows + 2 * nodes + 1024),
            bytes_accessed=count * feature * 8,
            transcendentals=count * feature,
        ),
    )(live, send3, recv3, edges, table, own, *params)


def backward_kernel(
    block, masked, table_out, live, send, recv, edges, preact, upstream, table, own, collected,
    edge_in, edge_out, node_in, node_out,
    *rest,
):
    grad_own, grad_edge_in, grad_edge_out, grad_node_in, grad_node_out = rest[:5]
    grad_table = rest[5] if table_out else None
    wide, grad2, send_total, recv_total = rest[-4:]
    step = pl.program_id(0)
    table_half, own_half = send_total.shape[0], recv_total.shape[0]

    @pl.when(step == 0)
    def _():
        wide[...] = widened(edge_out[...])
        send_total[...] = jnp.zeros_like(send_total)
        recv_total[...] = jnp.zeros_like(recv_total)
        grad_edge_in[...] = jnp.zeros_like(grad_edge_in)
        grad_edge_out[...] = jnp.zeros_like(grad_edge_out)
        wide_node = widened(node_out[...])
        into, out_of = node_in[...], node_out[...]
        total_in = jnp.zeros((2 * LANES, LANES), F32)
        total_out = jnp.zeros((LANES, LANES), F32)
        rows = min(own_half, 512)
        for start in range(0, 2 * own_half, rows):
            place = pl.ds(start, rows)
            inputs = jnp.concatenate([own[place, :], collected[place, :]], axis=1)
            pre = dot(inputs, into)
            sigmoid_pre, hidden, normed, inv_std = mlp_rest(pre, wide_node)
            up = upstream[place, :]
            centred_grad = (
                up
                - jnp.mean(up, axis=-1, keepdims=True)
                - normed * jnp.mean(up * normed, axis=-1, keepdims=True)
            )
            grad_output = (inv_std * centred_grad).astype(BF16)
            total_out = total_out + dot_tn(hidden, grad_output)
            grad_hidden = dot_nt(grad_output, out_of)
            grad_pre = (
                grad_hidden * sigmoid_pre * (1.0 + pre * (1.0 - sigmoid_pre))
            ).astype(BF16)
            total_in = total_in + dot_tn(inputs, grad_pre)
            back = dot_nt(grad_pre, into)
            grad_own[place, :] = up + back[:, :LANES]
            grad_collected = back[:, LANES:]
            grad_collected = grad_collected - jnp.mean(grad_collected, axis=-1, keepdims=True)
            if start < own_half:
                grad2[start : start + rows, :LANES] = grad_collected.astype(BF16)
            else:
                grad2[start - own_half : start - own_half + rows, LANES:] = grad_collected.astype(
                    BF16
                )
        grad_node_in[...] = total_in
        grad_node_out[...] = total_out

    send_rows = send[...].reshape(block // LANES, LANES).astype(F32)
    recv_rows = recv[...].reshape(block // LANES, LANES).astype(F32)
    send_columns = as_columns(send_rows)
    recv_columns = as_columns(recv_rows)
    grad_updated = gather(recv_columns, grad2[...])
    if masked:
        slot = step * block + lax.broadcasted_iota(jnp.int32, (block, LANES), 0)
        grad_updated = jnp.where(slot < live[0], grad_updated, 0.0)
    pre = preact[...]
    sigmoid_pre, hidden, normed, inv_std = mlp_rest(pre, wide[...])
    centred_grad = grad_updated - normed * lane_mean(grad_updated * normed)
    grad_output = (inv_std * centred_grad).astype(BF16)
    grad_edge_out[...] += dot_tn(hidden, grad_output)
    grad_hidden = dot_nt(grad_output, edge_out[...])
    edge_grad = (grad_hidden * sigmoid_pre * (1.0 + pre * (1.0 - sigmoid_pre))).astype(BF16)
    grad_edge_in[2 * LANES :, :] += dot_tn(edges[...], edge_grad)
    send_total[...] += spread(send_rows, send_columns, edge_grad, table_half)
    recv_total[...] += spread(recv_rows, recv_columns, edge_grad, own_half)

    @pl.when(step == pl.num_programs(0) - 1)
    def _():
        from_send = edge_in[:LANES, :]
        from_recv = edge_in[LANES : 2 * LANES, :]
        twice_send = jnp.concatenate([from_send, from_send], axis=1)
        twice_recv = jnp.concatenate([from_recv, from_recv], axis=1)
        nodes = 2 * own_half

        def part(total, half, start, rows):
            if start < half:
                return halves(total[start : start + rows, :LANES])
            return halves(total[start - half : start - half + rows, LANES:])

        weight_recv = jnp.zeros((LANES, 2 * LANES), F32)
        rows = min(own_half, 512)
        for start in range(0, nodes, rows):
            place = pl.ds(start, rows)
            split = part(recv_total, own_half, start, rows)
            weight_recv = weight_recv + dot_tn(own[place, :], split)
            grad_own[place, :] += dot_nt(split, twice_recv)
        grad_edge_in[LANES : 2 * LANES, :] = weight_recv[:, :LANES] + weight_recv[:, LANES:]

        weight_send = jnp.zeros((LANES, 2 * LANES), F32)
        for start in range(0, 2 * table_half, LANES):
            place = pl.ds(start, LANES)
            split = part(send_total, table_half, start, LANES)
            weight_send = weight_send + dot_tn(table[place, :], split)
            back = dot_nt(split, twice_send)
            if table_out == "whole":
                grad_table[place, :] = back.astype(BF16)
            elif start < nodes:
                grad_own[place, :] += back
            else:
                grad_table[pl.ds(start - nodes, LANES), :] = back.astype(BF16)
        grad_edge_in[:LANES, :] = weight_send[:, :LANES] + weight_send[:, LANES:]


def layer_backward(
    upstream, table, own, collected, edges, preact, send, recv, live, params, block, masked, table_out
):
    count, feature = edges.shape
    steps = count // block
    send3 = send.reshape(steps, block // LANES, LANES)
    recv3 = recv.reshape(steps, block // LANES, LANES)
    ids = pl.BlockSpec((1, block // LANES, LANES), lambda step: (step, 0, 0))
    edge_spec = pl.BlockSpec((block, feature), lambda step: (step, 0))
    nodes, rows = own.shape[0], table.shape[0]
    full = lambda n: pl.BlockSpec((n, feature), lambda step: (0, 0))
    out = [(nodes, F32), (3 * feature, F32), (feature, F32), (2 * feature, F32), (feature, F32)]
    if table_out == "whole":
        out.append((rows, BF16))
    elif table_out == "rest":
        out.append((rows - nodes, BF16))
    return pl.pallas_call(
        functools.partial(backward_kernel, block, masked, table_out),
        grid=(steps,),
        in_specs=[
            pl.BlockSpec(memory_space=pltpu.SMEM),
            ids,
            ids,
            edge_spec,
            edge_spec,
            full(nodes),
            full(rows),
            full(nodes),
            full(nodes),
        ]
        + [whole(weight) for weight in params],
        out_specs=[full(n) for n, _ in out],
        out_shape=[jax.ShapeDtypeStruct((n, feature), kind) for n, kind in out],
        scratch_shapes=[
            pltpu.VMEM((2 * feature, 2 * feature), BF16),
            pltpu.VMEM((nodes // 2, 2 * feature), BF16),
            pltpu.VMEM((rows // 2, 2 * feature), F32),
            pltpu.VMEM((nodes // 2, 2 * feature), F32),
        ],
        compiler_params=pltpu.CompilerParams(vmem_limit_bytes=VMEM_LIMIT),
        cost_estimate=pl.CostEstimate(
            flops=2 * count * feature * (rows + 2 * nodes + 1024),
            bytes_accessed=count * feature * 8,
            transcendentals=count * feature,
        ),
    )(live, send3, recv3, edges, preact, upstream, table, own, collected, *params)


def pool_kernel(owned, ids, left, right, out, counts):
    target = pl.program_id(0)
    rows = ids[...].astype(F32)

    @pl.when(target == 0)
    def _():
        high_rows = jnp.floor(rows * (1.0 / LANES))
        low_rows = rows - high_rows * float(LANES)
        high = one_hot_t(high_rows, counts.shape[0])
        low = one_hot_t(low_rows, LANES)
        counts[...] = dot_nt(high, low)

    base = target.astype(F32) * float(owned)
    both = jnp.concatenate([left[...].astype(BF16), right[...].astype(BF16)], axis=1)
    out[0, :owned, :] = dot(one_hot_t(rows - base, owned), both).astype(BF16)
    hits = jnp.concatenate(
        [counts[pl.ds(target * 2, 1), :], counts[pl.ds(target * 2 + 1, 1), :]], axis=1
    )
    high = jnp.floor(hits * (1.0 / 64.0))
    low = hits - high * 64.0
    tail = lax.broadcasted_iota(jnp.int32, (16, 2 * LANES), 0)
    tail = jnp.where(tail == 0, high, jnp.where(tail == 1, low, 0.0))
    out[0, owned:, :] = tail.astype(BF16)


def pool_fine_nodes(ids, left, right, parts, owned):
    count, feature = left.shape
    return pl.pallas_call(
        functools.partial(pool_kernel, owned),
        grid=(parts,),
        in_specs=[
            pl.BlockSpec((count // LANES, LANES), lambda step: (0, 0)),
            pl.BlockSpec((count, feature), lambda step: (0, 0)),
            pl.BlockSpec((count, feature), lambda step: (0, 0)),
        ],
        out_specs=pl.BlockSpec((1, owned + 16, 2 * feature), lambda step: (step, 0, 0)),
        out_shape=jax.ShapeDtypeStruct((parts, owned + 16, 2 * feature), BF16),
        scratch_shapes=[pltpu.VMEM((parts * owned // LANES, LANES), F32)],
        compiler_params=pltpu.CompilerParams(vmem_limit_bytes=VMEM_LIMIT),
        cost_estimate=pl.CostEstimate(
            flops=4 * count * parts * owned * feature, bytes_accessed=4 * count * feature, transcendentals=0
        ),
    )(ids.reshape(count // LANES, LANES), left, right)


def pool_mid_kernel(ids, left, right, out):
    rows = ids[...].astype(F32)
    both = jnp.concatenate(
        [left[...].astype(BF16), right[...].astype(BF16), jnp.ones(left.shape, BF16)], axis=1
    )
    out[...] = dot(one_hot_t(rows, out.shape[0]), both).astype(BF16)


def pool_mid_nodes(ids, left, right, targets):
    count, feature = left.shape
    return pl.pallas_call(
        pool_mid_kernel,
        out_shape=jax.ShapeDtypeStruct((targets, 3 * feature), BF16),
        compiler_params=pltpu.CompilerParams(vmem_limit_bytes=VMEM_LIMIT),
        cost_estimate=pl.CostEstimate(
            flops=6 * count * targets * feature, bytes_accessed=6 * targets * feature, transcendentals=0
        ),
    )(ids.reshape(count // LANES, LANES), left, right)


def lift_kernel(ids, base, table, out, table2):
    @pl.when(pl.program_id(0) == 0)
    def _():
        half = table2.shape[0]
        table2[:, :LANES] = table[:half, :].astype(BF16)
        table2[:, LANES:] = table[half:, :].astype(BF16)

    rows = ids[...].reshape(ids.shape[1], LANES).astype(F32)
    out[...] = (base[...].astype(F32) + gather(as_columns(rows), table2[...])).astype(out.dtype)


def lift(base, table, ids, kind):
    count, feature = base.shape
    rows = table.shape[0]
    block = min(count, 512)
    steps = count // block
    return pl.pallas_call(
        lift_kernel,
        grid=(steps,),
        in_specs=[
            pl.BlockSpec((1, block // LANES, LANES), lambda step: (step, 0, 0)),
            pl.BlockSpec((block, feature), lambda step: (step, 0)),
            pl.BlockSpec((rows, feature), lambda step: (0, 0)),
        ],
        out_specs=pl.BlockSpec((block, feature), lambda step: (step, 0)),
        out_shape=jax.ShapeDtypeStruct((count, feature), kind),
        scratch_shapes=[pltpu.VMEM((rows // 2, 2 * feature), BF16)],
        compiler_params=pltpu.CompilerParams(vmem_limit_bytes=VMEM_LIMIT),
        cost_estimate=pl.CostEstimate(
            flops=2 * count * rows * feature, bytes_accessed=8 * count * feature, transcendentals=0
        ),
    )(ids.reshape(steps, block // LANES, LANES), base, table)


def add_rows_kernel(ids, base, values, out):
    rows = ids[...].astype(F32)
    out[...] = base[...] + dot(one_hot_t(rows, out.shape[0]), values[...])


def add_rows(base, ids, values):
    return pl.pallas_call(
        add_rows_kernel,
        out_shape=jax.ShapeDtypeStruct(base.shape, base.dtype),
        compiler_params=pltpu.CompilerParams(vmem_limit_bytes=VMEM_LIMIT),
        cost_estimate=pl.CostEstimate(
            flops=2 * base.shape[0] * values.shape[0] * LANES, bytes_accessed=base.size * 8, transcendentals=0
        ),
    )(ids.reshape(-1, LANES), base, values)


def shared_out(block, axes, count):
    sent = jnp.broadcast_to(block[None], (count,) + block.shape)
    return lax.all_to_all(sent, axes, split_axis=0, concat_axis=0, tiled=True)


def summed_in(blocks, axes):
    got = lax.all_to_all(blocks, axes, split_axis=0, concat_axis=0, tiled=True)
    return jnp.sum(got.astype(F32), axis=0)


def shards(
    nodes,
    edges,
    senders,
    receivers,
    edge_live,
    halo_rows,
    pool_fine,
    mid_edges,
    mid_senders,
    mid_receivers,
    pool_mid,
    coarse_edges,
    coarse_senders,
    coarse_receivers,
    w_edge_in,
    w_edge_out,
    w_node_in,
    w_node_out,
    cotangent,
):
    every = ("grp", "sub")
    feature = nodes.shape[1]
    fine_count = nodes.shape[0]
    halo_width = halo_rows.shape[1]
    owned_mids = pool_mid.shape[0]
    sub_count = lax.axis_size("sub")
    device_count = sub_count * lax.axis_size("grp")
    group_mids = owned_mids * sub_count
    coarse_count = coarse_edges.shape[0] // 6
    stacks = (w_edge_in, w_edge_out, w_node_in, w_node_out)
    fine_params = [stack[0] for stack in stacks]
    mid_params = [stack[1] for stack in stacks]
    coarse_params = [stack[2] for stack in stacks]
    up = [(i, i + 1) for i in range(device_count - 1)]
    down = [(i + 1, i) for i in range(device_count - 1)]

    halo = jnp.take(nodes, halo_rows.reshape(-1), axis=0)
    from_prev = lax.ppermute(halo[:halo_width], every, up)
    from_next = lax.ppermute(halo[halo_width:], every, down)
    fine_table = jnp.concatenate([nodes, from_prev, from_next], axis=0)

    fine_new, fine_collected, fine_pre = layer_forward(
        fine_table, nodes, edges, senders, receivers, edge_live, fine_params, 1024, True
    )
    pooled = pool_fine_nodes(pool_fine, fine_new, cotangent, sub_count, owned_mids)
    owned = summed_in(pooled, "sub")
    owned_counts = (64.0 * owned[owned_mids] + owned[owned_mids + 1])[:, None]
    owned_counts = jnp.maximum(owned_counts, 1.0)
    mid_own = (owned[:owned_mids, :feature] / owned_counts).astype(BF16)
    grad_mid = owned[:owned_mids, feature:]
    mid_table = shared_out(mid_own, "sub", sub_count).reshape(group_mids, feature)
    mid_new, mid_collected, mid_pre = layer_forward(
        mid_table, mid_own, mid_edges, mid_senders, mid_receivers, edge_live, mid_params, 512, False
    )

    coarse_sent = pool_mid_nodes(pool_mid, mid_new, grad_mid, coarse_count)
    coarse_rows = coarse_count // device_count
    mine = summed_in(coarse_sent.reshape(device_count, coarse_rows, 3 * feature), every)
    my_scale = 1.0 / jnp.maximum(mine[:, 2 * feature :], 1.0)
    coarse_mine = jnp.concatenate(
        [mine[:, :feature] * my_scale, mine[:, feature : 2 * feature], my_scale], axis=1
    ).astype(BF16)
    coarse_all = shared_out(coarse_mine, every, device_count).reshape(coarse_count, 3 * feature)
    coarse_in = coarse_all[:, :feature]
    grad_coarse = coarse_all[:, feature : 2 * feature].astype(F32)
    coarse_scale = coarse_all[:, 2 * feature :].astype(F32)

    coarse_new, coarse_collected, coarse_pre = layer_forward(
        coarse_in, coarse_in, coarse_edges, coarse_senders, coarse_receivers, edge_live, coarse_params, 1024, False
    )
    mid_out = lift(mid_new, coarse_new, pool_mid, BF16)
    lift_table = lax.all_gather(mid_out, "sub", axis=0, tiled=True)

    coarse_back, *coarse_grads = layer_backward(
        grad_coarse,
        coarse_in,
        coarse_in,
        coarse_collected,
        coarse_edges,
        coarse_pre,
        coarse_senders,
        coarse_receivers,
        edge_live,
        coarse_params,
        1024,
        False,
        None,
    )
    grad_mid = lift(grad_mid, coarse_back * coarse_scale, pool_mid, F32)
    mid_own_grad, *mid_grads = layer_backward(
        grad_mid,
        mid_table,
        mid_own,
        mid_collected,
        mid_edges,
        mid_pre,
        mid_senders,
        mid_receivers,
        edge_live,
        mid_params,
        512,
        False,
        "whole",
    )
    mid_table_grad = mid_grads.pop()
    owned_total = mid_own_grad + summed_in(
        mid_table_grad.reshape(sub_count, owned_mids, feature), "sub"
    )
    owned_scaled = (owned_total / owned_counts).astype(BF16)
    grad_partial = shared_out(owned_scaled, "sub", sub_count).reshape(group_mids, feature)
    grad_fine = lift(cotangent, grad_partial, pool_fine, F32)
    grad_nodes, *fine_grads = layer_backward(
        grad_fine,
        fine_table,
        nodes,
        fine_collected,
        edges,
        fine_pre,
        senders,
        receivers,
        edge_live,
        fine_params,
        1024,
        True,
        "rest",
    )
    halo_grad = fine_grads.pop()
    to_prev = lax.ppermute(halo_grad[:halo_width], every, down)
    to_next = lax.ppermute(halo_grad[halo_width:], every, up)
    result = lift(fine_new, lift_table, pool_fine, BF16)
    grad_nodes = add_rows(
        grad_nodes, halo_rows, jnp.concatenate([to_prev, to_next], axis=0)
    )

    sizes = [grad.shape[0] for grad in fine_grads + mid_grads]
    flat = jnp.concatenate([grad.astype(BF16) for grad in fine_grads + mid_grads], axis=0)
    share = -(-flat.shape[0] // (16 * device_count)) * 16
    flat = jnp.pad(flat, ((0, share * device_count - flat.shape[0]), (0, 0)))
    my_sum = summed_in(flat.reshape(device_count, share, feature), every).astype(BF16)
    total = shared_out(my_sum, every, device_count).reshape(device_count * share, feature)
    total = total.astype(F32)
    pieces, start = [], 0
    for size in sizes:
        pieces.append(total[start : start + size])
        start += size
    grads = [jnp.stack([pieces[k], pieces[k + 4], coarse_grads[k]]) for k in range(4)]
    return (result, grad_nodes, grads[0], grads[1], grads[2], grads[3])


def solution(mesh):
    row, flat = P(("grp", "sub"), None), P(("grp", "sub"))
    in_specs = (row, row, flat, flat, flat, row, flat, row, flat, flat, flat) + (P(),) * 7 + (row,)
    out_specs = (row, row, P(), P(), P(), P())
    return jax.shard_map(shards, mesh=mesh, in_specs=in_specs, out_specs=out_specs, check_vma=False)
```

```python
import functools
import jax
import jax.numpy as jnp
from jax import lax
from jax.experimental import pallas as pl
from jax.experimental.pallas import tpu as pltpu
from jax.sharding import PartitionSpec as P

epsilon = 1e-05
F32 = jnp.float32
BF16 = jnp.bfloat16
LANES = 128
VMEM_LIMIT = 56 * 1024 * 1024


def dot(a, b):
    return jnp.dot(a, b, preferred_element_type=F32)


def dot_nt(a, b):
    return lax.dot_general(a, b, (((1,), (1,)), ((), ())), preferred_element_type=F32)


def dot_tn(a, b):
    return lax.dot_general(a, b, (((0,), (0,)), ((), ())), preferred_element_type=F32)


def halves(values):
    high = values.astype(BF16)
    low = (values - high.astype(F32)).astype(BF16)
    return jnp.concatenate([high, low], axis=1)


def as_columns(rows):
    count = rows.shape[0]
    return jnp.concatenate(
        [jnp.broadcast_to(rows[k : k + 1, :], (LANES, LANES)).T for k in range(count)], axis=0
    )


def parts_of(index):
    high = jnp.floor(index * (1.0 / LANES))
    return high.astype(BF16), (index - high * float(LANES)).astype(BF16)


def one_hot(columns, width):
    high, low = parts_of(columns)
    lane = lax.broadcasted_iota(jnp.int32, (1, LANES), 1).astype(F32).astype(BF16)
    one, zero = jnp.ones((), BF16), jnp.zeros((), BF16)
    base = jnp.where(low == lane, one, zero)
    return jnp.concatenate(
        [jnp.where(high == jnp.asarray(j, BF16), base, zero) for j in range(width // LANES)], axis=1
    )


def one_hot_t(rows, height):
    high, low = parts_of(rows)
    place = lax.broadcasted_iota(jnp.int32, (LANES, LANES), 0).astype(F32).astype(BF16)
    one, zero = jnp.ones((), BF16), jnp.zeros((), BF16)
    pieces = []
    for k in range(rows.shape[0]):
        base = jnp.where(place == low[k : k + 1, :], one, zero)
        pieces.append(
            jnp.concatenate(
                [
                    jnp.where(high[k : k + 1, :] == jnp.asarray(j, BF16), base, zero)
                    for j in range(height // LANES)
                ],
                axis=0,
            )
        )
    return jnp.concatenate(pieces, axis=1)


def gather(columns, table2):
    half = table2.shape[0]
    upper = columns >= float(half)
    local = jnp.where(upper, columns - float(half), columns)
    both = dot(one_hot(local, half), table2)
    return jnp.where(upper, both[:, LANES:], both[:, :LANES])


def spread(rows, columns, values, half):
    local = jnp.where(rows >= float(half), rows - float(half), rows)
    upper = columns >= float(half)
    values = values.astype(F32)
    both = jnp.concatenate(
        [jnp.where(upper, 0.0, values).astype(BF16), jnp.where(upper, values, 0.0).astype(BF16)],
        axis=1,
    )
    return dot(one_hot_t(local, half), both)


def widened(weight_out):
    row_mean = jnp.broadcast_to(
        jnp.mean(weight_out.astype(F32), axis=1, keepdims=True), weight_out.shape
    )
    high = row_mean.astype(BF16)
    low = (row_mean - high.astype(F32)).astype(BF16)
    top = jnp.concatenate([weight_out, high], axis=1)
    return jnp.concatenate(
        [top, jnp.concatenate([jnp.zeros_like(weight_out), low], axis=1)], axis=0
    )


def lane_mean(values):
    return jnp.mean(values, axis=-1, keepdims=True)


def mlp_rest(preact, wide_out):
    sigmoid_pre = jax.nn.sigmoid(preact)
    hidden = (preact * sigmoid_pre).astype(BF16)
    both = dot(jnp.concatenate([hidden, hidden], axis=1), wide_out)
    centred = both[:, :LANES] - both[:, LANES:]
    inv_std = lax.rsqrt(lane_mean(centred * centred) + epsilon)
    return sigmoid_pre, hidden, centred * inv_std, inv_std


def fill_halves(target, source, half):
    target[:, :LANES] = source[:half, :]
    target[:, LANES:] = source[half:, :]


def forward_kernel(
    block, masked, split, live, send, recv, edges, table, own, edge_in, edge_out, node_in, node_out,
    *rest,
):
    if split:
        part, preact, table2, own2, wide, total = rest
    else:
        new, collected, preact, table2, own2, wide, total = rest
    step = pl.program_id(0)
    table_half, own_half = table2.shape[0], own2.shape[0]

    @pl.when(step == 0)
    def _():
        fill_halves(table2, table, table_half)
        fill_halves(own2, own, own_half)
        wide[...] = widened(edge_out[...])
        total[...] = jnp.zeros_like(total)

    send_rows = send[...].reshape(block // LANES, LANES).astype(F32)
    recv_rows = recv[...].reshape(block // LANES, LANES).astype(F32)
    recv_columns = as_columns(recv_rows)
    from_send = gather(as_columns(send_rows), table2[...]).astype(BF16)
    from_recv = gather(recv_columns, own2[...]).astype(BF16)
    feat = edges[...]
    pre = dot(jnp.concatenate([from_send, from_recv], axis=1), edge_in[: 2 * LANES, :])
    pre = pre + dot(feat, edge_in[2 * LANES :, :])
    preact[...] = pre
    _, _, normed, _ = mlp_rest(pre, wide[...])
    updated = feat.astype(F32) + normed
    if masked:
        slot = step * block + lax.broadcasted_iota(jnp.int32, (block, LANES), 0)
        updated = jnp.where(slot < live[0], updated, 0.0)
    total[...] += spread(recv_rows, recv_columns, updated, own_half)

    @pl.when(step == pl.num_programs(0) - 1)
    def _():
        if split:
            part[:own_half, :] = total[:, :LANES]
            part[own_half:, :] = total[:, LANES:]
            return
        wide_node = widened(node_out[...])
        rows = min(own_half, 512)
        for start in range(0, 2 * own_half, rows):
            place = pl.ds(start, rows)
            if start < own_half:
                gathered = total[start : start + rows, :LANES].astype(BF16)
            else:
                gathered = total[start - own_half : start - own_half + rows, LANES:].astype(BF16)
            collected[place, :] = gathered
            mine = own[place, :]
            pre_node = dot(jnp.concatenate([mine, gathered], axis=1), node_in[...])
            _, _, node_normed, _ = mlp_rest(pre_node, wide_node)
            new[place, :] = mine.astype(F32) + node_normed


def whole(array):
    rank = array.ndim
    return pl.BlockSpec(array.shape, lambda step: (0,) * rank)


def layer_forward(table, own, edges, send, recv, live, params, block, masked, split=False):
    count, feature = edges.shape
    steps = count // block
    send3 = send.reshape(steps, block // LANES, LANES)
    recv3 = recv.reshape(steps, block // LANES, LANES)
    ids = pl.BlockSpec((1, block // LANES, LANES), lambda step: (step, 0, 0))
    edge_spec = pl.BlockSpec((block, feature), lambda step: (step, 0))
    nodes, rows = own.shape[0], table.shape[0]
    full = lambda n: pl.BlockSpec((n, feature), lambda step: (0, 0))
    return pl.pallas_call(
        functools.partial(forward_kernel, block, masked, split),
        grid=(steps,),
        in_specs=[pl.BlockSpec(memory_space=pltpu.SMEM), ids, ids, edge_spec, whole(table), whole(own)]
        + [whole(weight) for weight in params],
        out_specs=[full(nodes)] * (1 if split else 2) + [edge_spec],
        out_shape=[jax.ShapeDtypeStruct((nodes, feature), F32)]
        + ([] if split else [jax.ShapeDtypeStruct((nodes, feature), BF16)])
        + [jax.ShapeDtypeStruct((count, feature), F32)],
        scratch_shapes=[
            pltpu.VMEM((rows // 2, 2 * feature), BF16),
            pltpu.VMEM((nodes // 2, 2 * feature), BF16),
            pltpu.VMEM((2 * feature, 2 * feature), BF16),
            pltpu.VMEM((nodes // 2, 2 * feature), F32),
        ],
        compiler_params=pltpu.CompilerParams(vmem_limit_bytes=VMEM_LIMIT),
        cost_estimate=pl.CostEstimate(
            flops=2 * count * feature * (rows + 2 * nodes + 1024),
            bytes_accessed=count * feature * 8,
            transcendentals=count * feature,
        ),
    )(live, send3, recv3, edges, table, own, *params)


def node_kernel(own, mine, theirs, node_in, node_out, new, collected):
    wide_node = widened(node_out[...])
    gathered = (mine[...] + theirs[...]).astype(BF16)
    collected[...] = gathered
    pre = dot(jnp.concatenate([own[...], gathered], axis=1), node_in[...])
    _, _, normed, _ = mlp_rest(pre, wide_node)
    new[...] = own[...].astype(F32) + normed


def node_forward(own, mine, theirs, params):
    count, feature = own.shape
    block = min(count, 512)
    spec = pl.BlockSpec((block, feature), lambda step: (step, 0))
    return pl.pallas_call(
        node_kernel,
        grid=(count // block,),
        in_specs=[spec, spec, spec, whole(params[2]), whole(params[3])],
        out_specs=[spec, spec],
        out_shape=[
            jax.ShapeDtypeStruct((count, feature), F32),
            jax.ShapeDtypeStruct((count, feature), BF16),
        ],
        compiler_params=pltpu.CompilerParams(vmem_limit_bytes=VMEM_LIMIT),
        cost_estimate=pl.CostEstimate(
            flops=8 * count * feature * feature,
            bytes_accessed=16 * count * feature,
            transcendentals=count * feature,
        ),
    )(own, mine, theirs, params[2], params[3])


def backward_kernel(
    block, masked, lifted, table_out, live, send, recv, edges, preact, upstream, table, own,
    collected, edge_in, edge_out, node_in, node_out,
    *rest,
):
    if lifted:
        lift_ids, lift_table = rest[:2]
        lift2 = rest[-1]
        rest = rest[2:-1]
    grad_own, grad_edge_in, grad_edge_out, grad_node_in, grad_node_out = rest[:5]
    grad_table = rest[5] if table_out else None
    wide, grad2, send_total, recv_total = rest[-4:]
    step = pl.program_id(0)
    table_half, own_half = send_total.shape[0], recv_total.shape[0]

    @pl.when(step == 0)
    def _():
        wide[...] = widened(edge_out[...])
        send_total[...] = jnp.zeros_like(send_total)
        recv_total[...] = jnp.zeros_like(recv_total)
        grad_edge_in[...] = jnp.zeros_like(grad_edge_in)
        grad_edge_out[...] = jnp.zeros_like(grad_edge_out)
        wide_node = widened(node_out[...])
        into, out_of = node_in[...], node_out[...]
        total_in = jnp.zeros((2 * LANES, LANES), F32)
        total_out = jnp.zeros((LANES, LANES), F32)
        if lifted:
            fill_halves(lift2, lift_table, lift2.shape[0])
            ids = lift_ids[...].astype(F32)
        rows = min(own_half, 512)
        for start in range(0, 2 * own_half, rows):
            place = pl.ds(start, rows)
            inputs = jnp.concatenate([own[place, :], collected[place, :]], axis=1)
            pre = dot(inputs, into)
            sigmoid_pre, hidden, normed, inv_std = mlp_rest(pre, wide_node)
            up = upstream[place, :].astype(F32)
            if lifted:
                places = as_columns(ids[start // LANES : (start + rows) // LANES, :])
                up = up + gather(places, lift2[...])
            centred_grad = (
                up
                - jnp.mean(up, axis=-1, keepdims=True)
                - normed * jnp.mean(up * normed, axis=-1, keepdims=True)
            )
            grad_output = (inv_std * centred_grad).astype(BF16)
            total_out = total_out + dot_tn(hidden, grad_output)
            grad_hidden = dot_nt(grad_output, out_of)
            grad_pre = (
                grad_hidden * sigmoid_pre * (1.0 + pre * (1.0 - sigmoid_pre))
            ).astype(BF16)
            total_in = total_in + dot_tn(inputs, grad_pre)
            back = dot_nt(grad_pre, into)
            if table_out == "split":
                grad_table[place, :] = up + back[:, :LANES]
                grad_own[place, :] = jnp.zeros((rows, LANES), F32)
            else:
                grad_own[place, :] = up + back[:, :LANES]
            grad_collected = back[:, LANES:]
            grad_collected = grad_collected - jnp.mean(grad_collected, axis=-1, keepdims=True)
            if start < own_half:
                grad2[start : start + rows, :LANES] = grad_collected.astype(BF16)
            else:
                grad2[start - own_half : start - own_half + rows, LANES:] = grad_collected.astype(
                    BF16
                )
        grad_node_in[...] = total_in
        grad_node_out[...] = total_out

    send_rows = send[...].reshape(block // LANES, LANES).astype(F32)
    recv_rows = recv[...].reshape(block // LANES, LANES).astype(F32)
    send_columns = as_columns(send_rows)
    recv_columns = as_columns(recv_rows)
    grad_updated = gather(recv_columns, grad2[...])
    if masked:
        slot = step * block + lax.broadcasted_iota(jnp.int32, (block, LANES), 0)
        grad_updated = jnp.where(slot < live[0], grad_updated, 0.0)
    pre = preact[...]
    sigmoid_pre, hidden, normed, inv_std = mlp_rest(pre, wide[...])
    centred_grad = grad_updated - normed * lane_mean(grad_updated * normed)
    grad_output = (inv_std * centred_grad).astype(BF16)
    grad_edge_out[...] += dot_tn(hidden, grad_output)
    grad_hidden = dot_nt(grad_output, edge_out[...])
    edge_grad = (grad_hidden * sigmoid_pre * (1.0 + pre * (1.0 - sigmoid_pre))).astype(BF16)
    grad_edge_in[2 * LANES :, :] += dot_tn(edges[...], edge_grad)
    send_total[...] += spread(send_rows, send_columns, edge_grad, table_half)
    recv_total[...] += spread(recv_rows, recv_columns, edge_grad, own_half)

    @pl.when(step == pl.num_programs(0) - 1)
    def _():
        from_send = edge_in[:LANES, :]
        from_recv = edge_in[LANES : 2 * LANES, :]
        twice_send = jnp.concatenate([from_send, from_send], axis=1)
        twice_recv = jnp.concatenate([from_recv, from_recv], axis=1)
        nodes = 2 * own_half

        def part(total, half, start, rows):
            if start < half:
                return halves(total[start : start + rows, :LANES])
            return halves(total[start - half : start - half + rows, LANES:])

        weight_recv = jnp.zeros((LANES, 2 * LANES), F32)
        rows = min(own_half, 512)
        for start in range(0, nodes, rows):
            place = pl.ds(start, rows)
            split = part(recv_total, own_half, start, rows)
            weight_recv = weight_recv + dot_tn(own[place, :], split)
            grad_own[place, :] += dot_nt(split, twice_recv)
        grad_edge_in[LANES : 2 * LANES, :] = weight_recv[:, :LANES] + weight_recv[:, LANES:]

        weight_send = jnp.zeros((LANES, 2 * LANES), F32)
        for start in range(0, 2 * table_half, LANES):
            place = pl.ds(start, LANES)
            split = part(send_total, table_half, start, LANES)
            weight_send = weight_send + dot_tn(table[place, :], split)
            back = dot_nt(split, twice_send)
            if table_out == "whole":
                grad_table[place, :] = back.astype(BF16)
            elif start < nodes:
                grad_own[place, :] += back
            else:
                grad_table[pl.ds(start - nodes, LANES), :] = back.astype(BF16)
        grad_edge_in[:LANES, :] = weight_send[:, :LANES] + weight_send[:, LANES:]


def layer_backward(
    upstream, table, own, collected, edges, preact, send, recv, live, params, block, masked,
    table_out, lift_ids=None, lift_table=None,
):
    lifted = lift_ids is not None
    count, feature = edges.shape
    steps = count // block
    send3 = send.reshape(steps, block // LANES, LANES)
    recv3 = recv.reshape(steps, block // LANES, LANES)
    ids = pl.BlockSpec((1, block // LANES, LANES), lambda step: (step, 0, 0))
    edge_spec = pl.BlockSpec((block, feature), lambda step: (step, 0))
    nodes, rows = own.shape[0], table.shape[0]
    full = lambda n: pl.BlockSpec((n, feature), lambda step: (0, 0))
    out = [(nodes, F32), (3 * feature, F32), (feature, F32), (2 * feature, F32), (feature, F32)]
    if table_out == "whole":
        out.append((rows, BF16))
    elif table_out == "rest":
        out.append((rows - nodes, BF16))
    elif table_out == "split":
        out.append((nodes, F32))
    extra, extra_specs, extra_scratch = [], [], []
    if lifted:
        extra = [lift_ids.reshape(nodes // LANES, LANES), lift_table]
        extra_specs = [whole(array) for array in extra]
        extra_scratch = [pltpu.VMEM((lift_table.shape[0] // 2, 2 * feature), BF16)]
    return pl.pallas_call(
        functools.partial(backward_kernel, block, masked, lifted, table_out),
        grid=(steps,),
        in_specs=[
            pl.BlockSpec(memory_space=pltpu.SMEM),
            ids,
            ids,
            edge_spec,
            edge_spec,
            full(nodes),
            full(rows),
            full(nodes),
            full(nodes),
        ]
        + [whole(weight) for weight in params]
        + extra_specs,
        out_specs=[full(n) for n, _ in out],
        out_shape=[jax.ShapeDtypeStruct((n, feature), kind) for n, kind in out],
        scratch_shapes=[
            pltpu.VMEM((2 * feature, 2 * feature), BF16),
            pltpu.VMEM((nodes // 2, 2 * feature), BF16),
            pltpu.VMEM((rows // 2, 2 * feature), F32),
            pltpu.VMEM((nodes // 2, 2 * feature), F32),
        ]
        + extra_scratch,
        compiler_params=pltpu.CompilerParams(vmem_limit_bytes=VMEM_LIMIT),
        cost_estimate=pl.CostEstimate(
            flops=2 * count * feature * (rows + 2 * nodes + 1024),
            bytes_accessed=count * feature * 8,
            transcendentals=count * feature,
        ),
    )(live, send3, recv3, edges, preact, upstream, table, own, collected, *params, *extra)


def pool_kernel(block, counted, ids, values, out, both, counts):
    step = pl.program_id(0)
    steps = pl.num_programs(0)
    half = float(steps * block)
    rows = ids[...].astype(F32)

    @pl.when(step == 0)
    def _():
        upper = as_columns(rows) >= half
        taken = values[...].astype(F32)
        both[:, :LANES] = jnp.where(upper, 0.0, taken).astype(BF16)
        both[:, LANES:] = jnp.where(upper, taken, 0.0).astype(BF16)
        if counted:
            high_rows = jnp.floor(rows * (1.0 / LANES))
            low_rows = rows - high_rows * float(LANES)
            counts[...] = dot_nt(one_hot_t(high_rows, LANES), one_hot_t(low_rows, LANES))

    base = (step * block).astype(F32)
    local = jnp.where(rows >= half, rows - half, rows) - base
    local = jnp.where((local >= 0.0) & (local < float(block)), local, float(block))
    sums = dot(one_hot_t(local, block), both[...]).astype(BF16)
    out[0, 0, :block, :] = sums[:, :LANES]
    out[1, 0, :block, :] = sums[:, LANES:]
    if counted:
        lines = block // LANES
        for side in range(2):
            place = (side * steps + step) * lines
            hits = counts[pl.ds(place, lines), :]
            high = jnp.floor(hits * (1.0 / 64.0))
            tail = jnp.concatenate(
                [high, hits - high * 64.0, jnp.zeros((16 - 2 * lines, LANES), F32)], axis=0
            )
            out[side, 0, block:, :] = tail.astype(BF16)


def pool_fine_nodes(ids, values, parts, owned, counted):
    count, feature = values.shape
    rows = owned + (16 if counted else 0)
    pooled = pl.pallas_call(
        functools.partial(pool_kernel, owned, counted),
        grid=(parts // 2,),
        in_specs=[
            pl.BlockSpec((count // LANES, LANES), lambda step: (0, 0)),
            pl.BlockSpec((count, feature), lambda step: (0, 0)),
        ],
        out_specs=pl.BlockSpec((2, 1, rows, feature), lambda step: (0, step, 0, 0)),
        out_shape=jax.ShapeDtypeStruct((2, parts // 2, rows, feature), BF16),
        scratch_shapes=[
            pltpu.VMEM((count, 2 * feature), BF16),
            pltpu.VMEM((LANES, LANES), F32),
        ],
        compiler_params=pltpu.CompilerParams(vmem_limit_bytes=VMEM_LIMIT),
        cost_estimate=pl.CostEstimate(
            flops=2 * count * parts * owned * feature,
            bytes_accessed=4 * count * feature,
            transcendentals=0,
        ),
    )(ids.reshape(count // LANES, LANES), values)
    return pooled.reshape(parts, rows, feature)


def pool_mid_kernel(ids, left, right, out):
    rows = ids[...].astype(F32)
    both = jnp.concatenate(
        [left[...].astype(BF16), right[...].astype(BF16), jnp.ones(left.shape, BF16)], axis=1
    )
    out[...] = dot(one_hot_t(rows, out.shape[0]), both).astype(BF16)


def pool_mid_nodes(ids, left, right, targets):
    count, feature = left.shape
    return pl.pallas_call(
        pool_mid_kernel,
        out_shape=jax.ShapeDtypeStruct((targets, 3 * feature), BF16),
        compiler_params=pltpu.CompilerParams(vmem_limit_bytes=VMEM_LIMIT),
        cost_estimate=pl.CostEstimate(
            flops=6 * count * targets * feature, bytes_accessed=6 * targets * feature, transcendentals=0
        ),
    )(ids.reshape(count // LANES, LANES), left, right)


def lift_kernel(ids, base, table, out, table2):
    @pl.when(pl.program_id(0) == 0)
    def _():
        half = table2.shape[0]
        table2[:, :LANES] = table[:half, :].astype(BF16)
        table2[:, LANES:] = table[half:, :].astype(BF16)

    rows = ids[...].reshape(ids.shape[1], LANES).astype(F32)
    out[...] = (base[...].astype(F32) + gather(as_columns(rows), table2[...])).astype(out.dtype)


def lift(base, table, ids, kind):
    count, feature = base.shape
    rows = table.shape[0]
    block = min(count, 512)
    steps = count // block
    return pl.pallas_call(
        lift_kernel,
        grid=(steps,),
        in_specs=[
            pl.BlockSpec((1, block // LANES, LANES), lambda step: (step, 0, 0)),
            pl.BlockSpec((block, feature), lambda step: (step, 0)),
            pl.BlockSpec((rows, feature), lambda step: (0, 0)),
        ],
        out_specs=pl.BlockSpec((block, feature), lambda step: (step, 0)),
        out_shape=jax.ShapeDtypeStruct((count, feature), kind),
        scratch_shapes=[pltpu.VMEM((rows // 2, 2 * feature), BF16)],
        compiler_params=pltpu.CompilerParams(vmem_limit_bytes=VMEM_LIMIT),
        cost_estimate=pl.CostEstimate(
            flops=2 * count * rows * feature, bytes_accessed=8 * count * feature, transcendentals=0
        ),
    )(ids.reshape(steps, block // LANES, LANES), base, table)


def add_rows_kernel(ids, base, values, out):
    rows = ids[...].astype(F32)
    out[...] = base[...] + dot(one_hot_t(rows, out.shape[0]), values[...])


def add_rows(base, ids, values):
    return pl.pallas_call(
        add_rows_kernel,
        out_shape=jax.ShapeDtypeStruct(base.shape, base.dtype),
        compiler_params=pltpu.CompilerParams(vmem_limit_bytes=VMEM_LIMIT),
        cost_estimate=pl.CostEstimate(
            flops=2 * base.shape[0] * values.shape[0] * LANES, bytes_accessed=base.size * 8, transcendentals=0
        ),
    )(ids.reshape(-1, LANES), base, values)


def shared_out(block, axes, count):
    sent = jnp.broadcast_to(block[None], (count,) + block.shape)
    return lax.all_to_all(sent, axes, split_axis=0, concat_axis=0, tiled=True)


def summed_in(blocks, axes):
    got = lax.all_to_all(blocks, axes, split_axis=0, concat_axis=0, tiled=True)
    return jnp.sum(got.astype(F32), axis=0)


def shards(
    nodes,
    edges,
    senders,
    receivers,
    edge_live,
    halo_rows,
    pool_fine,
    mid_edges,
    mid_senders,
    mid_receivers,
    pool_mid,
    coarse_edges,
    coarse_senders,
    coarse_receivers,
    w_edge_in,
    w_edge_out,
    w_node_in,
    w_node_out,
    cotangent,
):
    every = ("grp", "sub")
    feature = nodes.shape[1]
    fine_count = nodes.shape[0]
    halo_width = halo_rows.shape[1]
    owned_mids = pool_mid.shape[0]
    sub_count = lax.axis_size("sub")
    device_count = sub_count * lax.axis_size("grp")
    group_mids = owned_mids * sub_count
    coarse_count = coarse_edges.shape[0] // 6
    stacks = (w_edge_in, w_edge_out, w_node_in, w_node_out)
    fine_params = [stack[0] for stack in stacks]
    mid_params = [stack[1] for stack in stacks]
    coarse_params = [stack[2] for stack in stacks]
    up = [(i, i + 1) for i in range(device_count - 1)]
    down = [(i + 1, i) for i in range(device_count - 1)]

    pairs = [(i, i ^ 1) for i in range(lax.axis_size("grp"))]
    halo = jnp.take(nodes, halo_rows.reshape(-1), axis=0)
    from_prev = lax.ppermute(halo[:halo_width], every, up)
    from_next = lax.ppermute(halo[halo_width:], every, down)
    lift_sent = pool_fine_nodes(pool_fine, cotangent, sub_count, owned_mids, False)
    lift_sent, from_prev, from_next = lax.optimization_barrier((lift_sent, from_prev, from_next))
    grad_mid = lax.psum_scatter(
        lift_sent.reshape(group_mids, feature), "sub", scatter_dimension=0, tiled=True
    ).astype(F32)
    fine_table = jnp.concatenate([nodes, from_prev, from_next], axis=0)

    fine_new, fine_collected, fine_pre = layer_forward(
        fine_table, nodes, edges, senders, receivers, edge_live, fine_params, 4096, True
    )
    pooled = pool_fine_nodes(pool_fine, fine_new, sub_count, owned_mids, True)
    owned = summed_in(pooled, "sub")
    lines = owned_mids // feature
    tail = owned[owned_mids : owned_mids + 2 * lines]
    owned_counts = (64.0 * tail[:lines] + tail[lines:]).reshape(owned_mids, 1)
    owned_counts = jnp.maximum(owned_counts, 1.0)
    mid_own = (owned[:owned_mids] / owned_counts).astype(BF16)
    mid_table = shared_out(mid_own, "sub", sub_count).reshape(group_mids, feature)
    mid_new, mid_collected, mid_pre = layer_forward(
        mid_table, mid_own, mid_edges, mid_senders, mid_receivers, edge_live, mid_params, 512, False
    )

    coarse_sent = pool_mid_nodes(pool_mid, mid_new, grad_mid, coarse_count)
    coarse_rows = coarse_count // device_count
    mine = summed_in(coarse_sent.reshape(device_count, coarse_rows, 3 * feature), every)
    my_scale = 1.0 / jnp.maximum(mine[:, 2 * feature :], 1.0)
    coarse_mine = jnp.concatenate(
        [mine[:, :feature] * my_scale, mine[:, feature : 2 * feature], my_scale], axis=1
    ).astype(BF16)
    coarse_all = shared_out(coarse_mine, every, device_count).reshape(coarse_count, 3 * feature)
    coarse_in = coarse_all[:, :feature]
    grad_coarse = coarse_all[:, feature : 2 * feature].astype(F32)
    coarse_scale = coarse_all[:, 2 * feature :].astype(F32)

    half_edges = coarse_edges.shape[0] // 2
    first = lax.rem(lax.axis_index("grp"), 2) * half_edges
    my_edges = lax.dynamic_slice_in_dim(coarse_edges, first, half_edges)
    my_senders = lax.dynamic_slice_in_dim(coarse_senders, first, half_edges)
    my_receivers = lax.dynamic_slice_in_dim(coarse_receivers, first, half_edges)
    coarse_part, coarse_pre = layer_forward(
        coarse_in, coarse_in, my_edges, my_senders, my_receivers, edge_live, coarse_params, 3072, False, True
    )
    coarse_other = lax.ppermute(coarse_part, "grp", pairs)
    coarse_new, coarse_collected = node_forward(
        coarse_in, coarse_part, coarse_other, coarse_params
    )
    mid_out = lift(mid_new, coarse_new, pool_mid, BF16)
    lift_table = lax.all_gather(mid_out, "sub", axis=0, tiled=True)

    coarse_back, *coarse_grads, coarse_base = layer_backward(
        grad_coarse,
        coarse_in,
        coarse_in,
        coarse_collected,
        my_edges,
        coarse_pre,
        my_senders,
        my_receivers,
        edge_live,
        coarse_params,
        3072,
        False,
        "split",
    )
    coarse_back = coarse_back + lax.ppermute(coarse_back, "grp", pairs) + coarse_base
    for k in range(2):
        coarse_grads[k] = coarse_grads[k] + lax.ppermute(coarse_grads[k], "grp", pairs)
    mid_own_grad, *mid_grads = layer_backward(
        grad_mid,
        mid_table,
        mid_own,
        mid_collected,
        mid_edges,
        mid_pre,
        mid_senders,
        mid_receivers,
        edge_live,
        mid_params,
        512,
        False,
        "whole",
        pool_mid,
        (coarse_back * coarse_scale).astype(BF16),
    )
    mid_table_grad = mid_grads.pop()
    owned_total = mid_own_grad + summed_in(
        mid_table_grad.reshape(sub_count, owned_mids, feature), "sub"
    )
    owned_scaled = (owned_total / owned_counts).astype(BF16)
    grad_partial = shared_out(owned_scaled, "sub", sub_count).reshape(group_mids, feature)
    grad_nodes, *fine_grads = layer_backward(
        cotangent,
        fine_table,
        nodes,
        fine_collected,
        edges,
        fine_pre,
        senders,
        receivers,
        edge_live,
        fine_params,
        4096,
        True,
        "rest",
        pool_fine,
        grad_partial,
    )
    halo_grad = fine_grads.pop()
    to_prev = lax.ppermute(halo_grad[:halo_width], every, down)
    to_next = lax.ppermute(halo_grad[halo_width:], every, up)
    result = lift(fine_new, lift_table, pool_fine, BF16)
    grad_nodes = add_rows(
        grad_nodes, halo_rows, jnp.concatenate([to_prev, to_next], axis=0)
    )

    sizes = [grad.shape[0] for grad in fine_grads + mid_grads]
    flat = jnp.concatenate([grad.astype(BF16) for grad in fine_grads + mid_grads], axis=0)
    share = -(-flat.shape[0] // (16 * device_count)) * 16
    flat = jnp.pad(flat, ((0, share * device_count - flat.shape[0]), (0, 0)))
    my_sum = summed_in(flat.reshape(device_count, share, feature), every).astype(BF16)
    total = shared_out(my_sum, every, device_count).reshape(device_count * share, feature)
    total = total.astype(F32)
    pieces, start = [], 0
    for size in sizes:
        pieces.append(total[start : start + size])
        start += size
    grads = [jnp.stack([pieces[k], pieces[k + 4], coarse_grads[k]]) for k in range(4)]
    return (result, grad_nodes, grads[0], grads[1], grads[2], grads[3])


def solution(mesh):
    row, flat = P(("grp", "sub"), None), P(("grp", "sub"))
    in_specs = (row, row, flat, flat, flat, row, flat, row, flat, flat, flat) + (P(),) * 7 + (row,)
    out_specs = (row, row, P(), P(), P(), P())
    return jax.shard_map(shards, mesh=mesh, in_specs=in_specs, out_specs=out_specs, check_vma=False)
```

```python
import functools
import jax
import jax.numpy as jnp
from jax import lax
from jax.experimental import pallas as pl
from jax.experimental.pallas import tpu as pltpu
from jax.sharding import PartitionSpec as P

epsilon = 1e-05
F32 = jnp.float32
BF16 = jnp.bfloat16
LANES = 128
VMEM_LIMIT = 56 * 1024 * 1024


def dot(a, b):
    return jnp.dot(a, b, preferred_element_type=F32)


def dot_nt(a, b):
    return lax.dot_general(a, b, (((1,), (1,)), ((), ())), preferred_element_type=F32)


def dot_tn(a, b):
    return lax.dot_general(a, b, (((0,), (0,)), ((), ())), preferred_element_type=F32)


def halves(values):
    high = values.astype(BF16)
    low = (values - high.astype(F32)).astype(BF16)
    return jnp.concatenate([high, low], axis=1)


def as_columns(rows):
    count = rows.shape[0]
    return jnp.concatenate(
        [jnp.broadcast_to(rows[k : k + 1, :], (LANES, LANES)).T for k in range(count)], axis=0
    )


def parts_of(index):
    high = jnp.floor(index * (1.0 / LANES))
    return high.astype(BF16), (index - high * float(LANES)).astype(BF16)


def one_hot(columns, width):
    high, low = parts_of(columns)
    lane = lax.broadcasted_iota(jnp.int32, (1, LANES), 1).astype(F32).astype(BF16)
    one, zero = jnp.ones((), BF16), jnp.zeros((), BF16)
    base = jnp.where(low == lane, one, zero)
    return jnp.concatenate(
        [jnp.where(high == jnp.asarray(j, BF16), base, zero) for j in range(width // LANES)], axis=1
    )


def one_hot_t(rows, height):
    high, low = parts_of(rows)
    place = lax.broadcasted_iota(jnp.int32, (LANES, LANES), 0).astype(F32).astype(BF16)
    one, zero = jnp.ones((), BF16), jnp.zeros((), BF16)
    pieces = []
    for k in range(rows.shape[0]):
        base = jnp.where(place == low[k : k + 1, :], one, zero)
        pieces.append(
            jnp.concatenate(
                [
                    jnp.where(high[k : k + 1, :] == jnp.asarray(j, BF16), base, zero)
                    for j in range(height // LANES)
                ],
                axis=0,
            )
        )
    return jnp.concatenate(pieces, axis=1)


def gather(columns, table2):
    half = table2.shape[0]
    upper = columns >= float(half)
    local = jnp.where(upper, columns - float(half), columns)
    both = dot(one_hot(local, half), table2)
    return jnp.where(upper, both[:, LANES:], both[:, :LANES])


def spread(rows, columns, values, half):
    local = jnp.where(rows >= float(half), rows - float(half), rows)
    upper = columns >= float(half)
    values = values.astype(F32)
    both = jnp.concatenate(
        [jnp.where(upper, 0.0, values).astype(BF16), jnp.where(upper, values, 0.0).astype(BF16)],
        axis=1,
    )
    return dot(one_hot_t(local, half), both)


def widened(weight_out):
    row_mean = jnp.broadcast_to(
        jnp.mean(weight_out.astype(F32), axis=1, keepdims=True), weight_out.shape
    )
    high = row_mean.astype(BF16)
    low = (row_mean - high.astype(F32)).astype(BF16)
    top = jnp.concatenate([weight_out, high], axis=1)
    return jnp.concatenate(
        [top, jnp.concatenate([jnp.zeros_like(weight_out), low], axis=1)], axis=0
    )


def lane_mean(values):
    return jnp.mean(values, axis=-1, keepdims=True)


def mlp_rest(preact, wide_out):
    sigmoid_pre = jax.nn.sigmoid(preact)
    hidden = (preact * sigmoid_pre).astype(BF16)
    both = dot(jnp.concatenate([hidden, hidden], axis=1), wide_out)
    centred = both[:, :LANES] - both[:, LANES:]
    inv_std = lax.rsqrt(lane_mean(centred * centred) + epsilon)
    return sigmoid_pre, hidden, centred * inv_std, inv_std


def fill_halves(target, source, half):
    target[:, :LANES] = source[:half, :]
    target[:, LANES:] = source[half:, :]


def forward_kernel(
    block, masked, split, live, send, recv, edges, table, own, edge_in, edge_out, node_in, node_out,
    *rest,
):
    if split:
        part, preact, table2, own2, wide, total = rest
    else:
        new, collected, preact, table2, own2, wide, total = rest
    step = pl.program_id(0)
    table_half, own_half = table2.shape[0], own2.shape[0]

    @pl.when(step == 0)
    def _():
        fill_halves(table2, table, table_half)
        fill_halves(own2, own, own_half)
        wide[...] = widened(edge_out[...])
        total[...] = jnp.zeros_like(total)

    send_rows = send[...].reshape(block // LANES, LANES).astype(F32)
    recv_rows = recv[...].reshape(block // LANES, LANES).astype(F32)
    recv_columns = as_columns(recv_rows)
    from_send = gather(as_columns(send_rows), table2[...]).astype(BF16)
    from_recv = gather(recv_columns, own2[...]).astype(BF16)
    feat = edges[...]
    pre = dot(jnp.concatenate([from_send, from_recv], axis=1), edge_in[: 2 * LANES, :])
    pre = pre + dot(feat, edge_in[2 * LANES :, :])
    preact[...] = pre
    _, _, normed, _ = mlp_rest(pre, wide[...])
    updated = feat.astype(F32) + normed
    if masked:
        slot = step * block + lax.broadcasted_iota(jnp.int32, (block, LANES), 0)
        updated = jnp.where(slot < live[0], updated, 0.0)
    total[...] += spread(recv_rows, recv_columns, updated, own_half)

    @pl.when(step == pl.num_programs(0) - 1)
    def _():
        if split:
            part[:own_half, :] = total[:, :LANES]
            part[own_half:, :] = total[:, LANES:]
            return
        wide_node = widened(node_out[...])
        rows = min(own_half, 512)
        for start in range(0, 2 * own_half, rows):
            place = pl.ds(start, rows)
            if start < own_half:
                gathered = total[start : start + rows, :LANES].astype(BF16)
            else:
                gathered = total[start - own_half : start - own_half + rows, LANES:].astype(BF16)
            collected[place, :] = gathered
            mine = own[place, :]
            pre_node = dot(jnp.concatenate([mine, gathered], axis=1), node_in[...])
            _, _, node_normed, _ = mlp_rest(pre_node, wide_node)
            new[place, :] = mine.astype(F32) + node_normed


def whole(array):
    rank = array.ndim
    return pl.BlockSpec(array.shape, lambda step: (0,) * rank)


def level_specs(params):
    stacks, level = params
    return [
        pl.BlockSpec((None,) + stack.shape[1:], lambda step: (level, 0, 0)) for stack in stacks
    ]


def column_block(source):
    array, column = source if isinstance(source, tuple) else (source, 0)
    return array, pl.BlockSpec((array.shape[0], LANES), lambda step: (0, column))


def layer_forward(table, own, edges, send, recv, live, params, block, masked, split=False):
    count, feature = edges.shape
    (table, table_spec), (own, own_spec) = column_block(table), column_block(own)
    steps = count // block
    send3 = send.reshape(steps, block // LANES, LANES)
    recv3 = recv.reshape(steps, block // LANES, LANES)
    ids = pl.BlockSpec((1, block // LANES, LANES), lambda step: (step, 0, 0))
    edge_spec = pl.BlockSpec((block, feature), lambda step: (step, 0))
    nodes, rows = own.shape[0], table.shape[0]
    full = lambda n: pl.BlockSpec((n, feature), lambda step: (0, 0))
    return pl.pallas_call(
        functools.partial(forward_kernel, block, masked, split),
        grid=(steps,),
        in_specs=[pl.BlockSpec(memory_space=pltpu.SMEM), ids, ids, edge_spec, table_spec, own_spec]
        + level_specs(params),
        out_specs=[full(nodes)] * (1 if split else 2) + [edge_spec],
        out_shape=[jax.ShapeDtypeStruct((nodes, feature), F32)]
        + ([] if split else [jax.ShapeDtypeStruct((nodes, feature), BF16)])
        + [jax.ShapeDtypeStruct((count, feature), F32)],
        scratch_shapes=[
            pltpu.VMEM((rows // 2, 2 * feature), BF16),
            pltpu.VMEM((nodes // 2, 2 * feature), BF16),
            pltpu.VMEM((2 * feature, 2 * feature), BF16),
            pltpu.VMEM((nodes // 2, 2 * feature), F32),
        ],
        compiler_params=pltpu.CompilerParams(vmem_limit_bytes=VMEM_LIMIT),
        cost_estimate=pl.CostEstimate(
            flops=2 * count * feature * (rows + 2 * nodes + 1024),
            bytes_accessed=count * feature * 8,
            transcendentals=count * feature,
        ),
    )(live, send3, recv3, edges, table, own, *params[0])


def backward_kernel(
    block, masked, lifted, table_out, live, send, recv, edges, preact, upstream, table, own,
    collected, edge_in, edge_out, node_in, node_out,
    *rest,
):
    split = table_out == "split"
    if split:
        other, rest = rest[0], rest[1:]
    if lifted:
        lift_ids, lift_tables = rest[0], rest[1 : 1 + lifted]
        lift2 = rest[-1]
        rest = rest[1 + lifted : -1]
    grad_own, grads = rest[:2]
    grad_edge_in = grads.at[pl.ds(0, 3 * LANES), :]
    grad_edge_out = grads.at[pl.ds(3 * LANES, LANES), :]
    grad_node_in = grads.at[pl.ds(4 * LANES, 2 * LANES), :]
    grad_node_out = grads.at[pl.ds(6 * LANES, LANES), :]
    grad_table = rest[2] if table_out else None
    new = rest[3] if split else None
    wide, grad2, send_total, recv_total = rest[-4:]
    step = pl.program_id(0)
    table_half, own_half = send_total.shape[0], recv_total.shape[0]

    @pl.when(step == 0)
    def _():
        wide[...] = widened(edge_out[...])
        send_total[...] = jnp.zeros_like(send_total)
        recv_total[...] = jnp.zeros_like(recv_total)
        grad_edge_in[...] = jnp.zeros_like(grad_edge_in)
        grad_edge_out[...] = jnp.zeros_like(grad_edge_out)
        wide_node = widened(node_out[...])
        into, out_of = node_in[...], node_out[...]
        total_in = jnp.zeros((2 * LANES, LANES), F32)
        total_out = jnp.zeros((LANES, LANES), F32)
        if lifted:
            height = lift2.shape[0]
            for side in range(2):
                lines = pl.ds(side * height, height)
                term = lift_tables[0][lines, :]
                if lifted > 1:
                    for more in lift_tables[1:-1]:
                        term = term + more[lines, :]
                    term = term * lift_tables[-1][lines, :].astype(F32)
                lift2[:, side * LANES : (side + 1) * LANES] = term.astype(BF16)
            ids = lift_ids[...].astype(F32)
        rows = min(own_half, 512)
        for start in range(0, 2 * own_half, rows):
            place = pl.ds(start, rows)
            taken = collected[place, :]
            if split:
                taken = (taken + other[place, :]).astype(BF16)
            inputs = jnp.concatenate([own[place, :], taken], axis=1)
            pre = dot(inputs, into)
            sigmoid_pre, hidden, normed, inv_std = mlp_rest(pre, wide_node)
            up = upstream[place, :].astype(F32)
            if lifted:
                places = as_columns(ids[start // LANES : (start + rows) // LANES, :])
                up = up + gather(places, lift2[...])
            centred_grad = (
                up
                - jnp.mean(up, axis=-1, keepdims=True)
                - normed * jnp.mean(up * normed, axis=-1, keepdims=True)
            )
            grad_output = (inv_std * centred_grad).astype(BF16)
            total_out = total_out + dot_tn(hidden, grad_output)
            grad_hidden = dot_nt(grad_output, out_of)
            grad_pre = (
                grad_hidden * sigmoid_pre * (1.0 + pre * (1.0 - sigmoid_pre))
            ).astype(BF16)
            total_in = total_in + dot_tn(inputs, grad_pre)
            back = dot_nt(grad_pre, into)
            if split:
                new[place, :] = own[place, :].astype(F32) + normed
                grad_table[place, :] = up + back[:, :LANES]
                grad_own[place, :] = jnp.zeros((rows, LANES), F32)
            else:
                grad_own[place, :] = up + back[:, :LANES]
            grad_collected = back[:, LANES:]
            grad_collected = grad_collected - jnp.mean(grad_collected, axis=-1, keepdims=True)
            if start < own_half:
                grad2[start : start + rows, :LANES] = grad_collected.astype(BF16)
            else:
                grad2[start - own_half : start - own_half + rows, LANES:] = grad_collected.astype(
                    BF16
                )
        grad_node_in[...] = total_in
        grad_node_out[...] = total_out

    send_rows = send[...].reshape(block // LANES, LANES).astype(F32)
    recv_rows = recv[...].reshape(block // LANES, LANES).astype(F32)
    send_columns = as_columns(send_rows)
    recv_columns = as_columns(recv_rows)
    grad_updated = gather(recv_columns, grad2[...])
    if masked:
        slot = step * block + lax.broadcasted_iota(jnp.int32, (block, LANES), 0)
        grad_updated = jnp.where(slot < live[0], grad_updated, 0.0)
    pre = preact[...]
    sigmoid_pre, hidden, normed, inv_std = mlp_rest(pre, wide[...])
    centred_grad = grad_updated - normed * lane_mean(grad_updated * normed)
    grad_output = (inv_std * centred_grad).astype(BF16)
    grad_edge_out[...] += dot_tn(hidden, grad_output)
    grad_hidden = dot_nt(grad_output, edge_out[...])
    edge_grad = (grad_hidden * sigmoid_pre * (1.0 + pre * (1.0 - sigmoid_pre))).astype(BF16)
    grad_edge_in[2 * LANES :, :] += dot_tn(edges[...], edge_grad)
    send_total[...] += spread(send_rows, send_columns, edge_grad, table_half)
    recv_total[...] += spread(recv_rows, recv_columns, edge_grad, own_half)

    @pl.when(step == pl.num_programs(0) - 1)
    def _():
        from_send = edge_in[:LANES, :]
        from_recv = edge_in[LANES : 2 * LANES, :]
        twice_send = jnp.concatenate([from_send, from_send], axis=1)
        twice_recv = jnp.concatenate([from_recv, from_recv], axis=1)
        nodes = 2 * own_half

        def part(total, half, start, rows):
            if start < half:
                return halves(total[start : start + rows, :LANES])
            return halves(total[start - half : start - half + rows, LANES:])

        weight_recv = jnp.zeros((LANES, 2 * LANES), F32)
        rows = min(own_half, 512)
        for start in range(0, nodes, rows):
            place = pl.ds(start, rows)
            recv_sum = part(recv_total, own_half, start, rows)
            weight_recv = weight_recv + dot_tn(own[place, :], recv_sum)
            grad_own[place, :] += dot_nt(recv_sum, twice_recv)
        grad_edge_in[LANES : 2 * LANES, :] = weight_recv[:, :LANES] + weight_recv[:, LANES:]

        weight_send = jnp.zeros((LANES, 2 * LANES), F32)
        cuts = sorted({0, table_half, nodes, 2 * table_half} if nodes > table_half else {0, table_half, 2 * table_half})
        pieces = []
        for first, last in zip(cuts[:-1], cuts[1:]):
            pieces += [(k, min(1152, last - k)) for k in range(first, last, 1152)]
        for start, rows in pieces:
            place = pl.ds(start, rows)
            split_sum = part(send_total, table_half, start, rows)
            weight_send = weight_send + dot_tn(table[place, :], split_sum)
            back = dot_nt(split_sum, twice_send)
            if table_out == "whole":
                grad_table[place, :] = back.astype(BF16)
            elif start < nodes:
                grad_own[place, :] += back
            else:
                grad_table[pl.ds(start - nodes, rows), :] = back.astype(BF16)
        grad_edge_in[:LANES, :] = weight_send[:, :LANES] + weight_send[:, LANES:]


def layer_backward(
    upstream, table, own, collected, edges, preact, send, recv, live, params, block, masked,
    table_out, lift_ids=None, lift_tables=(), other=None,
):
    lifted = len(lift_tables)
    (table, table_spec), (own, own_spec) = column_block(table), column_block(own)
    upstream, upstream_spec = column_block(upstream)
    count, feature = edges.shape
    steps = count // block
    send3 = send.reshape(steps, block // LANES, LANES)
    recv3 = recv.reshape(steps, block // LANES, LANES)
    ids = pl.BlockSpec((1, block // LANES, LANES), lambda step: (step, 0, 0))
    edge_spec = pl.BlockSpec((block, feature), lambda step: (step, 0))
    nodes, rows = own.shape[0], table.shape[0]
    full = lambda n: pl.BlockSpec((n, feature), lambda step: (0, 0))
    out = [(nodes, F32), (7 * feature, F32)]
    if table_out == "whole":
        out.append((rows, BF16))
    elif table_out == "rest":
        out.append((rows - nodes, BF16))
    elif table_out == "split":
        out += [(nodes, F32), (nodes, F32)]
    extra, extra_specs, extra_scratch = [], [], []
    if other is not None:
        extra.append(other)
        extra_specs.append(whole(other))
    if lifted:
        lift_ids = lift_ids.reshape(nodes // LANES, LANES)
        extra.append(lift_ids)
        extra_specs.append(whole(lift_ids))
        for source in lift_tables:
            array, spec = column_block(source)
            extra.append(array)
            extra_specs.append(spec)
        extra_scratch = [pltpu.VMEM((array.shape[0] // 2, 2 * feature), BF16)]
    return pl.pallas_call(
        functools.partial(backward_kernel, block, masked, lifted, table_out),
        grid=(steps,),
        in_specs=[
            pl.BlockSpec(memory_space=pltpu.SMEM),
            ids,
            ids,
            edge_spec,
            edge_spec,
            upstream_spec,
            table_spec,
            own_spec,
            full(nodes),
        ]
        + level_specs(params)
        + extra_specs,
        out_specs=[full(n) for n, _ in out],
        out_shape=[jax.ShapeDtypeStruct((n, feature), kind) for n, kind in out],
        scratch_shapes=[
            pltpu.VMEM((2 * feature, 2 * feature), BF16),
            pltpu.VMEM((nodes // 2, 2 * feature), BF16),
            pltpu.VMEM((rows // 2, 2 * feature), F32),
            pltpu.VMEM((nodes // 2, 2 * feature), F32),
        ]
        + extra_scratch,
        compiler_params=pltpu.CompilerParams(vmem_limit_bytes=VMEM_LIMIT),
        cost_estimate=pl.CostEstimate(
            flops=2 * count * feature * (rows + 2 * nodes + 1024),
            bytes_accessed=count * feature * 8,
            transcendentals=count * feature,
        ),
    )(live, send3, recv3, edges, preact, upstream, table, own, collected, *params[0], *extra)


def pool_kernel(owned, ids, left, right, out, counts):
    step = pl.program_id(0)
    group = out.shape[0]
    rows = ids[...].astype(F32)

    @pl.when(step == 0)
    def _():
        high_rows = jnp.floor(rows * (1.0 / LANES))
        low_rows = rows - high_rows * float(LANES)
        counts[...] = dot_nt(one_hot_t(high_rows, LANES), one_hot_t(low_rows, LANES))

    span = group * owned
    local = rows - (step * span).astype(F32)
    local = jnp.where((local >= 0.0) & (local < float(span)), local, float(span))
    both = jnp.concatenate([left[...].astype(BF16), right[...].astype(BF16)], axis=1)
    sums = dot(one_hot_t(local, span), both).astype(BF16)
    lines = owned // LANES
    for k in range(group):
        out[k, :owned, :] = sums[k * owned : (k + 1) * owned, :]
        hits = counts[pl.ds((step * group + k) * lines, lines), :]
        high = jnp.floor(hits * (1.0 / 64.0))
        tail = jnp.concatenate(
            [high, hits - high * 64.0, jnp.zeros((16 - 2 * lines, LANES), F32)], axis=0
        )
        out[k, owned:, :] = jnp.concatenate([tail, jnp.zeros_like(tail)], axis=1).astype(BF16)


def pool_fine_nodes(ids, left, right, parts, owned):
    count, feature = left.shape
    group = 4
    rows = owned + 16
    full = pl.BlockSpec((count, feature), lambda step: (0, 0))
    return pl.pallas_call(
        functools.partial(pool_kernel, owned),
        grid=(parts // group,),
        in_specs=[pl.BlockSpec((count // LANES, LANES), lambda step: (0, 0)), full, full],
        out_specs=pl.BlockSpec((group, rows, 2 * feature), lambda step: (step, 0, 0)),
        out_shape=jax.ShapeDtypeStruct((parts, rows, 2 * feature), BF16),
        scratch_shapes=[pltpu.VMEM((LANES, LANES), F32)],
        compiler_params=pltpu.CompilerParams(vmem_limit_bytes=VMEM_LIMIT),
        cost_estimate=pl.CostEstimate(
            flops=4 * count * parts * owned * feature,
            bytes_accessed=4 * count * feature,
            transcendentals=0,
        ),
    )(ids.reshape(count // LANES, LANES), left, right)


def pool_mid_kernel(ids, left, right, out):
    rows = ids[...].astype(F32)
    both = jnp.concatenate(
        [left[...].astype(BF16), right[...].astype(BF16), jnp.ones(left.shape, BF16)], axis=1
    )
    out[...] = dot(one_hot_t(rows, out.shape[0]), both).astype(BF16)


def pool_mid_nodes(ids, left, right, targets):
    count, feature = left.shape
    return pl.pallas_call(
        pool_mid_kernel,
        out_shape=jax.ShapeDtypeStruct((targets, 3 * feature), BF16),
        compiler_params=pltpu.CompilerParams(vmem_limit_bytes=VMEM_LIMIT),
        cost_estimate=pl.CostEstimate(
            flops=6 * count * targets * feature, bytes_accessed=6 * targets * feature, transcendentals=0
        ),
    )(ids.reshape(count // LANES, LANES), left, right)


def lift_kernel(ids, base, table, out, table2):
    @pl.when(pl.program_id(0) == 0)
    def _():
        half = table2.shape[0]
        table2[:, :LANES] = table[:half, :].astype(BF16)
        table2[:, LANES:] = table[half:, :].astype(BF16)

    rows = ids[...].reshape(ids.shape[1], LANES).astype(F32)
    out[...] = (base[...].astype(F32) + gather(as_columns(rows), table2[...])).astype(out.dtype)


def lift(base, table, ids, kind):
    count, feature = base.shape
    rows = table.shape[0]
    block = min(count, 512)
    steps = count // block
    return pl.pallas_call(
        lift_kernel,
        grid=(steps,),
        in_specs=[
            pl.BlockSpec((1, block // LANES, LANES), lambda step: (step, 0, 0)),
            pl.BlockSpec((block, feature), lambda step: (step, 0)),
            pl.BlockSpec((rows, feature), lambda step: (0, 0)),
        ],
        out_specs=pl.BlockSpec((block, feature), lambda step: (step, 0)),
        out_shape=jax.ShapeDtypeStruct((count, feature), kind),
        scratch_shapes=[pltpu.VMEM((rows // 2, 2 * feature), BF16)],
        compiler_params=pltpu.CompilerParams(vmem_limit_bytes=VMEM_LIMIT),
        cost_estimate=pl.CostEstimate(
            flops=2 * count * rows * feature, bytes_accessed=8 * count * feature, transcendentals=0
        ),
    )(ids.reshape(steps, block // LANES, LANES), base, table)


def add_rows_kernel(ids, base, values, out):
    rows = ids[...].astype(F32)
    out[...] = base[...] + dot(one_hot_t(rows, out.shape[0]), values[...])


def add_rows(base, ids, values):
    return pl.pallas_call(
        add_rows_kernel,
        out_shape=jax.ShapeDtypeStruct(base.shape, base.dtype),
        compiler_params=pltpu.CompilerParams(vmem_limit_bytes=VMEM_LIMIT),
        cost_estimate=pl.CostEstimate(
            flops=2 * base.shape[0] * values.shape[0] * LANES, bytes_accessed=base.size * 8, transcendentals=0
        ),
    )(ids.reshape(-1, LANES), base, values)


def shared_out(block, axes, count):
    sent = jnp.broadcast_to(block[None], (count,) + block.shape)
    return lax.all_to_all(sent, axes, split_axis=0, concat_axis=0, tiled=True)


def summed_in(blocks, axes):
    got = lax.all_to_all(blocks, axes, split_axis=0, concat_axis=0, tiled=True)
    return jnp.sum(got.astype(F32), axis=0)


def shards(
    nodes,
    edges,
    senders,
    receivers,
    edge_live,
    halo_rows,
    pool_fine,
    mid_edges,
    mid_senders,
    mid_receivers,
    pool_mid,
    coarse_edges,
    coarse_senders,
    coarse_receivers,
    w_edge_in,
    w_edge_out,
    w_node_in,
    w_node_out,
    cotangent,
):
    every = ("grp", "sub")
    feature = nodes.shape[1]
    fine_count = nodes.shape[0]
    halo_width = halo_rows.shape[1]
    owned_mids = pool_mid.shape[0]
    sub_count = lax.axis_size("sub")
    device_count = sub_count * lax.axis_size("grp")
    group_mids = owned_mids * sub_count
    coarse_count = coarse_edges.shape[0] // 6
    stacks = (w_edge_in, w_edge_out, w_node_in, w_node_out)
    fine_params, mid_params, coarse_params = (stacks, 0), (stacks, 1), (stacks, 2)
    up = [(i, i + 1) for i in range(device_count - 1)]
    down = [(i + 1, i) for i in range(device_count - 1)]

    pairs = [(i, i ^ 1) for i in range(lax.axis_size("grp"))]
    halo = nodes.at[halo_rows.reshape(-1)].get(mode="promise_in_bounds")
    from_prev = lax.ppermute(halo[:halo_width], every, up)
    from_next = lax.ppermute(halo[halo_width:], every, down)
    fine_table = jnp.concatenate([nodes, from_prev, from_next], axis=0)

    fine_new, fine_collected, fine_pre = layer_forward(
        fine_table, nodes, edges, senders, receivers, edge_live, fine_params, 4096, True
    )
    pooled = pool_fine_nodes(pool_fine, fine_new, cotangent, sub_count, owned_mids)
    owned = summed_in(pooled, "sub")
    lines = owned_mids // feature
    tail = owned[owned_mids : owned_mids + 2 * lines, :feature]
    owned_counts = (64.0 * tail[:lines] + tail[lines:]).reshape(owned_mids, 1)
    owned_counts = jnp.maximum(owned_counts, 1.0)
    mid_own = (owned[:owned_mids, :feature] / owned_counts).astype(BF16)
    grad_mid = owned[:owned_mids, feature:]
    mid_table = shared_out(mid_own, "sub", sub_count).reshape(group_mids, feature)
    mid_new, mid_collected, mid_pre = layer_forward(
        mid_table, mid_own, mid_edges, mid_senders, mid_receivers, edge_live, mid_params, 512, False
    )

    coarse_sent = pool_mid_nodes(pool_mid, mid_new, grad_mid, coarse_count)
    coarse_rows = coarse_count // device_count
    mine = summed_in(coarse_sent.reshape(device_count, coarse_rows, 3 * feature), every)
    my_scale = 1.0 / jnp.maximum(mine[:, 2 * feature :], 1.0)
    coarse_mine = jnp.concatenate(
        [mine[:, :feature] * my_scale, mine[:, feature : 2 * feature], my_scale], axis=1
    ).astype(BF16)
    coarse_all = shared_out(coarse_mine, every, device_count).reshape(coarse_count, 3 * feature)
    coarse_in, grad_coarse, coarse_scale = (coarse_all, 0), (coarse_all, 1), (coarse_all, 2)

    half_edges = coarse_edges.shape[0] // 2
    first = lax.rem(lax.axis_index("grp"), 2) * half_edges
    my_edges = lax.dynamic_slice_in_dim(coarse_edges, first, half_edges)
    my_senders = lax.dynamic_slice_in_dim(coarse_senders, first, half_edges)
    my_receivers = lax.dynamic_slice_in_dim(coarse_receivers, first, half_edges)
    coarse_part, coarse_pre = layer_forward(
        coarse_in, coarse_in, my_edges, my_senders, my_receivers, edge_live, coarse_params, 3072, False, True
    )
    coarse_other = lax.ppermute(coarse_part, "grp", pairs)
    coarse_back, coarse_grads, coarse_base, coarse_new = layer_backward(
        grad_coarse,
        coarse_in,
        coarse_in,
        coarse_part,
        my_edges,
        coarse_pre,
        my_senders,
        my_receivers,
        edge_live,
        coarse_params,
        3072,
        False,
        "split",
        other=coarse_other,
    )
    coarse_back_other = lax.ppermute(coarse_back, "grp", pairs)
    edge_rows = 4 * feature
    coarse_edge_grads = coarse_grads[:edge_rows]
    coarse_edge_grads = coarse_edge_grads + lax.ppermute(coarse_edge_grads, "grp", pairs)
    coarse_grads = jnp.concatenate([coarse_edge_grads, coarse_grads[edge_rows:]], axis=0)
    mid_out = lift(mid_new, coarse_new, pool_mid, BF16)
    lift_table = lax.all_gather(mid_out, "sub", axis=0, tiled=True)
    mid_own_grad, mid_grads, mid_table_grad = layer_backward(
        grad_mid,
        mid_table,
        mid_own,
        mid_collected,
        mid_edges,
        mid_pre,
        mid_senders,
        mid_receivers,
        edge_live,
        mid_params,
        512,
        False,
        "whole",
        pool_mid,
        (coarse_back, coarse_back_other, coarse_base, coarse_scale),
    )
    owned_total = mid_own_grad + summed_in(
        mid_table_grad.reshape(sub_count, owned_mids, feature), "sub"
    )
    owned_scaled = (owned_total / owned_counts).astype(BF16)
    grad_partial = shared_out(owned_scaled, "sub", sub_count).reshape(group_mids, feature)
    grad_nodes, fine_grads, halo_grad = layer_backward(
        cotangent,
        fine_table,
        nodes,
        fine_collected,
        edges,
        fine_pre,
        senders,
        receivers,
        edge_live,
        fine_params,
        4096,
        True,
        "rest",
        pool_fine,
        (grad_partial,),
    )
    to_prev = lax.ppermute(halo_grad[:halo_width], every, down)
    to_next = lax.ppermute(halo_grad[halo_width:], every, up)
    result = lift(fine_new, lift_table, pool_fine, BF16)
    grad_nodes = add_rows(
        grad_nodes, halo_rows, jnp.concatenate([to_prev, to_next], axis=0)
    )

    flat = jnp.concatenate([fine_grads.astype(BF16), mid_grads.astype(BF16)], axis=0)
    share = -(-flat.shape[0] // (16 * device_count)) * 16
    flat = jnp.pad(flat, ((0, share * device_count - flat.shape[0]), (0, 0)))
    my_sum = summed_in(flat.reshape(device_count, share, feature), every).astype(BF16)
    total = shared_out(my_sum, every, device_count).reshape(device_count * share, feature)
    total = total.astype(F32)
    grads, start, length = [], 0, fine_grads.shape[0]
    for stack in stacks:
        size = stack.shape[1]
        grads.append(
            jnp.stack(
                [
                    total[start : start + size],
                    total[length + start : length + start + size],
                    coarse_grads[start : start + size],
                ]
            )
        )
        start += size
    return (result, grad_nodes, grads[0], grads[1], grads[2], grads[3])


def solution(mesh):
    row, flat = P(("grp", "sub"), None), P(("grp", "sub"))
    in_specs = (row, row, flat, flat, flat, row, flat, row, flat, flat, flat) + (P(),) * 7 + (row,)
    out_specs = (row, row, P(), P(), P(), P())
    return jax.shard_map(shards, mesh=mesh, in_specs=in_specs, out_specs=out_specs, check_vma=False)
```

```python
import functools
import jax
import jax.numpy as jnp
from jax import lax
from jax.experimental import pallas as pl
from jax.experimental.pallas import tpu as pltpu
from jax.sharding import PartitionSpec as P

epsilon = 1e-05
F32 = jnp.float32
BF16 = jnp.bfloat16
LANES = 128
VMEM_LIMIT = 56 * 1024 * 1024


def dot(a, b):
    return jnp.dot(a, b, preferred_element_type=F32)


def dot_nt(a, b):
    return lax.dot_general(a, b, (((1,), (1,)), ((), ())), preferred_element_type=F32)


def dot_tn(a, b):
    return lax.dot_general(a, b, (((0,), (0,)), ((), ())), preferred_element_type=F32)


def as_columns(rows):
    count = rows.shape[0]
    return jnp.concatenate(
        [jnp.broadcast_to(rows[k : k + 1, :], (LANES, LANES)).T for k in range(count)], axis=0
    )


def parts_of(index):
    high = jnp.floor(index * (1.0 / LANES))
    return high.astype(BF16), (index - high * float(LANES)).astype(BF16)


def one_hot(columns, width):
    high, low = parts_of(columns)
    lane = lax.broadcasted_iota(jnp.int32, (1, LANES), 1).astype(F32).astype(BF16)
    one, zero = jnp.ones((), BF16), jnp.zeros((), BF16)
    base = jnp.where(low == lane, one, zero)
    return jnp.concatenate(
        [jnp.where(high == jnp.asarray(j, BF16), base, zero) for j in range(width // LANES)], axis=1
    )


def one_hot_t(rows, height):
    high, low = parts_of(rows)
    place = lax.broadcasted_iota(jnp.int32, (LANES, LANES), 0).astype(F32).astype(BF16)
    one, zero = jnp.ones((), BF16), jnp.zeros((), BF16)
    pieces = []
    for k in range(rows.shape[0]):
        base = jnp.where(place == low[k : k + 1, :], one, zero)
        pieces.append(
            jnp.concatenate(
                [
                    jnp.where(high[k : k + 1, :] == jnp.asarray(j, BF16), base, zero)
                    for j in range(height // LANES)
                ],
                axis=0,
            )
        )
    return jnp.concatenate(pieces, axis=1)


def gather(columns, table2):
    half = table2.shape[0]
    upper = columns >= float(half)
    local = jnp.where(upper, columns - float(half), columns)
    both = dot(one_hot(local, half), table2)
    return jnp.where(upper, both[:, LANES:], both[:, :LANES])


def spread(rows, columns, values, half):
    local = jnp.where(rows >= float(half), rows - float(half), rows)
    upper = columns >= float(half)
    values = values.astype(F32)
    both = jnp.concatenate(
        [jnp.where(upper, 0.0, values).astype(BF16), jnp.where(upper, values, 0.0).astype(BF16)],
        axis=1,
    )
    return dot(one_hot_t(local, half), both)


def widened(weight_out):
    row_mean = jnp.broadcast_to(
        jnp.mean(weight_out.astype(F32), axis=1, keepdims=True), weight_out.shape
    )
    high = row_mean.astype(BF16)
    low = (row_mean - high.astype(F32)).astype(BF16)
    top = jnp.concatenate([weight_out, high], axis=1)
    return jnp.concatenate(
        [top, jnp.concatenate([jnp.zeros_like(weight_out), low], axis=1)], axis=0
    )


def lane_mean(values):
    return jnp.mean(values, axis=-1, keepdims=True)


def mlp_rest(preact, wide_out):
    sigmoid_pre = jax.nn.sigmoid(preact)
    hidden = (preact * sigmoid_pre).astype(BF16)
    both = dot(jnp.concatenate([hidden, hidden], axis=1), wide_out)
    centred = both[:, :LANES] - both[:, LANES:]
    inv_std = lax.rsqrt(lane_mean(centred * centred) + epsilon)
    return sigmoid_pre, hidden, centred * inv_std, inv_std


def fill_halves(target, source, half):
    target[:, :LANES] = source[:half, :]
    target[:, LANES:] = source[half:, :]


def forward_kernel(
    block, masked, split, live, send, recv, edges, table, own, edge_in, edge_out, node_in, node_out,
    *rest,
):
    if split:
        part, preact, table2, own2, wide, total = rest
    else:
        new, collected, preact, table2, own2, wide, total = rest
    step = pl.program_id(0)
    table_half, own_half = table2.shape[0], own2.shape[0]

    @pl.when(step == 0)
    def _():
        fill_halves(table2, table, table_half)
        fill_halves(own2, own, own_half)
        wide[...] = widened(edge_out[...])
        total[...] = jnp.zeros_like(total)

    send_rows = send[...].reshape(block // LANES, LANES).astype(F32)
    recv_rows = recv[...].reshape(block // LANES, LANES).astype(F32)
    recv_columns = as_columns(recv_rows)
    from_send = gather(as_columns(send_rows), table2[...]).astype(BF16)
    from_recv = gather(recv_columns, own2[...]).astype(BF16)
    feat = edges[...]
    pre = dot(jnp.concatenate([from_send, from_recv], axis=1), edge_in[: 2 * LANES, :])
    pre = pre + dot(feat, edge_in[2 * LANES :, :])
    preact[...] = pre
    _, _, normed, _ = mlp_rest(pre, wide[...])
    updated = feat.astype(F32) + normed
    if masked:
        slot = step * block + lax.broadcasted_iota(jnp.int32, (block, LANES), 0)
        updated = jnp.where(slot < live[0], updated, 0.0)
    total[...] += spread(recv_rows, recv_columns, updated, own_half)

    @pl.when(step == pl.num_programs(0) - 1)
    def _():
        if split:
            part[:own_half, :] = total[:, :LANES]
            part[own_half:, :] = total[:, LANES:]
            return
        wide_node = widened(node_out[...])
        rows = min(own_half, 512)
        for start in range(0, 2 * own_half, rows):
            place = pl.ds(start, rows)
            if start < own_half:
                gathered = total[start : start + rows, :LANES].astype(BF16)
            else:
                gathered = total[start - own_half : start - own_half + rows, LANES:].astype(BF16)
            collected[place, :] = gathered
            mine = own[place, :]
            pre_node = dot(jnp.concatenate([mine, gathered], axis=1), node_in[...])
            _, _, node_normed, _ = mlp_rest(pre_node, wide_node)
            new[place, :] = mine.astype(F32) + node_normed


def whole(array):
    rank = array.ndim
    return pl.BlockSpec(array.shape, lambda step: (0,) * rank)


def level_specs(params):
    stacks, level = params
    return [
        pl.BlockSpec((None,) + stack.shape[1:], lambda step: (level, 0, 0)) for stack in stacks
    ]


def column_block(source):
    array, column = source if isinstance(source, tuple) else (source, 0)
    return array, pl.BlockSpec((array.shape[0], LANES), lambda step: (0, column))


def layer_forward(table, own, edges, send, recv, live, params, block, masked, split=False):
    count, feature = edges.shape
    (table, table_spec), (own, own_spec) = column_block(table), column_block(own)
    steps = count // block
    send3 = send.reshape(steps, block // LANES, LANES)
    recv3 = recv.reshape(steps, block // LANES, LANES)
    ids = pl.BlockSpec((1, block // LANES, LANES), lambda step: (step, 0, 0))
    edge_spec = pl.BlockSpec((block, feature), lambda step: (step, 0))
    nodes, rows = own.shape[0], table.shape[0]
    full = lambda n: pl.BlockSpec((n, feature), lambda step: (0, 0))
    return pl.pallas_call(
        functools.partial(forward_kernel, block, masked, split),
        grid=(steps,),
        in_specs=[pl.BlockSpec(memory_space=pltpu.SMEM), ids, ids, edge_spec, table_spec, own_spec]
        + level_specs(params),
        out_specs=[full(nodes)] * (1 if split else 2) + [edge_spec],
        out_shape=[jax.ShapeDtypeStruct((nodes, feature), F32)]
        + ([] if split else [jax.ShapeDtypeStruct((nodes, feature), BF16)])
        + [jax.ShapeDtypeStruct((count, feature), F32)],
        scratch_shapes=[
            pltpu.VMEM((rows // 2, 2 * feature), BF16),
            pltpu.VMEM((nodes // 2, 2 * feature), BF16),
            pltpu.VMEM((2 * feature, 2 * feature), BF16),
            pltpu.VMEM((nodes // 2, 2 * feature), F32),
        ],
        compiler_params=pltpu.CompilerParams(vmem_limit_bytes=VMEM_LIMIT),
        cost_estimate=pl.CostEstimate(
            flops=2 * count * feature * (rows + 2 * nodes + 1024),
            bytes_accessed=count * feature * 8,
            transcendentals=count * feature,
        ),
    )(live, send3, recv3, edges, table, own, *params[0])


def backward_kernel(
    block, masked, lifted, table_out, live, send, recv, edges, preact, upstream, table, own,
    collected, edge_in, edge_out, node_in, node_out,
    *rest,
):
    split = table_out == "split"
    if lifted:
        lift_ids, lift_tables = rest[0], rest[1 : 1 + lifted]
        lift2 = rest[-1]
        rest = rest[1 + lifted : -1]
    grad_own, grads_out = rest[:2]
    grad_table = rest[2] if table_out else None
    new = rest[3] if split else None
    wide, grad2, send_total, recv_total, grads = rest[-5:]
    grad_edge_in = grads.at[pl.ds(0, 3 * LANES), :]
    grad_edge_out = grads.at[pl.ds(3 * LANES, LANES), :]
    grad_node_in = grads.at[pl.ds(4 * LANES, 2 * LANES), :]
    grad_node_out = grads.at[pl.ds(6 * LANES, LANES), :]
    step = pl.program_id(0)
    table_half, own_half = send_total.shape[0], recv_total.shape[0]

    @pl.when(step == 0)
    def _():
        wide[...] = widened(edge_out[...])
        send_total[...] = jnp.zeros_like(send_total)
        recv_total[...] = jnp.zeros_like(recv_total)
        grad_edge_in[...] = jnp.zeros_like(grad_edge_in)
        grad_edge_out[...] = jnp.zeros_like(grad_edge_out)
        wide_node = widened(node_out[...])
        into, out_of = node_in[...], node_out[...]
        total_in = jnp.zeros((2 * LANES, LANES), F32)
        total_out = jnp.zeros((LANES, LANES), F32)
        if lifted:
            height = lift2.shape[0]
            for side in range(2):
                lines = pl.ds(side * height, height)
                term = lift_tables[0][lines, :]
                if lifted > 1:
                    for more in lift_tables[1:-1]:
                        term = term + more[lines, :]
                    term = term * lift_tables[-1][lines, :].astype(F32)
                lift2[:, side * LANES : (side + 1) * LANES] = term.astype(BF16)
            ids = lift_ids[...].astype(F32)
        rows = min(own_half, 512)
        for start in range(0, 2 * own_half, rows):
            place = pl.ds(start, rows)
            inputs = jnp.concatenate([own[place, :], collected[place, :]], axis=1)
            pre = dot(inputs, into)
            sigmoid_pre, hidden, normed, inv_std = mlp_rest(pre, wide_node)
            up = upstream[place, :].astype(F32)
            if lifted:
                places = as_columns(ids[start // LANES : (start + rows) // LANES, :])
                up = up + gather(places, lift2[...])
            centred_grad = (
                up
                - jnp.mean(up, axis=-1, keepdims=True)
                - normed * jnp.mean(up * normed, axis=-1, keepdims=True)
            )
            grad_output = (inv_std * centred_grad).astype(BF16)
            total_out = total_out + dot_tn(hidden, grad_output)
            grad_hidden = dot_nt(grad_output, out_of)
            grad_pre = (
                grad_hidden * sigmoid_pre * (1.0 + pre * (1.0 - sigmoid_pre))
            ).astype(BF16)
            total_in = total_in + dot_tn(inputs, grad_pre)
            back = dot_nt(grad_pre, into)
            if split:
                new[place, :] = own[place, :].astype(F32) + normed
                grad_table[place, :] = up + back[:, :LANES]
                grad_own[place, :] = jnp.zeros((rows, LANES), F32)
            else:
                grad_own[place, :] = up + back[:, :LANES]
            grad_collected = back[:, LANES:]
            grad_collected = grad_collected - jnp.mean(grad_collected, axis=-1, keepdims=True)
            if start < own_half:
                grad2[start : start + rows, :LANES] = grad_collected.astype(BF16)
            else:
                grad2[start - own_half : start - own_half + rows, LANES:] = grad_collected.astype(
                    BF16
                )
        grad_node_in[...] = total_in
        grad_node_out[...] = total_out

    send_rows = send[...].reshape(block // LANES, LANES).astype(F32)
    recv_rows = recv[...].reshape(block // LANES, LANES).astype(F32)
    send_columns = as_columns(send_rows)
    recv_columns = as_columns(recv_rows)
    grad_updated = gather(recv_columns, grad2[...])
    if masked:
        slot = step * block + lax.broadcasted_iota(jnp.int32, (block, LANES), 0)
        grad_updated = jnp.where(slot < live[0], grad_updated, 0.0)
    pre = preact[...]
    sigmoid_pre, hidden, normed, inv_std = mlp_rest(pre, wide[...])
    centred_grad = grad_updated - normed * lane_mean(grad_updated * normed)
    grad_output = (inv_std * centred_grad).astype(BF16)
    grad_edge_out[...] += dot_tn(hidden, grad_output)
    grad_hidden = dot_nt(grad_output, edge_out[...])
    edge_grad = (grad_hidden * sigmoid_pre * (1.0 + pre * (1.0 - sigmoid_pre))).astype(BF16)
    grad_edge_in[2 * LANES :, :] += dot_tn(edges[...], edge_grad)
    send_total[...] += spread(send_rows, send_columns, edge_grad, table_half)
    recv_total[...] += spread(recv_rows, recv_columns, edge_grad, own_half)

    @pl.when(step == pl.num_programs(0) - 1)
    def _():
        from_send = edge_in[:LANES, :]
        from_recv = edge_in[LANES : 2 * LANES, :]
        nodes = 2 * own_half

        def part(total, half, start, rows):
            if start < half:
                return total[start : start + rows, :LANES].astype(BF16)
            return total[start - half : start - half + rows, LANES:].astype(BF16)

        weight_recv = jnp.zeros((LANES, LANES), F32)
        rows = min(own_half, 512)
        for start in range(0, nodes, rows):
            place = pl.ds(start, rows)
            recv_sum = part(recv_total, own_half, start, rows)
            weight_recv = weight_recv + dot_tn(own[place, :], recv_sum)
            grad_own[place, :] += dot_nt(recv_sum, from_recv)
        grad_edge_in[LANES : 2 * LANES, :] = weight_recv

        weight_send = jnp.zeros((LANES, LANES), F32)
        cuts = sorted({0, table_half, nodes, 2 * table_half} if nodes > table_half else {0, table_half, 2 * table_half})
        pieces = []
        for first, last in zip(cuts[:-1], cuts[1:]):
            pieces += [(k, min(1152, last - k)) for k in range(first, last, 1152)]
        for start, rows in pieces:
            place = pl.ds(start, rows)
            split_sum = part(send_total, table_half, start, rows)
            weight_send = weight_send + dot_tn(table[place, :], split_sum)
            back = dot_nt(split_sum, from_send)
            if table_out == "whole":
                grad_table[place, :] = back.astype(BF16)
            elif start < nodes:
                grad_own[place, :] += back
            else:
                grad_table[pl.ds(start - nodes, rows), :] = back.astype(BF16)
        grad_edge_in[:LANES, :] = weight_send
        grads_out[...] = grads[...].astype(grads_out.dtype)


def layer_backward(
    upstream, table, own, collected, edges, preact, send, recv, live, params, block, masked,
    table_out, lift_ids=None, lift_tables=(),
):
    lifted = len(lift_tables)
    (table, table_spec), (own, own_spec) = column_block(table), column_block(own)
    upstream, upstream_spec = column_block(upstream)
    count, feature = edges.shape
    steps = count // block
    send3 = send.reshape(steps, block // LANES, LANES)
    recv3 = recv.reshape(steps, block // LANES, LANES)
    ids = pl.BlockSpec((1, block // LANES, LANES), lambda step: (step, 0, 0))
    edge_spec = pl.BlockSpec((block, feature), lambda step: (step, 0))
    nodes, rows = own.shape[0], table.shape[0]
    full = lambda n: pl.BlockSpec((n, feature), lambda step: (0, 0))
    out = [(nodes, F32), (7 * feature, F32 if table_out == "split" else BF16)]
    if table_out == "whole":
        out.append((rows, BF16))
    elif table_out == "rest":
        out.append((rows - nodes, BF16))
    elif table_out == "split":
        out += [(nodes, F32), (nodes, F32)]
    extra, extra_specs, extra_scratch = [], [], []
    if lifted:
        lift_ids = lift_ids.reshape(nodes // LANES, LANES)
        extra.append(lift_ids)
        extra_specs.append(whole(lift_ids))
        for source in lift_tables:
            array, spec = column_block(source)
            extra.append(array)
            extra_specs.append(spec)
        extra_scratch = [pltpu.VMEM((array.shape[0] // 2, 2 * feature), BF16)]
    return pl.pallas_call(
        functools.partial(backward_kernel, block, masked, lifted, table_out),
        grid=(steps,),
        in_specs=[
            pl.BlockSpec(memory_space=pltpu.SMEM),
            ids,
            ids,
            edge_spec,
            edge_spec,
            upstream_spec,
            table_spec,
            own_spec,
            full(nodes),
        ]
        + level_specs(params)
        + extra_specs,
        out_specs=[full(n) for n, _ in out],
        out_shape=[jax.ShapeDtypeStruct((n, feature), kind) for n, kind in out],
        scratch_shapes=[
            pltpu.VMEM((2 * feature, 2 * feature), BF16),
            pltpu.VMEM((nodes // 2, 2 * feature), BF16),
            pltpu.VMEM((rows // 2, 2 * feature), F32),
            pltpu.VMEM((nodes // 2, 2 * feature), F32),
            pltpu.VMEM((7 * feature, feature), F32),
        ]
        + extra_scratch,
        compiler_params=pltpu.CompilerParams(vmem_limit_bytes=VMEM_LIMIT),
        cost_estimate=pl.CostEstimate(
            flops=2 * count * feature * (rows + 2 * nodes + 1024),
            bytes_accessed=count * feature * 8,
            transcendentals=count * feature,
        ),
    )(live, send3, recv3, edges, preact, upstream, table, own, collected, *params[0], *extra)


def pool_kernel(owned, ids, left, right, out, counts):
    step = pl.program_id(0)
    group = out.shape[0]
    rows = ids[...].astype(F32)

    @pl.when(step == 0)
    def _():
        high_rows = jnp.floor(rows * (1.0 / LANES))
        low_rows = rows - high_rows * float(LANES)
        counts[...] = dot_nt(one_hot_t(high_rows, LANES), one_hot_t(low_rows, LANES))

    span = group * owned
    local = rows - (step * span).astype(F32)
    local = jnp.where((local >= 0.0) & (local < float(span)), local, float(span))
    both = jnp.concatenate([left[...].astype(BF16), right[...].astype(BF16)], axis=1)
    sums = dot(one_hot_t(local, span), both).astype(BF16)
    lines = owned // LANES
    for k in range(group):
        out[k, :owned, :] = sums[k * owned : (k + 1) * owned, :]
        hits = counts[pl.ds((step * group + k) * lines, lines), :]
        high = jnp.floor(hits * (1.0 / 64.0))
        tail = jnp.concatenate(
            [high, hits - high * 64.0, jnp.zeros((16 - 2 * lines, LANES), F32)], axis=0
        )
        out[k, owned:, :] = jnp.concatenate([tail, jnp.zeros_like(tail)], axis=1).astype(BF16)


def pool_fine_nodes(ids, left, right, parts, owned):
    count, feature = left.shape
    group = 4
    rows = owned + 16
    full = pl.BlockSpec((count, feature), lambda step: (0, 0))
    return pl.pallas_call(
        functools.partial(pool_kernel, owned),
        grid=(parts // group,),
        in_specs=[pl.BlockSpec((count // LANES, LANES), lambda step: (0, 0)), full, full],
        out_specs=pl.BlockSpec((group, rows, 2 * feature), lambda step: (step, 0, 0)),
        out_shape=jax.ShapeDtypeStruct((parts, rows, 2 * feature), BF16),
        scratch_shapes=[pltpu.VMEM((LANES, LANES), F32)],
        compiler_params=pltpu.CompilerParams(vmem_limit_bytes=VMEM_LIMIT),
        cost_estimate=pl.CostEstimate(
            flops=4 * count * parts * owned * feature,
            bytes_accessed=4 * count * feature,
            transcendentals=0,
        ),
    )(ids.reshape(count // LANES, LANES), left, right)


def pool_mid_kernel(ids, left, right, out):
    rows = ids[...].astype(F32)
    both = jnp.concatenate(
        [left[...].astype(BF16), right[...].astype(BF16), jnp.ones(left.shape, BF16)], axis=1
    )
    out[...] = dot(one_hot_t(rows, out.shape[0]), both).astype(BF16)


def pool_mid_nodes(ids, left, right, targets):
    count, feature = left.shape
    return pl.pallas_call(
        pool_mid_kernel,
        out_shape=jax.ShapeDtypeStruct((targets, 3 * feature), BF16),
        compiler_params=pltpu.CompilerParams(vmem_limit_bytes=VMEM_LIMIT),
        cost_estimate=pl.CostEstimate(
            flops=6 * count * targets * feature, bytes_accessed=6 * targets * feature, transcendentals=0
        ),
    )(ids.reshape(count // LANES, LANES), left, right)


def lift_kernel(ids, base, table, out, table2):
    @pl.when(pl.program_id(0) == 0)
    def _():
        half = table2.shape[0]
        table2[:, :LANES] = table[:half, :].astype(BF16)
        table2[:, LANES:] = table[half:, :].astype(BF16)

    rows = ids[...].reshape(ids.shape[1], LANES).astype(F32)
    out[...] = (base[...].astype(F32) + gather(as_columns(rows), table2[...])).astype(out.dtype)


def lift(base, table, ids, kind):
    count, feature = base.shape
    rows = table.shape[0]
    block = min(count, 512)
    steps = count // block
    return pl.pallas_call(
        lift_kernel,
        grid=(steps,),
        in_specs=[
            pl.BlockSpec((1, block // LANES, LANES), lambda step: (step, 0, 0)),
            pl.BlockSpec((block, feature), lambda step: (step, 0)),
            pl.BlockSpec((rows, feature), lambda step: (0, 0)),
        ],
        out_specs=pl.BlockSpec((block, feature), lambda step: (step, 0)),
        out_shape=jax.ShapeDtypeStruct((count, feature), kind),
        scratch_shapes=[pltpu.VMEM((rows // 2, 2 * feature), BF16)],
        compiler_params=pltpu.CompilerParams(vmem_limit_bytes=VMEM_LIMIT),
        cost_estimate=pl.CostEstimate(
            flops=2 * count * rows * feature, bytes_accessed=8 * count * feature, transcendentals=0
        ),
    )(ids.reshape(steps, block // LANES, LANES), base, table)


def add_rows_kernel(ids, base, values, out):
    rows = ids[...].astype(F32)
    out[...] = base[...] + dot(one_hot_t(rows, out.shape[0]), values[...])


def add_rows(base, ids, values):
    return pl.pallas_call(
        add_rows_kernel,
        out_shape=jax.ShapeDtypeStruct(base.shape, base.dtype),
        compiler_params=pltpu.CompilerParams(vmem_limit_bytes=VMEM_LIMIT),
        cost_estimate=pl.CostEstimate(
            flops=2 * base.shape[0] * values.shape[0] * LANES, bytes_accessed=base.size * 8, transcendentals=0
        ),
    )(ids.reshape(-1, LANES), base, values)


def unpack_kernel(total, coarse, coarse_other, *outs):
    length, shared = coarse.shape[0], coarse_other.shape[0]
    start = 0
    for out in outs:
        size = out.shape[1]
        out[0] = total[start : start + size, :].astype(F32)
        out[1] = total[length + start : length + start + size, :].astype(F32)
        last = coarse[start : start + size, :]
        if start + size <= shared:
            last = last + coarse_other[start : start + size, :]
        out[2] = last
        start += size


def unpack(total, coarse, coarse_other, stacks):
    return pl.pallas_call(
        unpack_kernel,
        out_shape=[jax.ShapeDtypeStruct(stack.shape, F32) for stack in stacks],
        compiler_params=pltpu.CompilerParams(vmem_limit_bytes=VMEM_LIMIT),
        cost_estimate=pl.CostEstimate(
            flops=0, bytes_accessed=8 * total.size, transcendentals=0
        ),
    )(total, coarse, coarse_other)


def shared_out(block, axes, count):
    sent = jnp.broadcast_to(block[None], (count,) + block.shape)
    return lax.all_to_all(sent, axes, split_axis=0, concat_axis=0, tiled=True)


def summed_in(blocks, axes):
    got = lax.all_to_all(blocks, axes, split_axis=0, concat_axis=0, tiled=True)
    return jnp.sum(got.astype(F32), axis=0)


def shards(
    nodes,
    edges,
    senders,
    receivers,
    edge_live,
    halo_rows,
    pool_fine,
    mid_edges,
    mid_senders,
    mid_receivers,
    pool_mid,
    coarse_edges,
    coarse_senders,
    coarse_receivers,
    w_edge_in,
    w_edge_out,
    w_node_in,
    w_node_out,
    cotangent,
):
    every = ("grp", "sub")
    feature = nodes.shape[1]
    fine_count = nodes.shape[0]
    halo_width = halo_rows.shape[1]
    owned_mids = pool_mid.shape[0]
    sub_count = lax.axis_size("sub")
    device_count = sub_count * lax.axis_size("grp")
    group_mids = owned_mids * sub_count
    coarse_count = coarse_edges.shape[0] // 6
    stacks = (w_edge_in, w_edge_out, w_node_in, w_node_out)
    fine_params, mid_params, coarse_params = (stacks, 0), (stacks, 1), (stacks, 2)
    up = [(i, i + 1) for i in range(device_count - 1)]
    down = [(i + 1, i) for i in range(device_count - 1)]

    pairs = [(i, i ^ 1) for i in range(lax.axis_size("grp"))]
    halo = nodes.at[halo_rows.reshape(-1)].get(mode="promise_in_bounds")
    from_prev = lax.ppermute(halo[:halo_width], every, up)
    from_next = lax.ppermute(halo[halo_width:], every, down)
    fine_table = jnp.concatenate([nodes, from_prev, from_next], axis=0)

    fine_new, fine_collected, fine_pre = layer_forward(
        fine_table, nodes, edges, senders, receivers, edge_live, fine_params, 4096, True
    )
    pooled = pool_fine_nodes(pool_fine, fine_new, cotangent, sub_count, owned_mids)
    owned = summed_in(pooled, "sub")
    lines = owned_mids // feature
    tail = owned[owned_mids : owned_mids + 2 * lines, :feature]
    owned_counts = (64.0 * tail[:lines] + tail[lines:]).reshape(owned_mids, 1)
    owned_counts = jnp.maximum(owned_counts, 1.0)
    mid_own = (owned[:owned_mids, :feature] / owned_counts).astype(BF16)
    grad_mid = owned[:owned_mids, feature:]
    mid_table = shared_out(mid_own, "sub", sub_count).reshape(group_mids, feature)
    mid_new, mid_collected, mid_pre = layer_forward(
        mid_table, mid_own, mid_edges, mid_senders, mid_receivers, edge_live, mid_params, 1536, False
    )

    coarse_sent = pool_mid_nodes(pool_mid, mid_new, grad_mid, coarse_count)
    coarse_rows = coarse_count // device_count
    mine = summed_in(coarse_sent.reshape(device_count, coarse_rows, 3 * feature), every)
    my_scale = 1.0 / jnp.maximum(mine[:, 2 * feature :], 1.0)
    coarse_mine = jnp.concatenate(
        [mine[:, :feature] * my_scale, mine[:, feature : 2 * feature], my_scale], axis=1
    ).astype(BF16)
    coarse_all = shared_out(coarse_mine, every, device_count).reshape(coarse_count, 3 * feature)
    coarse_in, grad_coarse, coarse_scale = (coarse_all, 0), (coarse_all, 1), (coarse_all, 2)

    half_edges = coarse_edges.shape[0] // 2
    first = lax.rem(lax.axis_index("grp"), 2) * half_edges
    my_edges = lax.dynamic_slice_in_dim(coarse_edges, first, half_edges)
    my_senders = lax.dynamic_slice_in_dim(coarse_senders, first, half_edges)
    my_receivers = lax.dynamic_slice_in_dim(coarse_receivers, first, half_edges)
    coarse_part, coarse_pre = layer_forward(
        coarse_in, coarse_in, my_edges, my_senders, my_receivers, edge_live, coarse_params, 3072, False, True
    )
    coarse_half = coarse_part.astype(BF16)
    coarse_other = lax.ppermute(coarse_half, "grp", pairs)
    coarse_collected = (coarse_half.astype(F32) + coarse_other.astype(F32)).astype(BF16)
    coarse_back, coarse_grads, coarse_base, coarse_new = layer_backward(
        grad_coarse,
        coarse_in,
        coarse_in,
        coarse_collected,
        my_edges,
        coarse_pre,
        my_senders,
        my_receivers,
        edge_live,
        coarse_params,
        3072,
        False,
        "split",
    )
    coarse_back_other = lax.ppermute(coarse_back, "grp", pairs)
    edge_rows = 4 * feature
    coarse_grads_other = lax.ppermute(coarse_grads[:edge_rows], "grp", pairs)
    mid_out = lift(mid_new, coarse_new, pool_mid, BF16)
    lift_table = lax.all_gather(mid_out, "sub", axis=0, tiled=True)
    mid_own_grad, mid_grads, mid_table_grad = layer_backward(
        grad_mid,
        mid_table,
        mid_own,
        mid_collected,
        mid_edges,
        mid_pre,
        mid_senders,
        mid_receivers,
        edge_live,
        mid_params,
        1536,
        False,
        "whole",
        pool_mid,
        (coarse_back, coarse_back_other, coarse_base, coarse_scale),
    )
    owned_total = mid_own_grad + summed_in(
        mid_table_grad.reshape(sub_count, owned_mids, feature), "sub"
    )
    owned_scaled = (owned_total / owned_counts).astype(BF16)
    grad_partial = shared_out(owned_scaled, "sub", sub_count).reshape(group_mids, feature)
    grad_nodes, fine_grads, halo_grad = layer_backward(
        cotangent,
        fine_table,
        nodes,
        fine_collected,
        edges,
        fine_pre,
        senders,
        receivers,
        edge_live,
        fine_params,
        4096,
        True,
        "rest",
        pool_fine,
        (grad_partial,),
    )
    to_prev = lax.ppermute(halo_grad[:halo_width], every, down)
    to_next = lax.ppermute(halo_grad[halo_width:], every, up)
    result = lift(fine_new, lift_table, pool_fine, BF16)
    flat = jnp.concatenate([fine_grads, mid_grads], axis=0)
    share = -(-flat.shape[0] // (16 * device_count)) * 16
    flat = jnp.pad(flat, ((0, share * device_count - flat.shape[0]), (0, 0)))
    my_sum = summed_in(flat.reshape(device_count, share, feature), every).astype(BF16)
    my_sum, result, to_prev, to_next = lax.optimization_barrier((my_sum, result, to_prev, to_next))
    total = shared_out(my_sum, every, device_count).reshape(device_count * share, feature)
    grad_nodes = add_rows(
        grad_nodes, halo_rows, jnp.concatenate([to_prev, to_next], axis=0)
    )
    grads = unpack(total, coarse_grads, coarse_grads_other, stacks)
    return (result, grad_nodes, grads[0], grads[1], grads[2], grads[3])


def solution(mesh):
    row, flat = P(("grp", "sub"), None), P(("grp", "sub"))
    in_specs = (row, row, flat, flat, flat, row, flat, row, flat, flat, flat) + (P(),) * 7 + (row,)
    out_specs = (row, row, P(), P(), P(), P())
    return jax.shard_map(shards, mesh=mesh, in_specs=in_specs, out_specs=out_specs, check_vma=False)
```

```python
import functools
import jax
import jax.numpy as jnp
from jax import lax
from jax.experimental import pallas as pl
from jax.experimental.pallas import tpu as pltpu
from jax.sharding import PartitionSpec as P

epsilon = 1e-05
F32 = jnp.float32
BF16 = jnp.bfloat16
LANES = 128
VMEM_LIMIT = 56 * 1024 * 1024


def dot(a, b):
    return jnp.dot(a, b, preferred_element_type=F32)


def dot_nt(a, b):
    return lax.dot_general(a, b, (((1,), (1,)), ((), ())), preferred_element_type=F32)


def dot_tn(a, b):
    return lax.dot_general(a, b, (((0,), (0,)), ((), ())), preferred_element_type=F32)


def as_columns(rows):
    count = rows.shape[0]
    return jnp.concatenate(
        [jnp.broadcast_to(rows[k : k + 1, :], (LANES, LANES)).T for k in range(count)], axis=0
    )


def parts_of(index):
    high = jnp.floor(index * (1.0 / LANES))
    return high.astype(BF16), (index - high * float(LANES)).astype(BF16)


def one_hot(columns, width):
    high, low = parts_of(columns)
    lane = lax.broadcasted_iota(jnp.int32, (1, LANES), 1).astype(F32).astype(BF16)
    one, zero = jnp.ones((), BF16), jnp.zeros((), BF16)
    base = jnp.where(low == lane, one, zero)
    return jnp.concatenate(
        [jnp.where(high == jnp.asarray(j, BF16), base, zero) for j in range(width // LANES)], axis=1
    )


def one_hot_t(rows, height):
    high, low = parts_of(rows)
    place = lax.broadcasted_iota(jnp.int32, (LANES, LANES), 0).astype(F32).astype(BF16)
    one, zero = jnp.ones((), BF16), jnp.zeros((), BF16)
    pieces = []
    for k in range(rows.shape[0]):
        base = jnp.where(place == low[k : k + 1, :], one, zero)
        pieces.append(
            jnp.concatenate(
                [
                    jnp.where(high[k : k + 1, :] == jnp.asarray(j, BF16), base, zero)
                    for j in range(height // LANES)
                ],
                axis=0,
            )
        )
    return jnp.concatenate(pieces, axis=1)


def gather(columns, table2):
    half = table2.shape[0]
    upper = columns >= float(half)
    local = jnp.where(upper, columns - float(half), columns)
    both = dot(one_hot(local, half), table2)
    return jnp.where(upper, both[:, LANES:], both[:, :LANES])


def spread(rows, columns, values, half):
    local = jnp.where(rows >= float(half), rows - float(half), rows)
    upper = columns >= float(half)
    values = values.astype(F32)
    both = jnp.concatenate(
        [jnp.where(upper, 0.0, values).astype(BF16), jnp.where(upper, values, 0.0).astype(BF16)],
        axis=1,
    )
    return dot(one_hot_t(local, half), both)


def widened(weight_out):
    row_mean = jnp.broadcast_to(
        jnp.mean(weight_out.astype(F32), axis=1, keepdims=True), weight_out.shape
    )
    high = row_mean.astype(BF16)
    low = (row_mean - high.astype(F32)).astype(BF16)
    top = jnp.concatenate([weight_out, high], axis=1)
    return jnp.concatenate(
        [top, jnp.concatenate([jnp.zeros_like(weight_out), low], axis=1)], axis=0
    )


def lane_mean(values):
    return jnp.mean(values, axis=-1, keepdims=True)


def mlp_rest(preact, wide_out):
    sigmoid_pre = jax.nn.sigmoid(preact)
    hidden = (preact * sigmoid_pre).astype(BF16)
    both = dot(jnp.concatenate([hidden, hidden], axis=1), wide_out)
    centred = both[:, :LANES] - both[:, LANES:]
    inv_std = lax.rsqrt(lane_mean(centred * centred) + epsilon)
    return sigmoid_pre, hidden, centred * inv_std, inv_std


def rows_of(tables, start, rows):
    parts, at = [], 0
    for ref in tables:
        size = ref.shape[0]
        first, last = max(start, at), min(start + rows, at + size)
        if first < last:
            parts.append(ref[first - at : last - at, :])
        at += size
    return parts[0] if len(parts) == 1 else jnp.concatenate(parts, axis=0)


def fill_halves(target, tables, weight):
    half = target.shape[0]
    for side in range(2):
        block = rows_of(tables, side * half, half)
        if weight is not None:
            block = dot(block, weight).astype(BF16)
        target[:, side * LANES : (side + 1) * LANES] = block


def forward_kernel(
    block, masked, split, early, count, live, send, recv, edges, *rest,
):
    tables, (own, edge_in, edge_out, node_in, node_out) = rest[:count], rest[count : count + 5]
    rest = rest[count + 5 :]
    if split:
        part, preact, table2, own2, wide, total = rest
    else:
        new, collected, preact, table2, own2, wide, total = rest
    step = pl.program_id(0)
    own_half = own2.shape[0]

    @pl.when(step == 0)
    def _():
        fill_halves(table2, tables, edge_in[:LANES, :] if early else None)
        fill_halves(own2, [own], edge_in[LANES : 2 * LANES, :] if early else None)
        wide[...] = widened(edge_out[...])
        total[...] = jnp.zeros_like(total)

    send_rows = send[...].reshape(block // LANES, LANES).astype(F32)
    recv_rows = recv[...].reshape(block // LANES, LANES).astype(F32)
    recv_columns = as_columns(recv_rows)
    from_send = gather(as_columns(send_rows), table2[...])
    from_recv = gather(recv_columns, own2[...])
    feat = edges[...]
    if early:
        pre = from_send + from_recv
    else:
        both = jnp.concatenate([from_send.astype(BF16), from_recv.astype(BF16)], axis=1)
        pre = dot(both, edge_in[: 2 * LANES, :])
    pre = pre + dot(feat, edge_in[2 * LANES :, :])
    preact[...] = pre
    _, _, normed, _ = mlp_rest(pre, wide[...])
    updated = feat.astype(F32) + normed
    if masked:
        slot = step * block + lax.broadcasted_iota(jnp.int32, (block, LANES), 0)
        updated = jnp.where(slot < live[0], updated, 0.0)
    total[...] += spread(recv_rows, recv_columns, updated, own_half)

    @pl.when(step == pl.num_programs(0) - 1)
    def _():
        if split:
            part[:own_half, :] = total[:, :LANES]
            part[own_half:, :] = total[:, LANES:]
            return
        wide_node = widened(node_out[...])
        rows = min(own_half, 512)
        for start in range(0, 2 * own_half, rows):
            place = pl.ds(start, rows)
            if start < own_half:
                gathered = total[start : start + rows, :LANES].astype(BF16)
            else:
                gathered = total[start - own_half : start - own_half + rows, LANES:].astype(BF16)
            collected[place, :] = gathered
            mine = own[place, :]
            pre_node = dot(jnp.concatenate([mine, gathered], axis=1), node_in[...])
            _, _, node_normed, _ = mlp_rest(pre_node, wide_node)
            new[place, :] = mine.astype(F32) + node_normed


def whole(array):
    rank = array.ndim
    return pl.BlockSpec(array.shape, lambda step: (0,) * rank)


def level_specs(params):
    stacks, level = params
    return [
        pl.BlockSpec((None,) + stack.shape[1:], lambda step: (level, 0, 0)) for stack in stacks
    ]


def column_block(source):
    array, column = source if isinstance(source, tuple) else (source, 0)
    return array, pl.BlockSpec((array.shape[0], LANES), lambda step: (0, column))


def layer_forward(tables, own, edges, send, recv, live, params, block, masked, split=False):
    count, feature = edges.shape
    own, own_spec = column_block(own)
    tables, table_specs = zip(*[column_block(source) for source in tables])
    steps = count // block
    send3 = send.reshape(steps, block // LANES, LANES)
    recv3 = recv.reshape(steps, block // LANES, LANES)
    ids = pl.BlockSpec((1, block // LANES, LANES), lambda step: (step, 0, 0))
    edge_spec = pl.BlockSpec((block, feature), lambda step: (step, 0))
    nodes, rows = own.shape[0], sum(array.shape[0] for array in tables)
    early = count >= rows
    full = lambda n: pl.BlockSpec((n, feature), lambda step: (0, 0))
    return pl.pallas_call(
        functools.partial(forward_kernel, block, masked, split, early, len(tables)),
        grid=(steps,),
        in_specs=[pl.BlockSpec(memory_space=pltpu.SMEM), ids, ids, edge_spec, *table_specs, own_spec]
        + level_specs(params),
        out_specs=[full(nodes)] * (1 if split else 2) + [edge_spec],
        out_shape=[jax.ShapeDtypeStruct((nodes, feature), F32)]
        + ([] if split else [jax.ShapeDtypeStruct((nodes, feature), BF16)])
        + [jax.ShapeDtypeStruct((count, feature), F32)],
        scratch_shapes=[
            pltpu.VMEM((rows // 2, 2 * feature), BF16),
            pltpu.VMEM((nodes // 2, 2 * feature), BF16),
            pltpu.VMEM((2 * feature, 2 * feature), BF16),
            pltpu.VMEM((nodes // 2, 2 * feature), F32),
        ],
        compiler_params=pltpu.CompilerParams(vmem_limit_bytes=VMEM_LIMIT),
        cost_estimate=pl.CostEstimate(
            flops=2 * count * feature * (rows + 2 * nodes + 1024),
            bytes_accessed=count * feature * 8,
            transcendentals=count * feature,
        ),
    )(live, send3, recv3, edges, *tables, own, *params[0])


def backward_kernel(
    block, masked, lifted, table_out, count, live, send, recv, edges, preact, upstream, *rest,
):
    tables, rest = rest[:count], rest[count:]
    own, collected, edge_in, edge_out, node_in, node_out = rest[:6]
    rest = rest[6:]
    split = table_out == "split"
    if lifted:
        lift_ids, lift_tables = rest[0], rest[1 : 1 + lifted]
        lift2 = rest[-1]
        rest = rest[1 + lifted : -1]
    grad_own, grads_out = rest[:2]
    grad_table = rest[2] if table_out else None
    new = rest[3] if split else None
    wide, grad2, send_total, recv_total, grads = rest[-5:]
    grad_edge_in = grads.at[pl.ds(0, 3 * LANES), :]
    grad_edge_out = grads.at[pl.ds(3 * LANES, LANES), :]
    grad_node_in = grads.at[pl.ds(4 * LANES, 2 * LANES), :]
    grad_node_out = grads.at[pl.ds(6 * LANES, LANES), :]
    step = pl.program_id(0)
    table_half, own_half = send_total.shape[0], recv_total.shape[0]

    @pl.when(step == 0)
    def _():
        wide[...] = widened(edge_out[...])
        send_total[...] = jnp.zeros_like(send_total)
        recv_total[...] = jnp.zeros_like(recv_total)
        grad_edge_in[...] = jnp.zeros_like(grad_edge_in)
        grad_edge_out[...] = jnp.zeros_like(grad_edge_out)
        wide_node = widened(node_out[...])
        into, out_of = node_in[...], node_out[...]
        total_in = jnp.zeros((2 * LANES, LANES), F32)
        total_out = jnp.zeros((LANES, LANES), F32)
        if lifted:
            height = lift2.shape[0]
            for side in range(2):
                lines = pl.ds(side * height, height)
                term = lift_tables[0][lines, :]
                if lifted > 1:
                    for more in lift_tables[1:-1]:
                        term = term + more[lines, :]
                    term = term * lift_tables[-1][lines, :].astype(F32)
                lift2[:, side * LANES : (side + 1) * LANES] = term.astype(BF16)
            ids = lift_ids[...].astype(F32)
        rows = min(own_half, 512)
        for start in range(0, 2 * own_half, rows):
            place = pl.ds(start, rows)
            inputs = jnp.concatenate([own[place, :], collected[place, :]], axis=1)
            pre = dot(inputs, into)
            sigmoid_pre, hidden, normed, inv_std = mlp_rest(pre, wide_node)
            up = upstream[place, :].astype(F32)
            if lifted:
                places = as_columns(ids[start // LANES : (start + rows) // LANES, :])
                up = up + gather(places, lift2[...])
            centred_grad = (
                up
                - jnp.mean(up, axis=-1, keepdims=True)
                - normed * jnp.mean(up * normed, axis=-1, keepdims=True)
            )
            grad_output = (inv_std * centred_grad).astype(BF16)
            total_out = total_out + dot_tn(hidden, grad_output)
            grad_hidden = dot_nt(grad_output, out_of)
            grad_pre = (
                grad_hidden * sigmoid_pre * (1.0 + pre * (1.0 - sigmoid_pre))
            ).astype(BF16)
            total_in = total_in + dot_tn(inputs, grad_pre)
            back = dot_nt(grad_pre, into)
            if split:
                new[place, :] = own[place, :].astype(F32) + normed
                grad_table[place, :] = up + back[:, :LANES]
                grad_own[place, :] = jnp.zeros((rows, LANES), F32)
            else:
                grad_own[place, :] = up + back[:, :LANES]
            grad_collected = back[:, LANES:]
            grad_collected = grad_collected - jnp.mean(grad_collected, axis=-1, keepdims=True)
            if start < own_half:
                grad2[start : start + rows, :LANES] = grad_collected.astype(BF16)
            else:
                grad2[start - own_half : start - own_half + rows, LANES:] = grad_collected.astype(
                    BF16
                )
        grad_node_in[...] = total_in
        grad_node_out[...] = total_out

    send_rows = send[...].reshape(block // LANES, LANES).astype(F32)
    recv_rows = recv[...].reshape(block // LANES, LANES).astype(F32)
    send_columns = as_columns(send_rows)
    recv_columns = as_columns(recv_rows)
    grad_updated = gather(recv_columns, grad2[...])
    if masked:
        slot = step * block + lax.broadcasted_iota(jnp.int32, (block, LANES), 0)
        grad_updated = jnp.where(slot < live[0], grad_updated, 0.0)
    pre = preact[...]
    sigmoid_pre, hidden, normed, inv_std = mlp_rest(pre, wide[...])
    centred_grad = grad_updated - normed * lane_mean(grad_updated * normed)
    grad_output = (inv_std * centred_grad).astype(BF16)
    grad_edge_out[...] += dot_tn(hidden, grad_output)
    grad_hidden = dot_nt(grad_output, edge_out[...])
    edge_grad = (grad_hidden * sigmoid_pre * (1.0 + pre * (1.0 - sigmoid_pre))).astype(BF16)
    grad_edge_in[2 * LANES :, :] += dot_tn(edges[...], edge_grad)
    send_total[...] += spread(send_rows, send_columns, edge_grad, table_half)
    recv_total[...] += spread(recv_rows, recv_columns, edge_grad, own_half)

    @pl.when(step == pl.num_programs(0) - 1)
    def _():
        from_send = edge_in[:LANES, :]
        from_recv = edge_in[LANES : 2 * LANES, :]
        nodes = 2 * own_half

        def part(total, half, start, rows):
            if start < half:
                return total[start : start + rows, :LANES].astype(BF16)
            return total[start - half : start - half + rows, LANES:].astype(BF16)

        weight_recv = jnp.zeros((LANES, LANES), F32)
        rows = min(own_half, 512)
        for start in range(0, nodes, rows):
            place = pl.ds(start, rows)
            recv_sum = part(recv_total, own_half, start, rows)
            weight_recv = weight_recv + dot_tn(own[place, :], recv_sum)
            grad_own[place, :] += dot_nt(recv_sum, from_recv)
        grad_edge_in[LANES : 2 * LANES, :] = weight_recv

        weight_send = jnp.zeros((LANES, LANES), F32)
        cuts = sorted({0, table_half, nodes, 2 * table_half} if nodes > table_half else {0, table_half, 2 * table_half})
        pieces = []
        for first, last in zip(cuts[:-1], cuts[1:]):
            pieces += [(k, min(1152, last - k)) for k in range(first, last, 1152)]
        for start, rows in pieces:
            place = pl.ds(start, rows)
            split_sum = part(send_total, table_half, start, rows)
            weight_send = weight_send + dot_tn(rows_of(tables, start, rows), split_sum)
            back = dot_nt(split_sum, from_send)
            if table_out == "whole":
                grad_table[place, :] = back.astype(BF16)
            elif start < nodes:
                grad_own[place, :] += back
            else:
                grad_table[pl.ds(start - nodes, rows), :] = back.astype(BF16)
        grad_edge_in[:LANES, :] = weight_send
        grads_out[...] = grads[...].astype(grads_out.dtype)


def layer_backward(
    upstream, tables, own, collected, edges, preact, send, recv, live, params, block, masked,
    table_out, lift_ids=None, lift_tables=(),
):
    lifted = len(lift_tables)
    own, own_spec = column_block(own)
    tables, table_specs = zip(*[column_block(source) for source in tables])
    upstream, upstream_spec = column_block(upstream)
    count, feature = edges.shape
    steps = count // block
    send3 = send.reshape(steps, block // LANES, LANES)
    recv3 = recv.reshape(steps, block // LANES, LANES)
    ids = pl.BlockSpec((1, block // LANES, LANES), lambda step: (step, 0, 0))
    edge_spec = pl.BlockSpec((block, feature), lambda step: (step, 0))
    nodes, rows = own.shape[0], sum(array.shape[0] for array in tables)
    full = lambda n: pl.BlockSpec((n, feature), lambda step: (0, 0))
    out = [(nodes, F32), (7 * feature, F32 if table_out == "split" else BF16)]
    if table_out == "whole":
        out.append((rows, BF16))
    elif table_out == "rest":
        out.append((rows - nodes, BF16))
    elif table_out == "split":
        out += [(nodes, F32), (nodes, F32)]
    extra, extra_specs, extra_scratch = [], [], []
    if lifted:
        lift_ids = lift_ids.reshape(nodes // LANES, LANES)
        extra.append(lift_ids)
        extra_specs.append(whole(lift_ids))
        for source in lift_tables:
            array, spec = column_block(source)
            extra.append(array)
            extra_specs.append(spec)
        extra_scratch = [pltpu.VMEM((array.shape[0] // 2, 2 * feature), BF16)]
    return pl.pallas_call(
        functools.partial(backward_kernel, block, masked, lifted, table_out, len(tables)),
        grid=(steps,),
        in_specs=[
            pl.BlockSpec(memory_space=pltpu.SMEM),
            ids,
            ids,
            edge_spec,
            edge_spec,
            upstream_spec,
            *table_specs,
            own_spec,
            full(nodes),
        ]
        + level_specs(params)
        + extra_specs,
        out_specs=[full(n) for n, _ in out],
        out_shape=[jax.ShapeDtypeStruct((n, feature), kind) for n, kind in out],
        scratch_shapes=[
            pltpu.VMEM((2 * feature, 2 * feature), BF16),
            pltpu.VMEM((nodes // 2, 2 * feature), BF16),
            pltpu.VMEM((rows // 2, 2 * feature), F32),
            pltpu.VMEM((nodes // 2, 2 * feature), F32),
            pltpu.VMEM((7 * feature, feature), F32),
        ]
        + extra_scratch,
        compiler_params=pltpu.CompilerParams(vmem_limit_bytes=VMEM_LIMIT),
        cost_estimate=pl.CostEstimate(
            flops=2 * count * feature * (rows + 2 * nodes + 1024),
            bytes_accessed=count * feature * 8,
            transcendentals=count * feature,
        ),
    )(live, send3, recv3, edges, preact, upstream, *tables, own, collected, *params[0], *extra)


def pool_kernel(owned, ids, left, right, out, counts):
    step = pl.program_id(0)
    group = out.shape[0]
    rows = ids[...].astype(F32)

    @pl.when(step == 0)
    def _():
        high_rows = jnp.floor(rows * (1.0 / LANES))
        low_rows = rows - high_rows * float(LANES)
        counts[...] = dot_nt(one_hot_t(high_rows, LANES), one_hot_t(low_rows, LANES))

    span = group * owned
    local = rows - (step * span).astype(F32)
    local = jnp.where((local >= 0.0) & (local < float(span)), local, float(span))
    both = jnp.concatenate([left[...].astype(BF16), right[...].astype(BF16)], axis=1)
    sums = dot(one_hot_t(local, span), both).astype(BF16)
    lines = owned // LANES
    for k in range(group):
        out[k, :owned, :] = sums[k * owned : (k + 1) * owned, :]
        hits = counts[pl.ds((step * group + k) * lines, lines), :]
        high = jnp.floor(hits * (1.0 / 64.0))
        tail = jnp.concatenate(
            [high, hits - high * 64.0, jnp.zeros((16 - 2 * lines, LANES), F32)], axis=0
        )
        out[k, owned:, :] = jnp.concatenate([tail, jnp.zeros_like(tail)], axis=1).astype(BF16)


def pool_fine_nodes(ids, left, right, parts, owned):
    count, feature = left.shape
    group = 4
    rows = owned + 16
    full = pl.BlockSpec((count, feature), lambda step: (0, 0))
    return pl.pallas_call(
        functools.partial(pool_kernel, owned),
        grid=(parts // group,),
        in_specs=[pl.BlockSpec((count // LANES, LANES), lambda step: (0, 0)), full, full],
        out_specs=pl.BlockSpec((group, rows, 2 * feature), lambda step: (step, 0, 0)),
        out_shape=jax.ShapeDtypeStruct((parts, rows, 2 * feature), BF16),
        scratch_shapes=[pltpu.VMEM((LANES, LANES), F32)],
        compiler_params=pltpu.CompilerParams(vmem_limit_bytes=VMEM_LIMIT),
        cost_estimate=pl.CostEstimate(
            flops=4 * count * parts * owned * feature,
            bytes_accessed=4 * count * feature,
            transcendentals=0,
        ),
    )(ids.reshape(count // LANES, LANES), left, right)


def pool_mid_kernel(ids, left, right, out):
    rows = ids[...].astype(F32)
    both = jnp.concatenate(
        [left[...].astype(BF16), right[...].astype(BF16), jnp.ones(left.shape, BF16)], axis=1
    )
    out[...] = dot(one_hot_t(rows, out.shape[0]), both).astype(BF16)


def pool_mid_nodes(ids, left, right, targets):
    count, feature = left.shape
    return pl.pallas_call(
        pool_mid_kernel,
        out_shape=jax.ShapeDtypeStruct((targets, 3 * feature), BF16),
        compiler_params=pltpu.CompilerParams(vmem_limit_bytes=VMEM_LIMIT),
        cost_estimate=pl.CostEstimate(
            flops=6 * count * targets * feature, bytes_accessed=6 * targets * feature, transcendentals=0
        ),
    )(ids.reshape(count // LANES, LANES), left, right)


def lift_kernel(ids, base, table, out, table2):
    @pl.when(pl.program_id(0) == 0)
    def _():
        half = table2.shape[0]
        table2[:, :LANES] = table[:half, :].astype(BF16)
        table2[:, LANES:] = table[half:, :].astype(BF16)

    rows = ids[...].reshape(ids.shape[1], LANES).astype(F32)
    out[...] = (base[...].astype(F32) + gather(as_columns(rows), table2[...])).astype(out.dtype)


def lift(base, table, ids, kind):
    count, feature = base.shape
    rows = table.shape[0]
    block = min(count, 512)
    steps = count // block
    return pl.pallas_call(
        lift_kernel,
        grid=(steps,),
        in_specs=[
            pl.BlockSpec((1, block // LANES, LANES), lambda step: (step, 0, 0)),
            pl.BlockSpec((block, feature), lambda step: (step, 0)),
            pl.BlockSpec((rows, feature), lambda step: (0, 0)),
        ],
        out_specs=pl.BlockSpec((block, feature), lambda step: (step, 0)),
        out_shape=jax.ShapeDtypeStruct((count, feature), kind),
        scratch_shapes=[pltpu.VMEM((rows // 2, 2 * feature), BF16)],
        compiler_params=pltpu.CompilerParams(vmem_limit_bytes=VMEM_LIMIT),
        cost_estimate=pl.CostEstimate(
            flops=2 * count * rows * feature, bytes_accessed=8 * count * feature, transcendentals=0
        ),
    )(ids.reshape(steps, block // LANES, LANES), base, table)


def add_rows_kernel(ids, base, values, out):
    rows = ids[...].astype(F32)
    out[...] = base[...] + dot(one_hot_t(rows, out.shape[0]), values[...])


def add_rows(base, ids, values):
    return pl.pallas_call(
        add_rows_kernel,
        out_shape=jax.ShapeDtypeStruct(base.shape, base.dtype),
        compiler_params=pltpu.CompilerParams(vmem_limit_bytes=VMEM_LIMIT),
        cost_estimate=pl.CostEstimate(
            flops=2 * base.shape[0] * values.shape[0] * LANES, bytes_accessed=base.size * 8, transcendentals=0
        ),
    )(ids.reshape(-1, LANES), base, values)


def unpack_kernel(total, coarse, coarse_other, *outs):
    length, shared = coarse.shape[0], coarse_other.shape[0]
    start = 0
    for out in outs:
        size = out.shape[1]
        out[0] = total[start : start + size, :].astype(F32)
        out[1] = total[length + start : length + start + size, :].astype(F32)
        last = coarse[start : start + size, :]
        if start + size <= shared:
            last = last + coarse_other[start : start + size, :]
        out[2] = last
        start += size


def unpack(total, coarse, coarse_other, stacks):
    return pl.pallas_call(
        unpack_kernel,
        out_shape=[jax.ShapeDtypeStruct(stack.shape, F32) for stack in stacks],
        compiler_params=pltpu.CompilerParams(vmem_limit_bytes=VMEM_LIMIT),
        cost_estimate=pl.CostEstimate(
            flops=0, bytes_accessed=8 * total.size, transcendentals=0
        ),
    )(total, coarse, coarse_other)


def shared_out(block, axes, count):
    sent = jnp.broadcast_to(block[None], (count,) + block.shape)
    return lax.all_to_all(sent, axes, split_axis=0, concat_axis=0, tiled=True)


def summed_in(blocks, axes):
    got = lax.all_to_all(blocks, axes, split_axis=0, concat_axis=0, tiled=True)
    return jnp.sum(got.astype(F32), axis=0)


def shards(
    nodes,
    edges,
    senders,
    receivers,
    edge_live,
    halo_rows,
    pool_fine,
    mid_edges,
    mid_senders,
    mid_receivers,
    pool_mid,
    coarse_edges,
    coarse_senders,
    coarse_receivers,
    w_edge_in,
    w_edge_out,
    w_node_in,
    w_node_out,
    cotangent,
):
    every = ("grp", "sub")
    feature = nodes.shape[1]
    fine_count = nodes.shape[0]
    halo_width = halo_rows.shape[1]
    owned_mids = pool_mid.shape[0]
    sub_count = lax.axis_size("sub")
    device_count = sub_count * lax.axis_size("grp")
    group_mids = owned_mids * sub_count
    coarse_count = coarse_edges.shape[0] // 6
    stacks = (w_edge_in, w_edge_out, w_node_in, w_node_out)
    fine_params, mid_params, coarse_params = (stacks, 0), (stacks, 1), (stacks, 2)
    up = [(i, i + 1) for i in range(device_count - 1)]
    down = [(i + 1, i) for i in range(device_count - 1)]

    pairs = [(i, i ^ 1) for i in range(lax.axis_size("grp"))]
    halo = nodes.at[halo_rows.reshape(-1)].get(mode="promise_in_bounds")
    from_prev = lax.ppermute(halo[:halo_width], every, up)
    from_next = lax.ppermute(halo[halo_width:], every, down)
    fine_tables = (nodes, from_prev, from_next)

    fine_new, fine_collected, fine_pre = layer_forward(
        fine_tables, nodes, edges, senders, receivers, edge_live, fine_params, 4096, True
    )
    pooled = pool_fine_nodes(pool_fine, fine_new, cotangent, sub_count, owned_mids)
    owned = summed_in(pooled, "sub")
    lines = owned_mids // feature
    tail = owned[owned_mids : owned_mids + 2 * lines, :feature]
    owned_counts = (64.0 * tail[:lines] + tail[lines:]).reshape(owned_mids, 1)
    owned_counts = jnp.maximum(owned_counts, 1.0)
    mid_own = (owned[:owned_mids, :feature] / owned_counts).astype(BF16)
    grad_mid = owned[:owned_mids, feature:]
    mid_table = shared_out(mid_own, "sub", sub_count).reshape(group_mids, feature)
    mid_new, mid_collected, mid_pre = layer_forward(
        (mid_table,), mid_own, mid_edges, mid_senders, mid_receivers, edge_live, mid_params, 1536, False
    )

    coarse_sent = pool_mid_nodes(pool_mid, mid_new, grad_mid, coarse_count)
    coarse_rows = coarse_count // device_count
    mine = summed_in(coarse_sent.reshape(device_count, coarse_rows, 3 * feature), every)
    my_scale = 1.0 / jnp.maximum(mine[:, 2 * feature :], 1.0)
    coarse_mine = jnp.concatenate(
        [mine[:, :feature] * my_scale, mine[:, feature : 2 * feature], my_scale], axis=1
    ).astype(BF16)
    coarse_all = shared_out(coarse_mine, every, device_count).reshape(coarse_count, 3 * feature)
    coarse_in, grad_coarse, coarse_scale = (coarse_all, 0), (coarse_all, 1), (coarse_all, 2)

    half_edges = coarse_edges.shape[0] // 2
    first = lax.rem(lax.axis_index("grp"), 2) * half_edges
    my_edges = lax.dynamic_slice_in_dim(coarse_edges, first, half_edges)
    my_senders = lax.dynamic_slice_in_dim(coarse_senders, first, half_edges)
    my_receivers = lax.dynamic_slice_in_dim(coarse_receivers, first, half_edges)
    coarse_part, coarse_pre = layer_forward(
        (coarse_in,), coarse_in, my_edges, my_senders, my_receivers, edge_live, coarse_params, 3072, False, True
    )
    coarse_half = coarse_part.astype(BF16)
    coarse_other = lax.ppermute(coarse_half, "grp", pairs)
    coarse_collected = (coarse_half.astype(F32) + coarse_other.astype(F32)).astype(BF16)
    coarse_back, coarse_grads, coarse_base, coarse_new = layer_backward(
        grad_coarse,
        (coarse_in,),
        coarse_in,
        coarse_collected,
        my_edges,
        coarse_pre,
        my_senders,
        my_receivers,
        edge_live,
        coarse_params,
        3072,
        False,
        "split",
    )
    coarse_back_other = lax.ppermute(coarse_back, "grp", pairs)
    edge_rows = 4 * feature
    coarse_grads_other = lax.ppermute(coarse_grads[:edge_rows], "grp", pairs)
    mid_out = lift(mid_new, coarse_new, pool_mid, BF16)
    lift_table = lax.all_gather(mid_out, "sub", axis=0, tiled=True)
    mid_own_grad, mid_grads, mid_table_grad = layer_backward(
        grad_mid,
        (mid_table,),
        mid_own,
        mid_collected,
        mid_edges,
        mid_pre,
        mid_senders,
        mid_receivers,
        edge_live,
        mid_params,
        1536,
        False,
        "whole",
        pool_mid,
        (coarse_back, coarse_back_other, coarse_base, coarse_scale),
    )
    owned_total = mid_own_grad + summed_in(
        mid_table_grad.reshape(sub_count, owned_mids, feature), "sub"
    )
    owned_scaled = (owned_total / owned_counts).astype(BF16)
    grad_partial = shared_out(owned_scaled, "sub", sub_count).reshape(group_mids, feature)
    grad_nodes, fine_grads, halo_grad = layer_backward(
        cotangent,
        fine_tables,
        nodes,
        fine_collected,
        edges,
        fine_pre,
        senders,
        receivers,
        edge_live,
        fine_params,
        4096,
        True,
        "rest",
        pool_fine,
        (grad_partial,),
    )
    to_prev = lax.ppermute(halo_grad[:halo_width], every, down)
    to_next = lax.ppermute(halo_grad[halo_width:], every, up)
    result = lift(fine_new, lift_table, pool_fine, BF16)
    flat = jnp.concatenate([fine_grads, mid_grads], axis=0)
    share = -(-flat.shape[0] // (16 * device_count)) * 16
    flat = jnp.pad(flat, ((0, share * device_count - flat.shape[0]), (0, 0)))
    my_sum = summed_in(flat.reshape(device_count, share, feature), every).astype(BF16)
    my_sum, result, to_prev, to_next = lax.optimization_barrier((my_sum, result, to_prev, to_next))
    total = shared_out(my_sum, every, device_count).reshape(device_count * share, feature)
    grad_nodes = add_rows(
        grad_nodes, halo_rows, jnp.concatenate([to_prev, to_next], axis=0)
    )
    grads = unpack(total, coarse_grads, coarse_grads_other, stacks)
    return (result, grad_nodes, grads[0], grads[1], grads[2], grads[3])


def solution(mesh):
    row, flat = P(("grp", "sub"), None), P(("grp", "sub"))
    in_specs = (row, row, flat, flat, flat, row, flat, row, flat, flat, flat) + (P(),) * 7 + (row,)
    out_specs = (row, row, P(), P(), P(), P())
    return jax.shard_map(shards, mesh=mesh, in_specs=in_specs, out_specs=out_specs, check_vma=False)
```

```python
import functools
import jax
import jax.numpy as jnp
from jax import lax
from jax.experimental import pallas as pl
from jax.experimental.pallas import tpu as pltpu
from jax.sharding import PartitionSpec as P

epsilon = 1e-05
F32 = jnp.float32
BF16 = jnp.bfloat16
LANES = 128
VMEM_LIMIT = 56 * 1024 * 1024


def dot(a, b):
    return jnp.dot(a, b, preferred_element_type=F32)


def dot_nt(a, b):
    return lax.dot_general(a, b, (((1,), (1,)), ((), ())), preferred_element_type=F32)


def dot_tn(a, b):
    return lax.dot_general(a, b, (((0,), (0,)), ((), ())), preferred_element_type=F32)


def as_columns(rows):
    count = rows.shape[0]
    return jnp.concatenate(
        [jnp.broadcast_to(rows[k : k + 1, :], (LANES, LANES)).T for k in range(count)], axis=0
    )


def parts_of(index):
    high = jnp.floor(index * (1.0 / LANES))
    return high.astype(BF16), (index - high * float(LANES)).astype(BF16)


def one_hot(columns, width):
    high, low = parts_of(columns)
    lane = lax.broadcasted_iota(jnp.int32, (1, LANES), 1).astype(F32).astype(BF16)
    one, zero = jnp.ones((), BF16), jnp.zeros((), BF16)
    base = jnp.where(low == lane, one, zero)
    return jnp.concatenate(
        [jnp.where(high == jnp.asarray(j, BF16), base, zero) for j in range(width // LANES)], axis=1
    )


def one_hot_t(rows, height):
    high, low = parts_of(rows)
    place = lax.broadcasted_iota(jnp.int32, (LANES, LANES), 0).astype(F32).astype(BF16)
    one, zero = jnp.ones((), BF16), jnp.zeros((), BF16)
    pieces = []
    for k in range(rows.shape[0]):
        base = jnp.where(place == low[k : k + 1, :], one, zero)
        pieces.append(
            jnp.concatenate(
                [
                    jnp.where(high[k : k + 1, :] == jnp.asarray(j, BF16), base, zero)
                    for j in range(height // LANES)
                ],
                axis=0,
            )
        )
    return jnp.concatenate(pieces, axis=1)


def gather(columns, table2):
    half = table2.shape[0]
    upper = columns >= float(half)
    local = jnp.where(upper, columns - float(half), columns)
    both = dot(one_hot(local, half), table2)
    return jnp.where(upper, both[:, LANES:], both[:, :LANES])


def spread(rows, columns, values, half):
    local = jnp.where(rows >= float(half), rows - float(half), rows)
    upper = columns >= float(half)
    values = values.astype(F32)
    both = jnp.concatenate(
        [jnp.where(upper, 0.0, values).astype(BF16), jnp.where(upper, values, 0.0).astype(BF16)],
        axis=1,
    )
    return dot(one_hot_t(local, half), both)


def widened(weight_out):
    row_mean = jnp.broadcast_to(
        jnp.mean(weight_out.astype(F32), axis=1, keepdims=True), weight_out.shape
    )
    high = row_mean.astype(BF16)
    low = (row_mean - high.astype(F32)).astype(BF16)
    top = jnp.concatenate([weight_out, high], axis=1)
    return jnp.concatenate(
        [top, jnp.concatenate([jnp.zeros_like(weight_out), low], axis=1)], axis=0
    )


def lane_mean(values):
    return jnp.mean(values, axis=-1, keepdims=True)


def mlp_rest(preact, wide_out):
    sigmoid_pre = jax.nn.sigmoid(preact)
    hidden = (preact * sigmoid_pre).astype(BF16)
    both = dot(jnp.concatenate([hidden, hidden], axis=1), wide_out)
    centred = both[:, :LANES] - both[:, LANES:]
    inv_std = lax.rsqrt(lane_mean(centred * centred) + epsilon)
    return sigmoid_pre, hidden, centred * inv_std, inv_std


def rows_of(tables, start, rows):
    parts, at = [], 0
    for ref in tables:
        size = ref.shape[0]
        first, last = max(start, at), min(start + rows, at + size)
        if first < last:
            parts.append(ref[first - at : last - at, :])
        at += size
    return parts[0] if len(parts) == 1 else jnp.concatenate(parts, axis=0)


def fill_halves(target, tables, weight):
    half = target.shape[0]
    for side in range(2):
        block = rows_of(tables, side * half, half)
        if weight is not None:
            block = dot(block, weight).astype(BF16)
        target[:, side * LANES : (side + 1) * LANES] = block


def forward_kernel(
    block, masked, split, early, count, live, send, recv, edges, *rest,
):
    tables, (own, edge_in, edge_out, node_in, node_out) = rest[:count], rest[count : count + 5]
    rest = rest[count + 5 :]
    if split:
        part, preact, table2, own2, wide, total = rest
    else:
        new, collected, preact, table2, own2, wide, total = rest
    step = pl.program_id(0)
    own_half = own2.shape[0]

    @pl.when(step == 0)
    def _():
        fill_halves(table2, tables, edge_in[:LANES, :] if early else None)
        fill_halves(own2, [own], edge_in[LANES : 2 * LANES, :] if early else None)
        wide[...] = widened(edge_out[...])
        total[...] = jnp.zeros_like(total)

    send_rows = send[...].reshape(block // LANES, LANES).astype(F32)
    recv_rows = recv[...].reshape(block // LANES, LANES).astype(F32)
    recv_columns = as_columns(recv_rows)
    from_send = gather(as_columns(send_rows), table2[...])
    from_recv = gather(recv_columns, own2[...])
    feat = edges[...]
    if early:
        pre = from_send + from_recv
    else:
        both = jnp.concatenate([from_send.astype(BF16), from_recv.astype(BF16)], axis=1)
        pre = dot(both, edge_in[: 2 * LANES, :])
    pre = pre + dot(feat, edge_in[2 * LANES :, :])
    preact[...] = pre
    _, _, normed, _ = mlp_rest(pre, wide[...])
    updated = feat.astype(F32) + normed
    if masked:
        slot = step * block + lax.broadcasted_iota(jnp.int32, (block, LANES), 0)
        updated = jnp.where(slot < live[0], updated, 0.0)
    total[...] += spread(recv_rows, recv_columns, updated, own_half)

    @pl.when(step == pl.num_programs(0) - 1)
    def _():
        if split:
            part[:own_half, :] = total[:, :LANES].astype(BF16)
            part[own_half:, :] = total[:, LANES:].astype(BF16)
            return
        wide_node = widened(node_out[...])
        rows = min(own_half, 512)
        for start in range(0, 2 * own_half, rows):
            place = pl.ds(start, rows)
            if start < own_half:
                gathered = total[start : start + rows, :LANES].astype(BF16)
            else:
                gathered = total[start - own_half : start - own_half + rows, LANES:].astype(BF16)
            collected[place, :] = gathered
            mine = own[place, :]
            pre_node = dot(jnp.concatenate([mine, gathered], axis=1), node_in[...])
            _, _, node_normed, _ = mlp_rest(pre_node, wide_node)
            new[place, :] = mine.astype(F32) + node_normed


def whole(array):
    rank = array.ndim
    return pl.BlockSpec(array.shape, lambda step: (0,) * rank)


def level_specs(params):
    stacks, level = params
    return [
        pl.BlockSpec((None,) + stack.shape[1:], lambda step: (level, 0, 0)) for stack in stacks
    ]


def column_block(source):
    array, column = source if isinstance(source, tuple) else (source, 0)
    return array, pl.BlockSpec((array.shape[0], LANES), lambda step: (0, column))


def layer_forward(tables, own, edges, send, recv, live, params, block, masked, split=False):
    count, feature = edges.shape
    own, own_spec = column_block(own)
    tables, table_specs = zip(*[column_block(source) for source in tables])
    steps = count // block
    send3 = send.reshape(steps, block // LANES, LANES)
    recv3 = recv.reshape(steps, block // LANES, LANES)
    ids = pl.BlockSpec((1, block // LANES, LANES), lambda step: (step, 0, 0))
    edge_spec = pl.BlockSpec((block, feature), lambda step: (step, 0))
    nodes, rows = own.shape[0], sum(array.shape[0] for array in tables)
    early = count >= rows
    full = lambda n: pl.BlockSpec((n, feature), lambda step: (0, 0))
    return pl.pallas_call(
        functools.partial(forward_kernel, block, masked, split, early, len(tables)),
        grid=(steps,),
        in_specs=[pl.BlockSpec(memory_space=pltpu.SMEM), ids, ids, edge_spec, *table_specs, own_spec]
        + level_specs(params),
        out_specs=[full(nodes)] * (1 if split else 2) + [edge_spec],
        out_shape=[jax.ShapeDtypeStruct((nodes, feature), BF16 if split else F32)]
        + ([] if split else [jax.ShapeDtypeStruct((nodes, feature), BF16)])
        + [jax.ShapeDtypeStruct((count, feature), F32)],
        scratch_shapes=[
            pltpu.VMEM((rows // 2, 2 * feature), BF16),
            pltpu.VMEM((nodes // 2, 2 * feature), BF16),
            pltpu.VMEM((2 * feature, 2 * feature), BF16),
            pltpu.VMEM((nodes // 2, 2 * feature), F32),
        ],
        compiler_params=pltpu.CompilerParams(vmem_limit_bytes=VMEM_LIMIT),
        cost_estimate=pl.CostEstimate(
            flops=2 * count * feature * (rows + 2 * nodes + 1024),
            bytes_accessed=count * feature * 8,
            transcendentals=count * feature,
        ),
    )(live, send3, recv3, edges, *tables, own, *params[0])


def backward_kernel(
    block, masked, lifted, table_out, count, live, send, recv, edges, preact, upstream, *rest,
):
    tables, rest = rest[:count], rest[count:]
    own, collected, edge_in, edge_out, node_in, node_out = rest[:6]
    rest = rest[6:]
    split = table_out == "split"
    if lifted:
        lift_ids, lift_tables = rest[0], rest[1 : 1 + lifted]
        lift2 = rest[-1]
        rest = rest[1 + lifted : -1]
    grad_own, grads_out = rest[:2]
    grad_table = rest[2] if table_out else None
    new = rest[3] if split else None
    wide, grad2, send_total, recv_total, grads = rest[-5:]
    grad_edge_in = grads.at[pl.ds(0, 3 * LANES), :]
    grad_edge_out = grads.at[pl.ds(3 * LANES, LANES), :]
    grad_node_in = grads.at[pl.ds(4 * LANES, 2 * LANES), :]
    grad_node_out = grads.at[pl.ds(6 * LANES, LANES), :]
    step = pl.program_id(0)
    table_half, own_half = send_total.shape[0], recv_total.shape[0]

    @pl.when(step == 0)
    def _():
        wide[...] = widened(edge_out[...])
        send_total[...] = jnp.zeros_like(send_total)
        recv_total[...] = jnp.zeros_like(recv_total)
        grad_edge_in[...] = jnp.zeros_like(grad_edge_in)
        grad_edge_out[...] = jnp.zeros_like(grad_edge_out)
        wide_node = widened(node_out[...])
        into, out_of = node_in[...], node_out[...]
        total_in = jnp.zeros((2 * LANES, LANES), F32)
        total_out = jnp.zeros((LANES, LANES), F32)
        if lifted:
            height = lift2.shape[0]
            for side in range(2):
                lines = pl.ds(side * height, height)
                term = lift_tables[0][lines, :]
                if lifted > 1:
                    for more in lift_tables[1:-1]:
                        term = term + more[lines, :]
                    term = term * lift_tables[-1][lines, :].astype(F32)
                lift2[:, side * LANES : (side + 1) * LANES] = term.astype(BF16)
            ids = lift_ids[...].astype(F32)
        rows = min(own_half, 512)
        for start in range(0, 2 * own_half, rows):
            place = pl.ds(start, rows)
            inputs = jnp.concatenate([own[place, :], collected[place, :]], axis=1)
            pre = dot(inputs, into)
            sigmoid_pre, hidden, normed, inv_std = mlp_rest(pre, wide_node)
            up = upstream[place, :].astype(F32)
            if lifted:
                places = as_columns(ids[start // LANES : (start + rows) // LANES, :])
                up = up + gather(places, lift2[...])
            centred_grad = (
                up
                - jnp.mean(up, axis=-1, keepdims=True)
                - normed * jnp.mean(up * normed, axis=-1, keepdims=True)
            )
            grad_output = (inv_std * centred_grad).astype(BF16)
            total_out = total_out + dot_tn(hidden, grad_output)
            grad_hidden = dot_nt(grad_output, out_of)
            grad_pre = (
                grad_hidden * sigmoid_pre * (1.0 + pre * (1.0 - sigmoid_pre))
            ).astype(BF16)
            total_in = total_in + dot_tn(inputs, grad_pre)
            back = dot_nt(grad_pre, into)
            if split:
                new[place, :] = own[place, :].astype(F32) + normed
                grad_table[place, :] = up + back[:, :LANES]
                grad_own[place, :] = jnp.zeros((rows, LANES), F32)
            else:
                grad_own[place, :] = up + back[:, :LANES]
            grad_collected = back[:, LANES:]
            grad_collected = grad_collected - jnp.mean(grad_collected, axis=-1, keepdims=True)
            if start < own_half:
                grad2[start : start + rows, :LANES] = grad_collected.astype(BF16)
            else:
                grad2[start - own_half : start - own_half + rows, LANES:] = grad_collected.astype(
                    BF16
                )
        grad_node_in[...] = total_in
        grad_node_out[...] = total_out

    send_rows = send[...].reshape(block // LANES, LANES).astype(F32)
    recv_rows = recv[...].reshape(block // LANES, LANES).astype(F32)
    send_columns = as_columns(send_rows)
    recv_columns = as_columns(recv_rows)
    grad_updated = gather(recv_columns, grad2[...])
    if masked:
        slot = step * block + lax.broadcasted_iota(jnp.int32, (block, LANES), 0)
        grad_updated = jnp.where(slot < live[0], grad_updated, 0.0)
    pre = preact[...]
    sigmoid_pre, hidden, normed, inv_std = mlp_rest(pre, wide[...])
    centred_grad = grad_updated - normed * lane_mean(grad_updated * normed)
    grad_output = (inv_std * centred_grad).astype(BF16)
    grad_edge_out[...] += dot_tn(hidden, grad_output)
    grad_hidden = dot_nt(grad_output, edge_out[...])
    edge_grad = (grad_hidden * sigmoid_pre * (1.0 + pre * (1.0 - sigmoid_pre))).astype(BF16)
    grad_edge_in[2 * LANES :, :] += dot_tn(edges[...], edge_grad)
    send_total[...] += spread(send_rows, send_columns, edge_grad, table_half)
    recv_total[...] += spread(recv_rows, recv_columns, edge_grad, own_half)

    @pl.when(step == pl.num_programs(0) - 1)
    def _():
        from_send = edge_in[:LANES, :]
        from_recv = edge_in[LANES : 2 * LANES, :]
        nodes = 2 * own_half

        def part(total, half, start, rows):
            if start < half:
                return total[start : start + rows, :LANES].astype(BF16)
            return total[start - half : start - half + rows, LANES:].astype(BF16)

        weight_recv = jnp.zeros((LANES, LANES), F32)
        rows = min(own_half, 512)
        for start in range(0, nodes, rows):
            place = pl.ds(start, rows)
            recv_sum = part(recv_total, own_half, start, rows)
            weight_recv = weight_recv + dot_tn(own[place, :], recv_sum)
            grad_own[place, :] += dot_nt(recv_sum, from_recv)
        grad_edge_in[LANES : 2 * LANES, :] = weight_recv

        weight_send = jnp.zeros((LANES, LANES), F32)
        cuts = sorted({0, table_half, nodes, 2 * table_half} if nodes > table_half else {0, table_half, 2 * table_half})
        pieces = []
        for first, last in zip(cuts[:-1], cuts[1:]):
            pieces += [(k, min(1152, last - k)) for k in range(first, last, 1152)]
        for start, rows in pieces:
            place = pl.ds(start, rows)
            split_sum = part(send_total, table_half, start, rows)
            weight_send = weight_send + dot_tn(rows_of(tables, start, rows), split_sum)
            back = dot_nt(split_sum, from_send)
            if table_out == "whole":
                grad_table[place, :] = back.astype(BF16)
            elif start < nodes:
                grad_own[place, :] += back
            else:
                grad_table[pl.ds(start - nodes, rows), :] = back.astype(BF16)
        grad_edge_in[:LANES, :] = weight_send
        grads_out[...] = grads[...].astype(grads_out.dtype)


def layer_backward(
    upstream, tables, own, collected, edges, preact, send, recv, live, params, block, masked,
    table_out, lift_ids=None, lift_tables=(),
):
    lifted = len(lift_tables)
    own, own_spec = column_block(own)
    tables, table_specs = zip(*[column_block(source) for source in tables])
    upstream, upstream_spec = column_block(upstream)
    count, feature = edges.shape
    steps = count // block
    send3 = send.reshape(steps, block // LANES, LANES)
    recv3 = recv.reshape(steps, block // LANES, LANES)
    ids = pl.BlockSpec((1, block // LANES, LANES), lambda step: (step, 0, 0))
    edge_spec = pl.BlockSpec((block, feature), lambda step: (step, 0))
    nodes, rows = own.shape[0], sum(array.shape[0] for array in tables)
    full = lambda n: pl.BlockSpec((n, feature), lambda step: (0, 0))
    out = [(nodes, F32), (7 * feature, F32 if table_out == "split" else BF16)]
    if table_out == "whole":
        out.append((rows, BF16))
    elif table_out == "rest":
        out.append((rows - nodes, BF16))
    elif table_out == "split":
        out += [(nodes, F32), (nodes, F32)]
    extra, extra_specs, extra_scratch = [], [], []
    if lifted:
        lift_ids = lift_ids.reshape(nodes // LANES, LANES)
        extra.append(lift_ids)
        extra_specs.append(whole(lift_ids))
        for source in lift_tables:
            array, spec = column_block(source)
            extra.append(array)
            extra_specs.append(spec)
        extra_scratch = [pltpu.VMEM((array.shape[0] // 2, 2 * feature), BF16)]
    return pl.pallas_call(
        functools.partial(backward_kernel, block, masked, lifted, table_out, len(tables)),
        grid=(steps,),
        in_specs=[
            pl.BlockSpec(memory_space=pltpu.SMEM),
            ids,
            ids,
            edge_spec,
            edge_spec,
            upstream_spec,
            *table_specs,
            own_spec,
            full(nodes),
        ]
        + level_specs(params)
        + extra_specs,
        out_specs=[full(n) for n, _ in out],
        out_shape=[jax.ShapeDtypeStruct((n, feature), kind) for n, kind in out],
        scratch_shapes=[
            pltpu.VMEM((2 * feature, 2 * feature), BF16),
            pltpu.VMEM((nodes // 2, 2 * feature), BF16),
            pltpu.VMEM((rows // 2, 2 * feature), F32),
            pltpu.VMEM((nodes // 2, 2 * feature), F32),
            pltpu.VMEM((7 * feature, feature), F32),
        ]
        + extra_scratch,
        compiler_params=pltpu.CompilerParams(vmem_limit_bytes=VMEM_LIMIT),
        cost_estimate=pl.CostEstimate(
            flops=2 * count * feature * (rows + 2 * nodes + 1024),
            bytes_accessed=count * feature * 8,
            transcendentals=count * feature,
        ),
    )(live, send3, recv3, edges, preact, upstream, *tables, own, collected, *params[0], *extra)


def pool_kernel(owned, ids, left, right, out, counts):
    step = pl.program_id(0)
    group = out.shape[0]
    rows = ids[...].astype(F32)

    @pl.when(step == 0)
    def _():
        high_rows = jnp.floor(rows * (1.0 / LANES))
        low_rows = rows - high_rows * float(LANES)
        counts[...] = dot_nt(one_hot_t(high_rows, LANES), one_hot_t(low_rows, LANES))

    span = group * owned
    local = rows - (step * span).astype(F32)
    local = jnp.where((local >= 0.0) & (local < float(span)), local, float(span))
    both = jnp.concatenate([left[...].astype(BF16), right[...].astype(BF16)], axis=1)
    sums = dot(one_hot_t(local, span), both).astype(BF16)
    lines = owned // LANES
    for k in range(group):
        out[k, :owned, :] = sums[k * owned : (k + 1) * owned, :]
        hits = counts[pl.ds((step * group + k) * lines, lines), :]
        high = jnp.floor(hits * (1.0 / 64.0))
        tail = jnp.concatenate(
            [high, hits - high * 64.0, jnp.zeros((16 - 2 * lines, LANES), F32)], axis=0
        )
        out[k, owned:, :] = jnp.concatenate([tail, jnp.zeros_like(tail)], axis=1).astype(BF16)


def pool_fine_nodes(ids, left, right, parts, owned):
    count, feature = left.shape
    group = 8
    rows = owned + 16
    full = pl.BlockSpec((count, feature), lambda step: (0, 0))
    return pl.pallas_call(
        functools.partial(pool_kernel, owned),
        grid=(parts // group,),
        in_specs=[pl.BlockSpec((count // LANES, LANES), lambda step: (0, 0)), full, full],
        out_specs=pl.BlockSpec((group, rows, 2 * feature), lambda step: (step, 0, 0)),
        out_shape=jax.ShapeDtypeStruct((parts, rows, 2 * feature), BF16),
        scratch_shapes=[pltpu.VMEM((LANES, LANES), F32)],
        compiler_params=pltpu.CompilerParams(vmem_limit_bytes=VMEM_LIMIT),
        cost_estimate=pl.CostEstimate(
            flops=4 * count * parts * owned * feature,
            bytes_accessed=4 * count * feature,
            transcendentals=0,
        ),
    )(ids.reshape(count // LANES, LANES), left, right)


def pool_mid_kernel(ids, left, right, out):
    rows = ids[...].astype(F32)
    both = jnp.concatenate(
        [left[...].astype(BF16), right[...].astype(BF16), jnp.ones(left.shape, BF16)], axis=1
    )
    out[...] = dot(one_hot_t(rows, out.shape[0]), both).astype(BF16)


def pool_mid_nodes(ids, left, right, targets):
    count, feature = left.shape
    return pl.pallas_call(
        pool_mid_kernel,
        out_shape=jax.ShapeDtypeStruct((targets, 3 * feature), BF16),
        compiler_params=pltpu.CompilerParams(vmem_limit_bytes=VMEM_LIMIT),
        cost_estimate=pl.CostEstimate(
            flops=6 * count * targets * feature, bytes_accessed=6 * targets * feature, transcendentals=0
        ),
    )(ids.reshape(count // LANES, LANES), left, right)


def lift_kernel(ids, base, table, out, table2):
    @pl.when(pl.program_id(0) == 0)
    def _():
        half = table2.shape[0]
        table2[:, :LANES] = table[:half, :].astype(BF16)
        table2[:, LANES:] = table[half:, :].astype(BF16)

    rows = ids[...].reshape(ids.shape[1], LANES).astype(F32)
    out[...] = (base[...].astype(F32) + gather(as_columns(rows), table2[...])).astype(out.dtype)


def lift(base, table, ids, kind):
    count, feature = base.shape
    rows = table.shape[0]
    block = min(count, 512)
    steps = count // block
    return pl.pallas_call(
        lift_kernel,
        grid=(steps,),
        in_specs=[
            pl.BlockSpec((1, block // LANES, LANES), lambda step: (step, 0, 0)),
            pl.BlockSpec((block, feature), lambda step: (step, 0)),
            pl.BlockSpec((rows, feature), lambda step: (0, 0)),
        ],
        out_specs=pl.BlockSpec((block, feature), lambda step: (step, 0)),
        out_shape=jax.ShapeDtypeStruct((count, feature), kind),
        scratch_shapes=[pltpu.VMEM((rows // 2, 2 * feature), BF16)],
        compiler_params=pltpu.CompilerParams(vmem_limit_bytes=VMEM_LIMIT),
        cost_estimate=pl.CostEstimate(
            flops=2 * count * rows * feature, bytes_accessed=8 * count * feature, transcendentals=0
        ),
    )(ids.reshape(steps, block // LANES, LANES), base, table)


def add_rows_kernel(ids, base, values, out):
    rows = ids[...].astype(F32)
    out[...] = base[...] + dot(one_hot_t(rows, out.shape[0]), values[...])


def add_rows(base, ids, values):
    return pl.pallas_call(
        add_rows_kernel,
        out_shape=jax.ShapeDtypeStruct(base.shape, base.dtype),
        compiler_params=pltpu.CompilerParams(vmem_limit_bytes=VMEM_LIMIT),
        cost_estimate=pl.CostEstimate(
            flops=2 * base.shape[0] * values.shape[0] * LANES, bytes_accessed=base.size * 8, transcendentals=0
        ),
    )(ids.reshape(-1, LANES), base, values)


def unpack_kernel(total, coarse, coarse_other, *outs):
    length, shared = coarse.shape[0], coarse_other.shape[0]
    start = 0
    for out in outs:
        size = out.shape[1]
        out[0] = total[start : start + size, :].astype(F32)
        out[1] = total[length + start : length + start + size, :].astype(F32)
        last = coarse[start : start + size, :]
        if start + size <= shared:
            last = last + coarse_other[start : start + size, :]
        out[2] = last
        start += size


def unpack(total, coarse, coarse_other, stacks):
    return pl.pallas_call(
        unpack_kernel,
        out_shape=[jax.ShapeDtypeStruct(stack.shape, F32) for stack in stacks],
        compiler_params=pltpu.CompilerParams(vmem_limit_bytes=VMEM_LIMIT),
        cost_estimate=pl.CostEstimate(
            flops=0, bytes_accessed=8 * total.size, transcendentals=0
        ),
    )(total, coarse, coarse_other)


def shared_out(block, axes, count):
    sent = jnp.broadcast_to(block[None], (count,) + block.shape)
    return lax.all_to_all(sent, axes, split_axis=0, concat_axis=0, tiled=True)


def summed_in(blocks, axes):
    got = lax.all_to_all(blocks, axes, split_axis=0, concat_axis=0, tiled=True)
    return jnp.sum(got.astype(F32), axis=0)


def shards(
    nodes,
    edges,
    senders,
    receivers,
    edge_live,
    halo_rows,
    pool_fine,
    mid_edges,
    mid_senders,
    mid_receivers,
    pool_mid,
    coarse_edges,
    coarse_senders,
    coarse_receivers,
    w_edge_in,
    w_edge_out,
    w_node_in,
    w_node_out,
    cotangent,
):
    every = ("grp", "sub")
    feature = nodes.shape[1]
    fine_count = nodes.shape[0]
    halo_width = halo_rows.shape[1]
    owned_mids = pool_mid.shape[0]
    sub_count = lax.axis_size("sub")
    device_count = sub_count * lax.axis_size("grp")
    group_mids = owned_mids * sub_count
    coarse_count = coarse_edges.shape[0] // 6
    stacks = (w_edge_in, w_edge_out, w_node_in, w_node_out)
    fine_params, mid_params, coarse_params = (stacks, 0), (stacks, 1), (stacks, 2)
    up = [(i, i + 1) for i in range(device_count - 1)]
    down = [(i + 1, i) for i in range(device_count - 1)]

    pairs = [(i, i ^ 1) for i in range(lax.axis_size("grp"))]
    halo = nodes.at[halo_rows.reshape(-1)].get(mode="promise_in_bounds")
    from_prev = lax.ppermute(halo[:halo_width], every, up)
    from_next = lax.ppermute(halo[halo_width:], every, down)
    fine_tables = (nodes, from_prev, from_next)

    fine_new, fine_collected, fine_pre = layer_forward(
        fine_tables, nodes, edges, senders, receivers, edge_live, fine_params, 4096, True
    )
    pooled = pool_fine_nodes(pool_fine, fine_new, cotangent, sub_count, owned_mids)
    owned = summed_in(pooled, "sub")
    lines = owned_mids // feature
    tail = owned[owned_mids : owned_mids + 2 * lines, :feature]
    owned_counts = (64.0 * tail[:lines] + tail[lines:]).reshape(owned_mids, 1)
    owned_counts = jnp.maximum(owned_counts, 1.0)
    mid_own = (owned[:owned_mids, :feature] / owned_counts).astype(BF16)
    grad_mid = owned[:owned_mids, feature:]
    mid_table = shared_out(mid_own, "sub", sub_count).reshape(group_mids, feature)
    mid_new, mid_collected, mid_pre = layer_forward(
        (mid_table,), mid_own, mid_edges, mid_senders, mid_receivers, edge_live, mid_params, 1536, False
    )

    coarse_sent = pool_mid_nodes(pool_mid, mid_new, grad_mid, coarse_count)
    coarse_rows = coarse_count // device_count
    mine = summed_in(coarse_sent.reshape(device_count, coarse_rows, 3 * feature), every)
    my_scale = 1.0 / jnp.maximum(mine[:, 2 * feature :], 1.0)
    coarse_mine = jnp.concatenate(
        [mine[:, :feature] * my_scale, mine[:, feature : 2 * feature], my_scale], axis=1
    ).astype(BF16)
    coarse_all = shared_out(coarse_mine, every, device_count).reshape(coarse_count, 3 * feature)
    coarse_in, grad_coarse, coarse_scale = (coarse_all, 0), (coarse_all, 1), (coarse_all, 2)

    half_edges = coarse_edges.shape[0] // 2
    first = lax.rem(lax.axis_index("grp"), 2) * half_edges
    my_edges = lax.dynamic_slice_in_dim(coarse_edges, first, half_edges)
    my_senders = lax.dynamic_slice_in_dim(coarse_senders, first, half_edges)
    my_receivers = lax.dynamic_slice_in_dim(coarse_receivers, first, half_edges)
    coarse_half, coarse_pre = layer_forward(
        (coarse_in,), coarse_in, my_edges, my_senders, my_receivers, edge_live, coarse_params, 3072, False, True
    )
    coarse_other = lax.ppermute(coarse_half, "grp", pairs)
    coarse_collected = (coarse_half.astype(F32) + coarse_other.astype(F32)).astype(BF16)
    coarse_back, coarse_grads, coarse_base, coarse_new = layer_backward(
        grad_coarse,
        (coarse_in,),
        coarse_in,
        coarse_collected,
        my_edges,
        coarse_pre,
        my_senders,
        my_receivers,
        edge_live,
        coarse_params,
        3072,
        False,
        "split",
    )
    coarse_back_other = lax.ppermute(coarse_back, "grp", pairs)
    edge_rows = 4 * feature
    coarse_grads_other = lax.ppermute(coarse_grads[:edge_rows], "grp", pairs)
    mid_out = lift(mid_new, coarse_new, pool_mid, BF16)
    lift_table = lax.all_gather(mid_out, "sub", axis=0, tiled=True)
    mid_own_grad, mid_grads, mid_table_grad = layer_backward(
        grad_mid,
        (mid_table,),
        mid_own,
        mid_collected,
        mid_edges,
        mid_pre,
        mid_senders,
        mid_receivers,
        edge_live,
        mid_params,
        1536,
        False,
        "whole",
        pool_mid,
        (coarse_back, coarse_back_other, coarse_base, coarse_scale),
    )
    owned_total = mid_own_grad + summed_in(
        mid_table_grad.reshape(sub_count, owned_mids, feature), "sub"
    )
    owned_scaled = (owned_total / owned_counts).astype(BF16)
    grad_partial = shared_out(owned_scaled, "sub", sub_count).reshape(group_mids, feature)
    grad_nodes, fine_grads, halo_grad = layer_backward(
        cotangent,
        fine_tables,
        nodes,
        fine_collected,
        edges,
        fine_pre,
        senders,
        receivers,
        edge_live,
        fine_params,
        4096,
        True,
        "rest",
        pool_fine,
        (grad_partial,),
    )
    to_prev = lax.ppermute(halo_grad[:halo_width], every, down)
    to_next = lax.ppermute(halo_grad[halo_width:], every, up)
    result = lift(fine_new, lift_table, pool_fine, BF16)
    flat = jnp.concatenate([fine_grads, mid_grads], axis=0)
    share = -(-flat.shape[0] // (16 * device_count)) * 16
    flat = jnp.pad(flat, ((0, share * device_count - flat.shape[0]), (0, 0)))
    my_sum = summed_in(flat.reshape(device_count, share, feature), every).astype(BF16)
    my_sum, result, to_prev, to_next = lax.optimization_barrier((my_sum, result, to_prev, to_next))
    total = shared_out(my_sum, every, device_count).reshape(device_count * share, feature)
    grad_nodes = add_rows(
        grad_nodes, halo_rows, jnp.concatenate([to_prev, to_next], axis=0)
    )
    grads = unpack(total, coarse_grads, coarse_grads_other, stacks)
    return (result, grad_nodes, grads[0], grads[1], grads[2], grads[3])


def solution(mesh):
    row, flat = P(("grp", "sub"), None), P(("grp", "sub"))
    in_specs = (row, row, flat, flat, flat, row, flat, row, flat, flat, flat) + (P(),) * 7 + (row,)
    out_specs = (row, row, P(), P(), P(), P())
    return jax.shard_map(shards, mesh=mesh, in_specs=in_specs, out_specs=out_specs, check_vma=False)
```
